32 devices in a mesh: expert: 8 (over z, y), shard: 4 (over x, core).
Axes of the slice: x: 2, y: 2, z: 4, core: 2. Of those that a mesh axis runs over, the one named last changes fastest.
Arguments:
- images: bfloat16 [128, 197, 512], P(('expert', 'shard')), may hold values from -26 to 26
- attention_in: bfloat16 [512, 1536], P('shard'), may hold values from -0.25 to 0.25
- attention_out: bfloat16 [512, 512], P('shard'), may hold values from -0.75 to 0.75
- layer_gain: bfloat16 [2, 512], P(None, 'shard'), may hold values from 0.099609375 to 1.8984375
- layer_shift: bfloat16 [2, 512], P(None, 'shard'), may hold values from -3 to 3
- attention_bias: bfloat16 [3, 512], P(None, 'shard'), may hold values from -3 to 3
- expert_up: bfloat16 [8, 512, 2048], P('expert'), may hold values from -0.25 to 0.25
- hidden_bias: bfloat16 [8, 2048], P('expert'), may hold values from -3 to 3
- expert_down: bfloat16 [8, 2048, 512], P('expert'), may hold values from -0.1875 to 0.1875
- expert_bias: bfloat16 [8, 512], P('expert'), may hold values from -3 to 3
- routes: int32 [128, 197, 2], P(('expert', 'shard')), may hold values from 0 to 7, all different within a row; in each aligned block of 788 rows (0 to 787, 788 to 1575, ..., all dimensions but the last counted through in order) at most 394 rows name the same one
- gates: float32 [128, 197, 2], P(('expert', 'shard')), may hold values from 0.1 to 1
- cotangent: bfloat16 [128, 197, 512], P(('expert', 'shard')), may hold values from -6 to 6
Outputs:
- block_output: bfloat16 [128, 197, 512], P(('expert', 'shard'))
- gradient_images: float32 [128, 197, 512], P(('expert', 'shard'))
- gradient_attention_in: float32 [512, 1536], P('shard')
- gradient_attention_out: float32 [512, 512], P('shard')
- gradient_layer_gain: float32 [2, 512], P(None, 'shard')
- gradient_layer_shift: float32 [2, 512], P(None, 'shard')
- gradient_attention_bias: float32 [3, 512], P(None, 'shard')
- gradient_expert_up: float32 [8, 512, 2048], P('expert')
- gradient_hidden_bias: float32 [8, 2048], P('expert')
- gradient_expert_down: float32 [8, 2048, 512], P('expert')
- gradient_expert_bias: float32 [8, 512], P('expert')
- gradient_gates: float32 [128, 197, 2], P(('expert', 'shard'))
- stream_magnitude: float32 [3], replicated
The draws below stay inside these ranges and needn't reach their ends.
Inputs may be any that keep to these rules, and one draw needn't show every extreme that they name: `routes`: the 2 experts of a token differ; among the tokens of one device no expert is named more than 394 times, and in every draw some device names some expert exactly 394 times.
All inputs are finite; a program needn't handle non-finite values.
Results may differ from the reference program's by a relative error of at most 0.019.
Values may be sent and summed in bfloat16 or wider, within the bound.
A program may use at most 128 MiB of HBM per device.

```python
import math
from functools import partial
import jax
import jax.numpy as jnp
import numpy as np
from jax import lax

D = 512
HEADS = 8
HEAD = 64
FF = 2048
SEQ = 197
TOP = 2
IMG_DEV = 4
EXPERTS = 8
TOK_DEV = 788
IMAGES = 128
CAP = 394


def draw_images(key, part):
    key_main, key_token = jax.random.split(key)
    rank_share = jnp.arange(IMAGES, dtype=jnp.float32) / max(IMAGES - 1, 1)
    row_scale = 0.3 * 10.0 ** rank_share
    sampled = jnp.clip(jax.random.normal(key_main, (IMAGES, SEQ, D), jnp.float32), -6.0, 6.0)
    token_scale = jnp.exp(jax.random.uniform(key_token, (IMAGES, SEQ, 1), jnp.float32, -0.35, 0.35))
    return (sampled * row_scale[:, None, None] * token_scale).astype(jnp.bfloat16)


def steps_of(own_key, shape, shards, smallest, largest):
    factor_of = 1.0
    for axis_at, shards_of in shards:
        draws = jax.random.uniform(jax.random.fold_in(jax.random.fold_in(own_key, 6), axis_at), (shards_of,), jnp.float32, smallest / len(shards), largest / len(shards))
        factor_of = factor_of * jnp.repeat(jnp.exp(draws), shape[axis_at] // shards_of).reshape((-1,) + (1,) * (len(shape) - 1 - axis_at))
    return factor_of


def routed_block(key, own, number, rows, count, top, limit, slope):
    sequence = jax.random.permutation(key, count)
    crowded, common = portions_of(count, rows * top, limit, slope, True), portions_of(count, rows * top, limit, slope, False)
    places = jnp.arange(count)

    def named(tallies, offset_by):
        used = int((tallies > 0).sum())
        fixed = max(1, used // 4)
        passed = fixed + (places - fixed + offset_by * (used - fixed)) % max(1, count - fixed)
        return jnp.zeros((count,), jnp.int32).at[sequence[jnp.where(places < fixed, places, passed)]].set(jnp.asarray(tallies, jnp.int32))

    tallies = jnp.where(number % 4 == 0, named(crowded, number // 4), named(common, number - number // 4 - 1))
    mixed = jax.random.permutation(jax.random.fold_in(own, 3), count)
    giver, taker = mixed[0:count // 2 * 2:2], mixed[1:count // 2 * 2:2]
    room = jnp.minimum(tallies[giver] - 1, limit - tallies[taker]) // 2
    room = jnp.where((giver == sequence[0]) | (taker == sequence[0]) | (tallies[taker] == 0), 0, jnp.maximum(room, 0))
    passed = jax.random.randint(jax.random.fold_in(own, 4), (count // 2,), 0, 1 << 20) % (room + 1)
    tallies = tallies.at[giver].add(-passed).at[taker].add(passed)
    items = jnp.searchsorted(jnp.cumsum(tallies), jnp.arange(rows * top), side="right").astype(jnp.int32)
    grid = items.reshape(top, rows).T
    grid = grid[jax.random.permutation(jax.random.fold_in(own, 1), rows)]
    offset_by = jax.random.randint(jax.random.fold_in(own, 2), (rows, 1), 0, top)
    return jnp.take_along_axis(grid, (jnp.arange(top)[None, :] + offset_by) % top, axis=1)


def portions_of(count, total, limit, slope, full):
    portions = [(1 << 20) // math.isqrt(grade ** slope) + 1 for grade in range(1, count + 1)]
    largest = limit if full else min(limit, max(-(-total // count), total * portions[0] // sum(portions)))
    least = 1 if total - largest >= count - 1 else 0
    given, surplus = [largest] + [least] * (count - 1), total - largest - least * (count - 1)
    while surplus > 0:
        movable = [i for i in range(1, count) if given[i] < largest] or [i for i in range(1, count) if given[i] < limit]
        pool, remaining = sum([portions[i] for i in movable]), surplus
        for i in movable:
            more = min(limit - given[i], max(1, remaining * portions[i] // pool), surplus)
            given[i] = given[i] + more
            surplus = surplus - more
    return np.array(given)


def noise(stream_key, dims, deviation, limit, cuts=(), kind=jnp.bfloat16):
    factor_of = steps_of(stream_key, dims, cuts, -0.22, 0.18) if cuts else 1.0
    drawn = jax.random.normal(stream_key, dims, jnp.float32) * deviation * factor_of
    return jnp.minimum(jnp.maximum(drawn, -limit), limit).astype(kind)


def setup_inputs(seed: int = 0) -> dict:
    key_of = jax.random.split(jax.random.key(seed), 14)
    images = draw_images(jax.random.fold_in(key_of[13], 71), 0)
    attention_in = noise(key_of[1], (D, 3 * D), D ** -0.5, 0.25, ((0, 4),))
    attention_out = noise(key_of[2], (D, D), (D // 8) ** -0.5, 0.75, ((0, 4),))
    layer_gain = jnp.clip(1.0 + 0.18 * jax.random.normal(key_of[3], (2, D), jnp.float32), 0.099609375, 1.8984375).astype(jnp.bfloat16)
    layer_shift = noise(key_of[4], (2, D), 0.5, 3.0, ((1, 4),))
    attention_bias = noise(key_of[5], (3, D), 0.5, 3.0, ((1, 4),))
    expert_up = noise(key_of[6], (EXPERTS, D, FF), D ** -0.5, 0.25, ((0, 8),))
    hidden_bias = noise(key_of[7], (EXPERTS, FF), 0.5, 3.0, ((0, 8),))
    expert_down = noise(key_of[8], (EXPERTS, FF, D), (FF // 2) ** -0.5, 0.1875, ((0, 8),))
    expert_bias = noise(key_of[9], (EXPERTS, D), 0.5, 3.0, ((0, 8),))
    routes_keys = jax.random.split(jax.random.fold_in(key_of[10], 1), IMAGES * SEQ // TOK_DEV)
    routes_turns = jax.random.permutation(jax.random.fold_in(key_of[10], 3), IMAGES * SEQ // TOK_DEV)
    routes = jax.vmap(lambda own, number: routed_block(jax.random.fold_in(key_of[10], 2), own, number, TOK_DEV, EXPERTS, TOP, CAP, 2))(routes_keys, routes_turns).reshape((IMAGES, SEQ, TOP))
    gates = jnp.clip(0.1 + 0.9 * jax.random.uniform(key_of[11], (IMAGES, SEQ, TOP), jnp.float32) ** steps_of(key_of[11], (IMAGES, SEQ, TOP), ((0, 32),), -0.2, 0.2), 0.1, 1.0)
    cotangent = noise(key_of[12], (IMAGES, SEQ, D), 1.0, 6.0, ((0, 32),))
    return {"images": images, "attention_in": attention_in, "attention_out": attention_out, "layer_gain": layer_gain, "layer_shift": layer_shift, "attention_bias": attention_bias, "expert_up": expert_up, "hidden_bias": hidden_bias, "expert_down": expert_down, "expert_bias": expert_bias, "routes": routes, "gates": gates, "cotangent": cotangent}


@jax.custom_vjp
def low(v):
    return lax.optimization_barrier(v.astype(jnp.bfloat16)).astype(jnp.float32)

@jax.custom_vjp
def low_back(v):
    return v

def low_keep(v):
    return (low(v), None)

def low_pass(kept, grad):
    return (grad,)

def back_keep(v):
    return (v, None)

def back_low(kept, grad):
    return (low(grad),)
low.defvjp(low_keep, low_pass)
low_back.defvjp(back_keep, back_low)
EPSILON = 1e-06
HIGHEST = lax.Precision.HIGHEST

def layer_norm(values, weight, offset):
    centre = values - lax.optimization_barrier(jnp.mean(values, axis=-1, keepdims=True))
    spread = lax.optimization_barrier(jnp.mean(centre * centre, axis=-1, keepdims=True))
    return centre * lax.rsqrt(spread + EPSILON) * weight + offset

def attention_part(block_rows, attention_in, attention_out, layer_gain, layer_shift, attention_bias):
    normed = low(layer_norm(block_rows, layer_gain[0], layer_shift[0]))
    projected = low_back(jnp.dot(normed, attention_in, precision=HIGHEST))
    shape_four = (IMG_DEV, SEQ, HEADS, HEAD)
    queries = low(projected[:, :D] + attention_bias[0]).reshape(shape_four)
    key_rows = low(projected[:, D:2 * D]).reshape(shape_four)
    values = low(projected[:, 2 * D:] + attention_bias[1]).reshape(shape_four)
    score_scale = 1.0 / math.sqrt(HEAD)
    scores = low_back(jnp.einsum('bqhd,bkhd->bhqk', queries, key_rows, precision=HIGHEST) * score_scale)
    weights = low(jax.nn.softmax(scores, axis=-1))
    context = jnp.einsum('bhqk,bkhd->bqhd', weights, values, precision=HIGHEST).reshape(IMG_DEV * SEQ, D)
    context = low(low_back(context))
    return low_back(jnp.dot(context, attention_out, precision=HIGHEST) + attention_bias[2])

def expert_part(packed):
    row_block, up_matrix, hidden_shift, down_matrix, output_shift = packed
    hidden = low_back(jnp.dot(row_block, up_matrix, precision=HIGHEST) + hidden_shift)
    active = low(jax.nn.gelu(hidden, approximate=False))
    return low(low_back(jnp.dot(active, down_matrix, precision=HIGHEST) + output_shift))

def forward(slot_index, images, attention_in, attention_out, layer_gain, layer_shift, attention_bias, expert_up, hidden_bias, expert_down, expert_bias, gates):
    groups = IMAGES // IMG_DEV
    stream = images.reshape(groups, IMG_DEV * SEQ, D)
    checked = jax.checkpoint(attention_part)

    def one_group(block_rows):
        return checked(block_rows, attention_in, attention_out, layer_gain, layer_shift, attention_bias)
    branch = lax.map(one_group, stream)
    middle = (stream + branch).reshape(IMAGES * SEQ, D)
    normed_two = low(layer_norm(middle, layer_gain[1], layer_shift[1]))
    paired = jnp.broadcast_to(normed_two[:, None, :], (IMAGES * SEQ, TOP, D)).reshape(IMAGES * SEQ * TOP, D)
    per_expert = groups * CAP
    routed = jnp.zeros((EXPERTS * per_expert, D), jnp.float32).at[slot_index].set(paired)
    routed = low_back(routed)
    produced = lax.map(jax.checkpoint(expert_part), (routed.reshape(EXPERTS, per_expert, D), expert_up, hidden_bias, expert_down, expert_bias))
    pair_out = produced.reshape(EXPERTS * per_expert, D)[slot_index].reshape(IMAGES * SEQ, TOP, D)
    block_stream = middle + lax.optimization_barrier(jnp.sum(pair_out * gates.reshape(IMAGES * SEQ, TOP)[:, :, None], axis=1))
    return (block_stream, middle)

def reference(images, attention_in, attention_out, layer_gain, layer_shift, attention_bias, expert_up, hidden_bias, expert_down, expert_bias, routes, gates, cotangent):
    pair_expert = routes.reshape(IMAGES * SEQ * TOP).astype(jnp.int32)
    labels = jnp.arange(EXPERTS, dtype=jnp.int32)
    onehot = (pair_expert[:, None] == labels[None, :]).astype(jnp.int32)
    position = lax.optimization_barrier(jnp.sum((jnp.cumsum(onehot, axis=0) - onehot) * onehot, axis=1)).astype(jnp.int32)
    slot_index = (pair_expert * (IMAGES // IMG_DEV * CAP) + position).astype(jnp.int32)
    floats = tuple((argument.astype(jnp.float32) for argument in (images, attention_in, attention_out, layer_gain, layer_shift, attention_bias, expert_up, hidden_bias, expert_down, expert_bias, gates)))
    block_stream, pullback, middle = jax.vjp(partial(forward, slot_index), *floats, has_aux=True)
    gradients = pullback(cotangent.reshape(IMAGES * SEQ, D).astype(jnp.float32))
    stream = floats[0]
    magnitude = jnp.sqrt(jnp.stack([jnp.mean(stream * stream), jnp.mean(middle * middle), jnp.mean(block_stream * block_stream)]))
    return (block_stream.astype(jnp.bfloat16).reshape(IMAGES, SEQ, D), gradients[0], gradients[1], gradients[2], gradients[3], gradients[4], gradients[5], gradients[6], gradients[7], gradients[8], gradients[9], gradients[10], magnitude)
```

```python
import functools

import jax
import jax.numpy as jnp
from jax import lax
from jax.experimental import pallas as pl
from jax.experimental.pallas import tpu as pltpu
from jax.sharding import PartitionSpec as P

HEAD = 64
SLAB = 2 * HEAD
TOP = 2
EPSILON = 1e-06
F32, BF16 = jnp.float32, jnp.bfloat16
VMEM_LIMIT = 60 * 1024 * 1024


def dot_of(contract):
    def run(left, right):
        return lax.dot_general(
            left, right, (contract, ((), ())), preferred_element_type=F32
        )

    return run


mm = dot_of(((1,), (0,)))
mt = dot_of(((1,), (1,)))
tm = dot_of(((0,), (0,)))


def up_to(value, step):
    return -(-value // step) * step


def normalize(values):
    centre = values - jnp.mean(values, axis=-1, keepdims=True)
    inverse = lax.rsqrt(jnp.mean(centre * centre, axis=-1, keepdims=True) + EPSILON)
    return centre * inverse, inverse


def normalize_back(incoming, unit, inverse, weight):
    scaled = incoming * weight
    first_mean = jnp.mean(scaled, axis=-1, keepdims=True)
    second_mean = jnp.mean(scaled * unit, axis=-1, keepdims=True)
    return inverse * (scaled - first_mean - unit * second_mean)


def gelu_pair(value):
    size = jnp.abs(value)
    t = 1.0 / (1.0 + (0.3275911 * 0.7071067811865476) * size)
    bell = jnp.exp(-0.5 * value * value)
    poly = 0.5 * 1.061405429
    for c in (-1.453152027, 1.421413741, -0.284496736, 0.254829592):
        poly = poly * t + 0.5 * c
    tail = poly * t * bell
    normal = jnp.where(value >= 0, 1.0 - tail, tail)
    return value * normal, normal + value * (bell * 0.3989422804014327)


def call(body, outs, args, scratch=(), cost=None):
    whole = pl.BlockSpec(memory_space=pltpu.VMEM)
    return pl.pallas_call(
        body,
        out_shape=[jax.ShapeDtypeStruct(s, d) for s, d in outs],
        in_specs=[whole] * len(args),
        out_specs=[whole] * len(outs),
        scratch_shapes=list(scratch),
        cost_estimate=cost,
        compiler_params=pltpu.CompilerParams(vmem_limit_bytes=VMEM_LIMIT),
    )(*args)


def place_kernel(col_in, row_in, col_out, row_out):
    tokens = col_in.shape[0]
    down = lax.broadcasted_iota(jnp.int32, (tokens, tokens), 0)
    across = lax.broadcasted_iota(jnp.int32, (tokens, tokens), 1)
    lanes = lax.broadcasted_iota(jnp.int32, col_out.shape, 1)
    named = (col_in[:, 0:1] == lanes) | (col_in[:, 1:2] == lanes)
    before = (across < down).astype(F32).astype(BF16)
    ranks = mm(before, named.astype(F32).astype(BF16))
    col_out[...] = jnp.where(named, ranks, -1.0)
    lines = lax.broadcasted_iota(jnp.int32, row_out.shape, 0)
    named = (row_in[0:1, :] == lines) | (row_in[1:2, :] == lines)
    before = (down < across).astype(F32).astype(BF16)
    ranks = mm(named.astype(F32).astype(BF16), before)
    row_out[...] = jnp.where(named, ranks, -1.0)


def chosen(row_ref, expert, slots):
    tokens = row_ref.shape[1]
    index = lax.broadcasted_iota(jnp.int32, (slots, tokens), 0).astype(F32)
    return jnp.where(index == row_ref[pl.ds(expert, 1), :], 1.0, 0.0).astype(BF16)


def taken(col, expert, slots):
    index = lax.broadcasted_iota(jnp.int32, (col.shape[0], slots), 1).astype(F32)
    return jnp.where(index == col[:, expert : expert + 1], 1.0, 0.0).astype(BF16)


def dispatch_grads_kernel(cot, gates, routes, row, out):
    experts, slots, _ = out.shape
    upstream = cot[...].astype(F32)
    for e in range(experts):
        gate = jnp.where(routes[:, 0:1] == e, gates[:, 0:1], 0.0) + jnp.where(
            routes[:, 1:2] == e, gates[:, 1:2], 0.0
        )
        scaled = (upstream * gate).astype(BF16)
        out[e] = mm(chosen(row, e, slots), scaled).astype(BF16)


def forward_kernel(
    images, real, x, w_in, w_out, gain, shift, bias, row, middle_out, qkv, context, send, squares, ctx_t
):
    tokens, width = x.shape
    lines = tokens // images
    stream = x[...].astype(F32)
    unit, _ = normalize(stream)
    normed = (unit * gain[0:1, :] + shift[0:1, :]).astype(BF16)
    projected = mm(normed, w_in[...])
    qkv[:, :width] = (projected[:, :width] + bias[0:1, :]).astype(BF16)
    qkv[:, width : 2 * width] = projected[:, width : 2 * width].astype(BF16)
    qkv[:, 2 * width :] = (projected[:, 2 * width :] + bias[1:2, :]).astype(BF16)
    valid = lax.broadcasted_iota(jnp.int32, (lines, lines), 0) < real
    half = lax.broadcasted_iota(jnp.int32, (lines, SLAB), 1) < HEAD

    def one_image(i, carry):
        rows = pl.ds(pl.multiple_of(i * lines, 16), lines)
        for s in range(width // SLAB):
            q = qkv[rows, s * SLAB : (s + 1) * SLAB]
            k = qkv[rows, width + s * SLAB : width + (s + 1) * SLAB]
            v = qkv[rows, 2 * width + s * SLAB : 2 * width + (s + 1) * SLAB]
            parts = []
            for h in range(2):
                keep = half if h == 0 else ~half
                scores = mt(jnp.where(keep, k, jnp.zeros_like(k)), q) * (HEAD**-0.5)
                scores = jnp.where(valid, scores, -1e30)
                powers = jnp.exp(scores - jnp.max(scores, axis=0, keepdims=True))
                soft = powers / jnp.sum(powers, axis=0, keepdims=True)
                parts.append(tm(soft.astype(BF16), v))
            context[rows, s * SLAB : (s + 1) * SLAB] = jnp.where(half, parts[0], parts[1]).astype(BF16)
        return carry

    lax.fori_loop(0, images, one_image, 0)
    middle = stream + mm(context[...], w_out[...]) + bias[2:3, :]
    middle_out[...] = middle
    unit, _ = normalize(middle)
    normed = (unit * gain[1:2, :] + shift[1:2, :]).astype(BF16)
    experts, slots, _ = send.shape
    for e in range(experts):
        send[e] = mm(chosen(row, e, slots), normed).astype(BF16)
    index = lax.broadcasted_iota(jnp.int32, (tokens, 1), 0)
    counts = jnp.where(lax.rem(index, lines) < real, 1.0, 0.0)
    squares[0:1, :] = jnp.sum(stream * stream, axis=0, keepdims=True)
    squares[1:2, :] = jnp.sum(middle * middle * counts, axis=0, keepdims=True)


def expert_kernel(
    chunk, rows, grads, up, hidden_bias, down, out_bias, made, back, d_up, d_hidden, d_down, d_out, sum_up, sum_down
):
    step, steps = pl.program_id(0), pl.num_programs(0)

    @pl.when(step == 0)
    def _():
        sum_up[...] = jnp.zeros_like(sum_up)
        sum_down[...] = jnp.zeros_like(sum_down)
        d_hidden[...] = jnp.zeros_like(d_hidden)
        d_out[...] = jnp.zeros_like(d_out)

    x, g = rows[...], grads[...]
    produced = jnp.zeros(x.shape, F32)
    routed = jnp.zeros(x.shape, F32)
    for j in range(up.shape[1] // chunk):
        cols = slice(j * chunk, (j + 1) * chunk)
        hidden = mm(x, up[:, cols]) + hidden_bias[:, cols]
        back_active = mt(g, down[cols, :])
        active, slope = gelu_pair(hidden)
        active = active.astype(BF16)
        back_hidden = back_active * slope
        d_hidden[:, cols] += jnp.sum(back_hidden, axis=0, keepdims=True)
        back_hidden = back_hidden.astype(BF16)
        produced += mm(active, down[cols, :])
        routed += mt(back_hidden, up[:, cols])
        sum_up[:, cols] += tm(x, back_hidden)
        sum_down[:, cols] += tm(g, active)
    d_out[...] += jnp.sum(g.astype(F32), axis=0, keepdims=True)
    made[...] = (produced + out_bias[...]).astype(BF16)
    back[...] = routed.astype(BF16)

    @pl.when(step == steps - 1)
    def _():
        d_up[...] = sum_up[...].astype(BF16)
        d_down[...] = sum_down[...].T.astype(BF16)


def backward_kernel(
    images, real, x, w_in, w_out, gain, shift, qkv, context, middle, cot, col, back,
    d_x, d_in, d_out, d_gain, d_shift, d_bias, d_qkv, d_context,
):
    tokens, width = x.shape
    lines = tokens // images
    experts, slots, _ = back.shape
    back_two = jnp.zeros((tokens, width), F32)
    for e in range(experts):
        back_two += mm(taken(col, e, slots), back[e])
    unit, inverse = normalize(middle[...])
    d_gain[1:2, :] = jnp.sum(back_two * unit, axis=0, keepdims=True)
    d_shift[1:2, :] = jnp.sum(back_two, axis=0, keepdims=True)
    back_middle = cot[...].astype(F32) + normalize_back(back_two, unit, inverse, gain[1:2, :])
    d_x[...] = back_middle
    branch = back_middle.astype(BF16)
    d_bias[2:3, :] = jnp.sum(branch.astype(F32), axis=0, keepdims=True)
    d_out[...] = tm(context[...], branch).astype(BF16)
    d_context[...] = mt(branch, w_out[...]).astype(BF16)
    valid = lax.broadcasted_iota(jnp.int32, (lines, lines), 0) < real
    half = lax.broadcasted_iota(jnp.int32, (lines, SLAB), 1) < HEAD
    scale = HEAD**-0.5
    d_bias[0:2, :] = jnp.zeros((2, width), F32)

    def one_image(i, carry):
        rows = pl.ds(pl.multiple_of(i * lines, 16), lines)
        for s in range(width // SLAB):
            cols = [slice(a * width + s * SLAB, a * width + (s + 1) * SLAB) for a in range(3)]
            q, k, v = (qkv[rows, c] for c in cols)
            given = d_context[rows, cols[0]]
            parts = []
            for h in range(2):
                keep = half if h == 0 else ~half
                zero = jnp.zeros_like(k)
                scores = mt(jnp.where(keep, k, zero), q) * scale
                scores = jnp.where(valid, scores, -1e30)
                powers = jnp.exp(scores - jnp.max(scores, axis=0, keepdims=True))
                soft = powers / jnp.sum(powers, axis=0, keepdims=True)
                back_soft = mt(jnp.where(keep, v, zero), given)
                shared = jnp.sum(back_soft * soft, axis=0, keepdims=True)
                back_scores = (soft * (back_soft - shared)).astype(BF16)
                parts.append((tm(back_scores, k), mm(back_scores, q), mm(soft.astype(BF16), given)))
            grads = [jnp.where(half, a, b) for a, b in zip(*parts)]
            grads = [grads[0] * scale, grads[1] * scale, grads[2]]
            d_bias[0:1, cols[0]] += jnp.sum(grads[0], axis=0, keepdims=True)
            d_bias[1:2, cols[0]] += jnp.sum(grads[2], axis=0, keepdims=True)
            for c, grad in zip(cols, grads):
                d_qkv[rows, c] = grad.astype(BF16)
        return carry

    lax.fori_loop(0, images, one_image, 0)
    unit, inverse = normalize(x[...].astype(F32))
    normed = (unit * gain[0:1, :] + shift[0:1, :]).astype(BF16)
    d_in[...] = tm(normed, d_qkv[...]).astype(BF16)
    back_one = mt(d_qkv[...], w_in[...])
    d_gain[0:1, :] = jnp.sum(back_one * unit, axis=0, keepdims=True)
    d_shift[0:1, :] = jnp.sum(back_one, axis=0, keepdims=True)
    d_x[...] += normalize_back(back_one, unit, inverse, gain[0:1, :])


def output_kernel(lines, real, middle, cot, gates, routes, col, returned, out, d_gates, squares):
    tokens, width = middle.shape
    experts, slots, _ = returned.shape
    rows = [jnp.zeros((tokens, width), F32) for _ in range(TOP)]
    for r in range(TOP):
        for e in range(experts):
            mine = jnp.where(routes[:, r : r + 1] == e, col[:, e : e + 1], -1.0)
            rows[r] += mm(taken(mine, 0, slots), returned[e])
    upstream = cot[...].astype(F32)
    total = middle[...]
    for r in range(TOP):
        total += rows[r] * gates[:, r : r + 1]
        d_gates[:, r : r + 1] = jnp.sum(rows[r] * upstream, axis=1, keepdims=True)
    out[...] = total.astype(BF16)
    index = lax.broadcasted_iota(jnp.int32, (tokens, 1), 0)
    counts = jnp.where(lax.rem(index, lines) < real, 1.0, 0.0)
    squares[...] = jnp.sum(total * total * counts, axis=0, keepdims=True)


def local(
    images, attention_in, attention_out, layer_gain, layer_shift, attention_bias, expert_up, hidden_bias,
    expert_down, expert_bias, routes, gates, cotangent,
):
    count, real, width = images.shape
    lines = up_to(real, 16)
    tokens = count * lines
    experts = lax.axis_size("expert")
    shards = lax.axis_size("shard")
    slots = up_to(max(2, 4 * count * real // experts), 16)
    hidden_units = expert_up.shape[2]

    def padded(values, fill=0):
        wide = jnp.pad(values, ((0, 0), (0, lines - real), (0, 0)), constant_values=fill)
        return wide.reshape(tokens, values.shape[2])

    matrices = jnp.concatenate([attention_in, attention_out], axis=1)
    vectors = jnp.concatenate([layer_gain, layer_shift, attention_bias], axis=0)
    matrices = lax.all_gather(matrices, "shard", axis=0, tiled=True)
    vectors = lax.all_gather(vectors, "shard", axis=1, tiled=True).astype(F32)
    full_in, full_out = matrices[:, : 3 * width], matrices[:, 3 * width :]
    gain, shift, bias = vectors[0:2], vectors[2:4], vectors[4:7]

    x, cot = padded(images), padded(cotangent)
    route_col, gate_col = padded(routes, -1), padded(gates)
    col, row = call(
        place_kernel,
        [((tokens, up_to(experts, 128)), F32), ((up_to(experts, 8), tokens), F32)],
        [route_col, route_col.T],
    )
    block = (experts, slots, width)
    send_grads = call(dispatch_grads_kernel, [(block, BF16)], [cot, gate_col, route_col, row])[0]
    exchange = functools.partial(
        lax.all_to_all, axis_name="expert", split_axis=0, concat_axis=0, tiled=True
    )
    grads = exchange(send_grads)
    middle, qkv, context, send_rows, squares = call(
        functools.partial(forward_kernel, count, real),
        [
            ((tokens, width), F32), ((tokens, 3 * width), BF16), ((tokens, width), BF16), (block, BF16),
            ((2, width), F32),
        ],
        [x, full_in, full_out, gain, shift, bias, row],
        [pltpu.VMEM((8, 128), F32)],
    )
    rows = exchange(send_rows)

    every = experts * slots
    steps = 8
    size = every // steps
    tile = lambda: pl.BlockSpec((size, width), lambda i: (i, 0))
    fixed = lambda *shape: pl.BlockSpec(shape, lambda i: (0, 0))
    made, back, d_up, d_hidden, d_down, d_eb = pl.pallas_call(
        functools.partial(expert_kernel, 512),
        grid=(steps,),
        out_shape=[
            jax.ShapeDtypeStruct((every, width), BF16),
            jax.ShapeDtypeStruct((every, width), BF16),
            jax.ShapeDtypeStruct((width, hidden_units), BF16),
            jax.ShapeDtypeStruct((1, hidden_units), F32),
            jax.ShapeDtypeStruct((hidden_units, width), BF16),
            jax.ShapeDtypeStruct((1, width), F32),
        ],
        in_specs=[
            tile(), tile(), fixed(width, hidden_units), fixed(1, hidden_units), fixed(hidden_units, width),
            fixed(1, width),
        ],
        out_specs=[
            tile(), tile(), fixed(width, hidden_units), fixed(1, hidden_units), fixed(hidden_units, width),
            fixed(1, width),
        ],
        scratch_shapes=[pltpu.VMEM((width, hidden_units), F32), pltpu.VMEM((width, hidden_units), F32)],
        compiler_params=pltpu.CompilerParams(vmem_limit_bytes=VMEM_LIMIT),
    )(
        rows.reshape(every, width), grads.reshape(every, width), expert_up[0], hidden_bias.astype(F32),
        expert_down[0], expert_bias.astype(F32),
    )
    routed = exchange(back.reshape(block))
    returned = exchange(made.reshape(block))
    up_total = lax.psum(d_up, "shard").astype(F32)
    down_total = lax.psum(d_down, "shard").astype(F32)
    small = jnp.concatenate([d_hidden, d_eb], axis=1).astype(BF16)
    small = lax.psum(small, "shard").astype(F32)

    d_x, d_in, d_out, d_gain, d_shift, d_bias = call(
        functools.partial(backward_kernel, count, real),
        [
            ((tokens, width), F32), ((width, 3 * width), BF16), ((width, width), BF16), ((2, width), F32),
            ((2, width), F32), ((3, width), F32),
        ],
        [x, full_in, full_out, gain, shift, qkv, context, middle, cot, col, routed],
        [pltpu.VMEM((tokens, 3 * width), BF16), pltpu.VMEM((tokens, width), BF16)],
    )
    block_output, d_gates, last = call(
        functools.partial(output_kernel, lines, real),
        [((tokens, width), BF16), ((tokens, TOP), F32), ((1, width), F32)],
        [middle, cot, gate_col, route_col, col, returned],
    )
    sums = jnp.sum(jnp.concatenate([squares, last], axis=0), axis=1)
    sums = lax.psum(sums, ("expert", "shard"))
    magnitude = jnp.sqrt(sums / float(count * real * width * experts * shards))

    seven = jnp.concatenate([d_gain, d_shift, d_bias], axis=0).astype(BF16)
    seven = jnp.pad(seven, ((0, 1), (0, 0))).T
    owned = jnp.concatenate([d_in, d_out, jnp.pad(seven, ((0, 0), (0, 120)))], axis=1)
    owned = lax.psum_scatter(owned, "shard", scatter_dimension=0, tiled=True)
    owned = lax.psum(owned, "expert").astype(F32)
    vectors = owned[:, 4 * width : 4 * width + 8].T

    def cut(values):
        return values.reshape(count, lines, values.shape[1])[:, :real]

    return (
        cut(block_output),
        cut(d_x),
        owned[:, : 3 * width],
        owned[:, 3 * width : 4 * width],
        vectors[0:2],
        vectors[2:4],
        vectors[4:7],
        up_total[None],
        small[:, :hidden_units],
        down_total[None],
        small[:, hidden_units:],
        cut(d_gates),
        magnitude,
    )


def solution(mesh):
    every = P(("expert", "shard"), None, None)
    return jax.shard_map(
        local,
        mesh=mesh,
        in_specs=(
            every, P("shard", None), P("shard", None), P(None, "shard"), P(None, "shard"), P(None, "shard"),
            P("expert", None, None), P("expert", None), P("expert", None, None), P("expert", None),
            every, every, every,
        ),
        out_specs=(
            every, every, P("shard", None), P("shard", None), P(None, "shard"), P(None, "shard"),
            P(None, "shard"), P("expert", None, None), P("expert", None), P("expert", None, None),
            P("expert", None), every, P(),
        ),
        check_vma=False,
    )
```

```python
import functools

import jax
import jax.numpy as jnp
from jax import lax
from jax.experimental import pallas as pl
from jax.experimental.pallas import tpu as pltpu
from jax.sharding import PartitionSpec as P

HEAD = 64
SLAB = 2 * HEAD
TOP = 2
EPSILON = 1e-06
F32, BF16 = jnp.float32, jnp.bfloat16
VMEM_LIMIT = 60 * 1024 * 1024


def dot_of(contract):
    def run(left, right):
        return lax.dot_general(
            left, right, (contract, ((), ())), preferred_element_type=F32
        )

    return run


mm = dot_of(((1,), (0,)))
mt = dot_of(((1,), (1,)))
tm = dot_of(((0,), (0,)))


def up_to(value, step):
    return -(-value // step) * step


def normalize(values):
    centre = values - jnp.mean(values, axis=-1, keepdims=True)
    inverse = lax.rsqrt(jnp.mean(centre * centre, axis=-1, keepdims=True) + EPSILON)
    return centre * inverse, inverse


def normalize_back(incoming, unit, inverse, weight):
    scaled = incoming * weight
    first_mean = jnp.mean(scaled, axis=-1, keepdims=True)
    second_mean = jnp.mean(scaled * unit, axis=-1, keepdims=True)
    return inverse * (scaled - first_mean - unit * second_mean)


def gelu_pair(value):
    size = jnp.abs(value)
    t = 1.0 / (1.0 + (0.3275911 * 0.7071067811865476) * size)
    bell = jnp.exp(-0.5 * value * value)
    poly = 0.5 * 1.061405429
    for c in (-1.453152027, 1.421413741, -0.284496736, 0.254829592):
        poly = poly * t + 0.5 * c
    tail = poly * t * bell
    normal = jnp.where(value >= 0, 1.0 - tail, tail)
    return value * normal, normal + value * (bell * 0.3989422804014327)


def call(body, outs, args, scratch=(), outside=(), collective=None):
    where = [
        pl.BlockSpec(memory_space=pl.ANY if i in outside else pltpu.VMEM) for i in range(len(args) + len(outs))
    ]
    return pl.pallas_call(
        body,
        out_shape=[jax.ShapeDtypeStruct(s, d) for s, d in outs],
        in_specs=where[: len(args)],
        out_specs=where[len(args) :],
        scratch_shapes=list(scratch),
        compiler_params=pltpu.CompilerParams(
            vmem_limit_bytes=VMEM_LIMIT, collective_id=collective, has_side_effects=collective is not None
        ),
    )(*args)


def axes():
    return (
        lax.axis_index("expert"), lax.axis_index("shard"), lax.axis_size("expert"), lax.axis_size("shard")
    )


def home(shard, shards):
    core = shard % 2
    return (shard // 2) * (1 - core) + (shards - 1 - shard // 2) * core


def expert_of(member, experts, shards):
    return home(member % shards, shards) * (experts // shards) + member // shards


class Place:
    def __init__(self):
        self.expert, self.shard, self.experts, self.shards = axes()
        self.width = self.experts // self.shards
        self.row = lax.div(self.expert, self.width)
        self.member = lax.rem(self.expert, self.width) * self.shards + self.shard
        self.core = lax.rem(self.shard, 2)
        self.chip = lax.div(self.shard, 2)
        self.root = self.chip * (1 - self.core) + (self.shards - 1 - self.chip) * self.core

    def peer(self, step):
        other = lax.rem(self.member + step, self.experts)
        return other, (self.row * self.width + lax.div(other, self.shards), lax.rem(other, self.shards))

    def along(self, step):
        return (self.expert + step * self.width, self.shard)

    def greet(self):
        barrier = pltpu.get_barrier_semaphore()
        for step in range(1, self.experts):
            tell(barrier, self.peer(step)[1])
        pl.when(self.row > 0)(lambda: tell(barrier, self.along(-1)))
        pl.when(self.row < self.shards - 1)(lambda: tell(barrier, self.along(1)))
        ends = jnp.where(self.row > 0, 1, 0) + jnp.where(self.row < self.shards - 1, 1, 0)
        pl.semaphore_wait(barrier, self.experts - 1 + ends)


def tell(semaphore, device):
    pl.semaphore_signal(semaphore, inc=1, device_id=device, device_id_type=pl.DeviceIdType.MESH)


def remote(src, dst, sent, came, device):
    return pltpu.make_async_remote_copy(
        src_ref=src, dst_ref=dst, send_sem=sent, recv_sem=came, device_id=device,
        device_id_type=pl.DeviceIdType.MESH,
    )


def exchange_copies(place, send, recv, sent, came):
    copies = []
    for step in range(1, place.experts):
        other, device = place.peer(step)
        copies.append(remote(send.at[other], recv.at[place.member], sent.at[step], came.at[step], device))
    own = pltpu.make_async_copy(send.at[place.member], recv.at[place.member], sent.at[0])
    return [own, *copies]


def placed(col_in, row_in, col_shape, row_shape):
    tokens = col_in.shape[0]
    down = lax.broadcasted_iota(jnp.int32, (tokens, tokens), 0)
    across = lax.broadcasted_iota(jnp.int32, (tokens, tokens), 1)
    lanes = lax.broadcasted_iota(jnp.int32, col_shape, 1)
    named = (col_in[:, 0:1] == lanes) | (col_in[:, 1:2] == lanes)
    before = (across < down).astype(F32).astype(BF16)
    ranks = mm(before, named.astype(F32).astype(BF16))
    col = jnp.where(named, ranks, -1.0)
    lines = lax.broadcasted_iota(jnp.int32, row_shape, 0)
    named = (row_in[0:1, :] == lines) | (row_in[1:2, :] == lines)
    before = (down < across).astype(F32).astype(BF16)
    ranks = mm(named.astype(F32).astype(BF16), before)
    return col, jnp.where(named, ranks, -1.0)


def chosen(row_ref, expert, slots):
    tokens = row_ref.shape[1]
    index = lax.broadcasted_iota(jnp.int32, (slots, tokens), 0).astype(F32)
    return jnp.where(index == row_ref[expert : expert + 1, :], 1.0, 0.0).astype(BF16)


def taken(col, expert, slots):
    index = lax.broadcasted_iota(jnp.int32, (col.shape[0], slots), 1).astype(F32)
    return jnp.where(index == col[:, expert : expert + 1], 1.0, 0.0).astype(BF16)


def ready_kernel(
    images, real, parts,
    x, cot, gates, routes, routes_row, mats, vecs, up, down, biases,
    rows_in, grads_in, up_out, down_out, biases_out, middle_out, qkv, context, squares, full, rows_of, col,
    send_grads, send_rows, row, vec_all, sent_g, came_g, sent_r, came_r, sent_p, came_p, sent_v, came_v,
    sent_w, came_w,
):
    place = Place()
    tokens, width = x.shape
    lines = tokens // images
    experts, slots, _ = send_rows.shape
    shards = place.shards
    place.greet()

    share = mats.shape[0]
    mine = pl.ds(place.shard * share, share)
    partner = (place.expert, place.shard + 1 - 2 * place.core)
    own = [
        pltpu.make_async_copy(mats, full.at[mine], sent_p.at[0]),
        pltpu.make_async_copy(vecs, vec_all.at[place.shard], sent_v.at[0]),
    ]
    for c in own:
        c.start()
    chips = []
    for step in range(1, shards // 2):
        there = (place.expert, lax.rem(place.chip + step, shards // 2) * 2 + place.core)
        chips.append(remote(mats, full.at[mine], sent_p.at[step], came_p.at[step], there))
        chips.append(remote(vecs, vec_all.at[place.shard], sent_v.at[step], came_v.at[step], there))
    for c in chips:
        c.start()

    def pieces(k, here, there, sent, came, device):
        wide = up.shape[1] // parts
        cols, lots = pl.ds(k * wide, wide), pl.ds(k * wide, wide)
        out = [
            remote(here[0].at[:, cols], there[0].at[:, cols], sent.at[3 * k], came.at[3 * k], device),
            remote(here[1].at[lots, :], there[1].at[lots, :], sent.at[3 * k + 1], came.at[3 * k + 1], device),
        ]
        if k == 0:
            out.append(remote(here[2], there[2], sent.at[3 * k + 2], came.at[3 * k + 2], device))
        return out

    held, landed = (up, down, biases), (up_out, down_out, biases_out)
    rightmost = place.shards - 1
    local = [pltpu.make_async_copy(h, t, sent_w.at[2, i]) for i, (h, t) in enumerate(zip(held, landed))]

    def matrices(k, source, way):
        return pieces(k, source, landed, sent_w.at[(way + 1) // 2], came_w, place.along(way))

    def start_all(copies):
        for c in copies:
            c.start()

    @pl.when(place.row == place.root)
    def _():
        start_all(local)
        for way, more in ((-1, place.row > 0), (1, place.row < rightmost)):

            @pl.when(more)
            def _(way=way):
                for k in range(parts):
                    start_all(matrices(k, held, way))

    def pass_on(k):
        @pl.when(place.row != place.root)
        def _():
            for c in matrices(k, landed, 1):
                c.wait_recv()

        for way, more in (
            (-1, (place.row > 0) & (place.row < place.root)),
            (1, (place.row < rightmost) & (place.row > place.root)),
        ):

            @pl.when(more)
            def _(way=way):
                start_all(matrices(k, landed, way))

    col_all, row_all = placed(routes, routes_row, col.shape, row.shape)
    col[...] = col_all
    row[...] = row_all
    upstream = cot[...].astype(F32)
    for j in range(experts):
        e = expert_of(j, experts, shards)
        gate = jnp.where(routes[:, 0:1] == e, gates[:, 0:1], 0.0) + jnp.where(
            routes[:, 1:2] == e, gates[:, 1:2], 0.0
        )
        send_grads[j] = mm(chosen(row, e, slots), (upstream * gate).astype(BF16)).astype(BF16)
    swap_g = exchange_copies(place, send_grads, grads_in, sent_g, came_g)
    start_all(swap_g)

    over = []
    for step in range(shards // 2):
        source = lax.rem(place.chip + step, shards // 2) * 2 + place.core
        block = pl.ds(source * share, share)
        if step:
            back = shards // 2 - step
            chips[2 * back - 2].wait_recv()
            chips[2 * back - 1].wait_recv()
        else:
            own[0].wait()
            own[1].wait()
        at = shards // 2 + step
        over.append(remote(full.at[block], full.at[block], sent_p.at[at], came_p.at[at], partner))
        over.append(remote(vec_all.at[source], vec_all.at[source], sent_v.at[at], came_v.at[at], partner))
        over[-2].start()
        over[-1].start()
    for c in over:
        c.wait_recv()
    vectors = vec_all[0]
    for s in range(1, shards):
        vectors = vectors + vec_all[s]
    rows_of[...] = vectors
    gain, shift, bias = vectors[0:2], vectors[2:4], vectors[4:7]
    w_in, w_out = full.at[:, : 3 * width], full.at[:, 3 * width :]
    pass_on(0)

    stream = x[...].astype(F32)
    unit, _ = normalize(stream)
    normed = (unit * gain[0:1, :] + shift[0:1, :]).astype(BF16)
    projected = mm(normed, w_in[...])
    qkv[:, :width] = (projected[:, :width] + bias[0:1, :]).astype(BF16)
    qkv[:, width : 2 * width] = projected[:, width : 2 * width].astype(BF16)
    qkv[:, 2 * width :] = (projected[:, 2 * width :] + bias[1:2, :]).astype(BF16)
    valid = lax.broadcasted_iota(jnp.int32, (lines, lines), 0) < real
    half = lax.broadcasted_iota(jnp.int32, (lines, SLAB), 1) < HEAD

    def one_image(i, carry):
        rows = pl.ds(pl.multiple_of(i * lines, 16), lines)
        for s in range(width // SLAB):
            q = qkv[rows, s * SLAB : (s + 1) * SLAB]
            k = qkv[rows, width + s * SLAB : width + (s + 1) * SLAB]
            v = qkv[rows, 2 * width + s * SLAB : 2 * width + (s + 1) * SLAB]
            heads = []
            for h in range(2):
                keep = half if h == 0 else ~half
                scores = mt(jnp.where(keep, k, jnp.zeros_like(k)), q) * (HEAD**-0.5)
                scores = jnp.where(valid, scores, -1e30)
                powers = jnp.exp(scores - jnp.max(scores, axis=0, keepdims=True))
                soft = powers / jnp.sum(powers, axis=0, keepdims=True)
                heads.append(tm(soft.astype(BF16), v))
            context[rows, s * SLAB : (s + 1) * SLAB] = jnp.where(half, heads[0], heads[1]).astype(BF16)
        return carry

    lax.fori_loop(0, images, one_image, 0)
    middle = stream + mm(context[...], w_out[...]) + bias[2:3, :]
    middle_out[...] = middle
    unit, _ = normalize(middle)
    normed = (unit * gain[1:2, :] + shift[1:2, :]).astype(BF16)
    for j in range(experts):
        send_rows[j] = mm(chosen(row, expert_of(j, experts, shards), slots), normed).astype(BF16)
    swap_r = exchange_copies(place, send_rows, rows_in, sent_r, came_r)
    start_all(swap_r)
    index = lax.broadcasted_iota(jnp.int32, (tokens, 1), 0)
    counts = jnp.where(lax.rem(index, lines) < real, 1.0, 0.0)
    squares[0:1, :] = jnp.sum(stream * stream, axis=0, keepdims=True)
    squares[1:2, :] = jnp.sum(middle * middle * counts, axis=0, keepdims=True)

    for k in range(1, parts):
        pass_on(k)
    for c in swap_g + swap_r:
        c.wait()
    for c in chips + over:
        c.wait_send()

    @pl.when(place.row == place.root)
    def _():
        for c in local:
            c.wait()

    for way, more in (
        (-1, (place.row > 0) & (place.row <= place.root)),
        (1, (place.row < rightmost) & (place.row >= place.root)),
    ):

        @pl.when(more)
        def _(way=way):
            for k in range(parts):
                for c in matrices(k, landed, way):
                    c.wait_send()


def give_back_kernel(
    parts, back, made, up, down, small,
    back_out, made_out, up_out, down_out, small_out,
    up_l, down_l, small_l, up_r, down_r, small_r,
    sent_b, came_b, sent_m, came_m, sent_c, came_l, came_r, sent_d, came_d, sent_o, came_o,
):
    place = Place()
    place.greet()
    swap_b = exchange_copies(place, back, back_out, sent_b, came_b)
    for c in swap_b:
        c.start()
    swap_m = exchange_copies(place, made, made_out, sent_m, came_m)
    for c in swap_m:
        c.start()
    rightmost = place.shards - 1
    row, root = place.row, place.root
    own, out = (up, down, small), (up_out, down_out, small_out)
    left, right = (up_l, down_l, small_l), (up_r, down_r, small_r)
    heights = (up.shape[0] // parts, down.shape[0] // parts)

    def piece(ref, i, k):
        return ref if i == 2 else ref.at[pl.ds(k * heights[i], heights[i])]

    def of(k):
        return range(3) if k == 0 else range(2)

    def hop(k, source, target, came, way):
        return [
            remote(piece(source[i], i, k), piece(target[i], i, k), sent_c.at[3 * k + i], came.at[3 * k + i], place.along(way))
            for i in of(k)
        ]

    def add(k, target, terms):
        for i in of(k):
            total = piece(terms[0][i], i, k)[...].astype(F32)
            for t in terms[1:]:
                total += piece(t[i], i, k)[...].astype(F32)
            piece(target[i], i, k)[...] = total.astype(target[i].dtype)

    def wait_for(k, buffer, came):
        for c in hop(k, buffer, buffer, came, 1):
            c.wait_recv()

    def go(copies):
        for c in copies:
            c.start()

    def chain(k):
        pl.when((row == 0) & (root > 0))(lambda: go(hop(k, own, left, came_l, 1)))
        pl.when((row == rightmost) & (root < rightmost))(lambda: go(hop(k, own, right, came_r, -1)))

        @pl.when((row > 0) & (row < root))
        def _():
            wait_for(k, left, came_l)
            add(k, left, [own, left])
            go(hop(k, left, left, came_l, 1))

        @pl.when((row < rightmost) & (row > root))
        def _():
            wait_for(k, right, came_r)
            add(k, right, [own, right])
            go(hop(k, right, right, came_r, -1))

        @pl.when((row == root) & (row > 0))
        def _():
            wait_for(k, left, came_l)
            add(k, out, [own, left])

        @pl.when((row == root) & (row == 0))
        def _():
            add(k, out, [own])

        @pl.when((row == root) & (row < rightmost))
        def _():
            wait_for(k, right, came_r)
            add(k, out, [out, right])

        @pl.when(row == root)
        def _():
            for step in range(1, place.shards // 2):
                go(spread(k, step))
            go(cross(k))

    root_core = jnp.where(row < place.shards // 2, 0, 1)
    root_chip = jnp.where(row < place.shards // 2, row, place.shards - 1 - row)

    def spread(k, step):
        there = (place.expert, lax.rem(place.chip + step, place.shards // 2) * 2 + place.core)
        at = lambda i: (step - 1, 3 * k + i)
        return [
            remote(piece(out[i], i, k), piece(out[i], i, k), sent_d.at[at(i)], came_d.at[3 * k + i], there) for i in of(k)
        ]

    def cross(k):
        there = (place.expert, place.shard + 1 - 2 * place.core)
        return [
            remote(piece(out[i], i, k), piece(out[i], i, k), sent_o.at[3 * k + i], came_o.at[3 * k + i], there) for i in of(k)
        ]

    def hand_out(k):
        @pl.when((place.core == root_core) & (place.chip != root_chip))
        def _():
            for c in spread(k, 1):
                c.wait_recv()
            go(cross(k))

        @pl.when(place.core != root_core)
        def _():
            for c in cross(k):
                c.wait_recv()

    lag = 3
    for k in range(parts + lag):
        if k < parts:
            chain(k)
        if k >= lag:
            hand_out(k - lag)
    for k in range(parts):

        @pl.when(row != root)
        def _(k=k):
            for c in hop(k, left, left, came_l, 1):
                c.wait_send()

        @pl.when(row == root)
        def _(k=k):
            for step in range(1, place.shards // 2):
                for c in spread(k, step):
                    c.wait_send()

        @pl.when(place.core == root_core)
        def _(k=k):
            for c in cross(k):
                c.wait_send()

    for c in swap_b + swap_m:
        c.wait()


def expert_kernel(
    chunk, rows, grads, up, hidden_bias, down, out_bias, made, back, d_up, d_hidden, d_down, d_out, sum_up, sum_down
):
    step, steps = pl.program_id(0), pl.num_programs(0)

    @pl.when(step == 0)
    def _():
        sum_up[...] = jnp.zeros_like(sum_up)
        sum_down[...] = jnp.zeros_like(sum_down)
        d_hidden[...] = jnp.zeros_like(d_hidden)
        d_out[...] = jnp.zeros_like(d_out)

    x, g = rows[...], grads[...]
    produced = jnp.zeros(x.shape, F32)
    routed = jnp.zeros(x.shape, F32)
    for j in range(up.shape[1] // chunk):
        cols = slice(j * chunk, (j + 1) * chunk)
        hidden = mm(x, up[:, cols]) + hidden_bias[:, cols]
        back_active = mt(g, down[cols, :])
        active, slope = gelu_pair(hidden)
        active = active.astype(BF16)
        back_hidden = back_active * slope
        d_hidden[:, cols] += jnp.sum(back_hidden, axis=0, keepdims=True)
        back_hidden = back_hidden.astype(BF16)
        produced += mm(active, down[cols, :])
        routed += mt(back_hidden, up[:, cols])
        sum_up[:, cols] += tm(x, back_hidden)
        sum_down[:, cols] += tm(g, active)
    d_out[...] += jnp.sum(g.astype(F32), axis=0, keepdims=True)
    made[...] = (produced + out_bias[...]).astype(BF16)
    back[...] = routed.astype(BF16)

    @pl.when(step == steps - 1)
    def _():
        d_up[...] = sum_up[...].astype(BF16)
        d_down[...] = sum_down[...].T.astype(BF16)


def backward_kernel(
    images, real, shards, x, w_in, w_out, gain, shift, qkv, context, middle, cot, col, back,
    d_x, d_in, d_out, d_gain, d_shift, d_bias, d_qkv, d_context,
):
    tokens, width = x.shape
    lines = tokens // images
    experts, slots, _ = back.shape
    back_two = jnp.zeros((tokens, width), F32)
    for e in range(experts):
        back_two += mm(taken(col, expert_of(e, experts, shards), slots), back[e])
    unit, inverse = normalize(middle[...])
    d_gain[1:2, :] = jnp.sum(back_two * unit, axis=0, keepdims=True)
    d_shift[1:2, :] = jnp.sum(back_two, axis=0, keepdims=True)
    back_middle = cot[...].astype(F32) + normalize_back(back_two, unit, inverse, gain[1:2, :])
    d_x[...] = back_middle
    branch = back_middle.astype(BF16)
    d_bias[2:3, :] = jnp.sum(branch.astype(F32), axis=0, keepdims=True)
    d_out[...] = tm(context[...], branch).astype(BF16)
    d_context[...] = mt(branch, w_out[...]).astype(BF16)
    valid = lax.broadcasted_iota(jnp.int32, (lines, lines), 0) < real
    half = lax.broadcasted_iota(jnp.int32, (lines, SLAB), 1) < HEAD
    scale = HEAD**-0.5
    d_bias[0:2, :] = jnp.zeros((2, width), F32)

    def one_image(i, carry):
        rows = pl.ds(pl.multiple_of(i * lines, 16), lines)
        for s in range(width // SLAB):
            cols = [slice(a * width + s * SLAB, a * width + (s + 1) * SLAB) for a in range(3)]
            q, k, v = (qkv[rows, c] for c in cols)
            given = d_context[rows, cols[0]]
            parts = []
            for h in range(2):
                keep = half if h == 0 else ~half
                zero = jnp.zeros_like(k)
                scores = mt(jnp.where(keep, k, zero), q) * scale
                scores = jnp.where(valid, scores, -1e30)
                powers = jnp.exp(scores - jnp.max(scores, axis=0, keepdims=True))
                soft = powers / jnp.sum(powers, axis=0, keepdims=True)
                back_soft = mt(jnp.where(keep, v, zero), given)
                shared = jnp.sum(back_soft * soft, axis=0, keepdims=True)
                back_scores = (soft * (back_soft - shared)).astype(BF16)
                parts.append((tm(back_scores, k), mm(back_scores, q), mm(soft.astype(BF16), given)))
            grads = [jnp.where(half, a, b) for a, b in zip(*parts)]
            grads = [grads[0] * scale, grads[1] * scale, grads[2]]
            d_bias[0:1, cols[0]] += jnp.sum(grads[0], axis=0, keepdims=True)
            d_bias[1:2, cols[0]] += jnp.sum(grads[2], axis=0, keepdims=True)
            for c, grad in zip(cols, grads):
                d_qkv[rows, c] = grad.astype(BF16)
        return carry

    lax.fori_loop(0, images, one_image, 0)
    unit, inverse = normalize(x[...].astype(F32))
    normed = (unit * gain[0:1, :] + shift[0:1, :]).astype(BF16)
    d_in[...] = tm(normed, d_qkv[...]).astype(BF16)
    back_one = mt(d_qkv[...], w_in[...])
    d_gain[0:1, :] = jnp.sum(back_one * unit, axis=0, keepdims=True)
    d_shift[0:1, :] = jnp.sum(back_one, axis=0, keepdims=True)
    d_x[...] += normalize_back(back_one, unit, inverse, gain[0:1, :])


def output_kernel(lines, real, shards, middle, cot, gates, routes, col, returned, out, d_gates, squares):
    tokens, width = middle.shape
    experts, slots, _ = returned.shape
    rows = [jnp.zeros((tokens, width), F32) for _ in range(TOP)]
    for r in range(TOP):
        for j in range(experts):
            e = expert_of(j, experts, shards)
            mine = jnp.where(routes[:, r : r + 1] == e, col[:, e : e + 1], -1.0)
            rows[r] += mm(taken(mine, 0, slots), returned[j])
    upstream = cot[...].astype(F32)
    total = middle[...]
    for r in range(TOP):
        total += rows[r] * gates[:, r : r + 1]
        d_gates[:, r : r + 1] = jnp.sum(rows[r] * upstream, axis=1, keepdims=True)
    out[...] = total.astype(BF16)
    index = lax.broadcasted_iota(jnp.int32, (tokens, 1), 0)
    counts = jnp.where(lax.rem(index, lines) < real, 1.0, 0.0)
    squares[...] = jnp.sum(total * total * counts, axis=0, keepdims=True)


def local(
    images, attention_in, attention_out, layer_gain, layer_shift, attention_bias, expert_up, hidden_bias,
    expert_down, expert_bias, routes, gates, cotangent,
):
    count, real, width = images.shape
    lines = up_to(real, 16)
    tokens = count * lines
    experts = lax.axis_size("expert")
    shards = lax.axis_size("shard")
    slots = up_to(max(2, 4 * count * real // experts), 16)
    hidden_units = expert_up.shape[2]

    def padded(values, fill=0):
        wide = jnp.pad(values, ((0, 0), (0, lines - real), (0, 0)), constant_values=fill)
        return wide.reshape(tokens, values.shape[2])

    mats = jnp.concatenate([attention_in, attention_out], axis=1)
    vectors = jnp.concatenate([layer_gain, layer_shift, attention_bias], axis=0).astype(F32)
    vectors = lax.dynamic_update_slice(
        jnp.zeros((8, width), F32), vectors, (0, lax.axis_index("shard") * vectors.shape[1])
    )
    biases = jnp.concatenate([hidden_bias, expert_bias], axis=1).astype(F32)

    x, cot = padded(images), padded(cotangent)
    route_col, gate_col = padded(routes, -1), padded(gates)
    block = (experts, slots, width)
    parts = 4
    dma = pltpu.SemaphoreType.DMA
    rows, grads, up_held, down_held, bias_held, middle, qkv, context, squares, full, vecs, col = call(
        functools.partial(ready_kernel, count, real, parts),
        [
            (block, BF16), (block, BF16), ((width, hidden_units), BF16), ((hidden_units, width), BF16),
            ((1, hidden_units + width), F32), ((tokens, width), F32), ((tokens, 3 * width), BF16),
            ((tokens, width), BF16), ((2, width), F32), ((width, 4 * width), BF16), ((8, width), F32),
            ((tokens, up_to(experts, 128)), F32),
        ],
        [
            x, cot, gate_col, route_col, route_col.T, mats, vectors, expert_up[0], expert_down[0], biases,
        ],
        [
            pltpu.VMEM(block, BF16), pltpu.VMEM(block, BF16), pltpu.VMEM((up_to(experts, 8), tokens), F32),
            pltpu.VMEM((shards, 8, width), F32),
            dma((experts,)), dma((experts,)), dma((experts,)), dma((experts,)),
            dma((shards,)), dma((shards,)), dma((shards,)), dma((shards,)),
            dma((3, 3 * parts)), dma((3 * parts,)),
        ],
        outside=(7, 8, 9, 12, 13, 14),
        collective=0,
    )
    full_in, full_out = full[:, : 3 * width], full[:, 3 * width :]
    gain, shift, bias = vecs[0:2], vecs[2:4], vecs[4:7]

    every = experts * slots
    steps = 8
    size = every // steps
    tile = lambda: pl.BlockSpec((size, width), lambda i: (i, 0))
    fixed = lambda *shape: pl.BlockSpec(shape, lambda i: (0, 0))
    made, back, d_up, d_hidden, d_down, d_eb = pl.pallas_call(
        functools.partial(expert_kernel, 512),
        grid=(steps,),
        out_shape=[
            jax.ShapeDtypeStruct((every, width), BF16),
            jax.ShapeDtypeStruct((every, width), BF16),
            jax.ShapeDtypeStruct((width, hidden_units), BF16),
            jax.ShapeDtypeStruct((1, hidden_units), F32),
            jax.ShapeDtypeStruct((hidden_units, width), BF16),
            jax.ShapeDtypeStruct((1, width), F32),
        ],
        in_specs=[
            tile(), tile(), fixed(width, hidden_units), fixed(1, hidden_units), fixed(hidden_units, width),
            fixed(1, width),
        ],
        out_specs=[
            tile(), tile(), fixed(width, hidden_units), fixed(1, hidden_units), fixed(hidden_units, width),
            fixed(1, width),
        ],
        scratch_shapes=[pltpu.VMEM((width, hidden_units), F32), pltpu.VMEM((width, hidden_units), F32)],
        compiler_params=pltpu.CompilerParams(vmem_limit_bytes=VMEM_LIMIT),
    )(
        rows.reshape(every, width), grads.reshape(every, width), up_held, bias_held[:, :hidden_units],
        down_held, bias_held[:, hidden_units:],
    )
    small = jnp.concatenate([d_hidden, d_eb], axis=1)
    parts = 8
    matrix_shapes = [(d_up.shape, BF16), (d_down.shape, BF16), (small.shape, F32)]
    routed, returned, up_total, down_total, small = call(
        functools.partial(give_back_kernel, parts),
        [(block, BF16), (block, BF16), *matrix_shapes],
        [back.reshape(block), made.reshape(block), d_up, d_down, small],
        [
            *[pltpu.VMEM(s, d) for s, d in 2 * matrix_shapes],
            dma((experts,)), dma((experts,)), dma((experts,)), dma((experts,)),
            dma((3 * parts,)), dma((3 * parts,)), dma((3 * parts,)),
            dma((shards // 2, 3 * parts)), dma((3 * parts,)), dma((3 * parts,)), dma((3 * parts,)),
        ],
        collective=1,
    )
    up_total, down_total = up_total.astype(F32), down_total.astype(F32)

    d_x, d_in, d_out, d_gain, d_shift, d_bias = call(
        functools.partial(backward_kernel, count, real, shards),
        [
            ((tokens, width), F32), ((width, 3 * width), BF16), ((width, width), BF16), ((2, width), F32),
            ((2, width), F32), ((3, width), F32),
        ],
        [x, full_in, full_out, gain, shift, qkv, context, middle, cot, col, routed],
        [pltpu.VMEM((tokens, 3 * width), BF16), pltpu.VMEM((tokens, width), BF16)],
    )
    block_output, d_gates, last = call(
        functools.partial(output_kernel, lines, real, shards),
        [((tokens, width), BF16), ((tokens, TOP), F32), ((1, width), F32)],
        [middle, cot, gate_col, route_col, col, returned],
    )
    sums = jnp.sum(jnp.concatenate([squares, last], axis=0), axis=1)
    sums = lax.psum(sums, ("expert", "shard"))
    magnitude = jnp.sqrt(sums / float(count * real * width * experts * shards))

    seven = jnp.concatenate([d_gain, d_shift, d_bias], axis=0).astype(BF16)
    seven = jnp.pad(seven, ((0, 1), (0, 0))).T
    owned = jnp.concatenate([d_in, d_out, jnp.pad(seven, ((0, 0), (0, 120)))], axis=1)
    owned = lax.psum_scatter(owned, "shard", scatter_dimension=0, tiled=True)
    owned = lax.psum(owned, "expert").astype(F32)
    vectors = owned[:, 4 * width : 4 * width + 8].T

    def cut(values):
        return values.reshape(count, lines, values.shape[1])[:, :real]

    return (
        cut(block_output),
        cut(d_x),
        owned[:, : 3 * width],
        owned[:, 3 * width : 4 * width],
        vectors[0:2],
        vectors[2:4],
        vectors[4:7],
        up_total[None],
        small[:, :hidden_units],
        down_total[None],
        small[:, hidden_units:],
        cut(d_gates),
        magnitude,
    )


def solution(mesh):
    every = P(("expert", "shard"), None, None)
    return jax.shard_map(
        local,
        mesh=mesh,
        in_specs=(
            every, P("shard", None), P("shard", None), P(None, "shard"), P(None, "shard"), P(None, "shard"),
            P("expert", None, None), P("expert", None), P("expert", None, None), P("expert", None),
            every, every, every,
        ),
        out_specs=(
            every, every, P("shard", None), P("shard", None), P(None, "shard"), P(None, "shard"),
            P(None, "shard"), P("expert", None, None), P("expert", None), P("expert", None, None),
            P("expert", None), every, P(),
        ),
        check_vma=False,
    )
```

```python
import functools

import jax
import jax.numpy as jnp
from jax import lax
from jax.experimental import pallas as pl
from jax.experimental.pallas import tpu as pltpu
from jax.sharding import PartitionSpec as P

HEAD = 64
SLAB = 2 * HEAD
TOP = 2
EPSILON = 1e-06
F32, BF16 = jnp.float32, jnp.bfloat16
VMEM_LIMIT = 60 * 1024 * 1024


def dot_of(contract):
    def run(left, right):
        return lax.dot_general(
            left, right, (contract, ((), ())), preferred_element_type=F32
        )

    return run


mm = dot_of(((1,), (0,)))
mt = dot_of(((1,), (1,)))
tm = dot_of(((0,), (0,)))


def up_to(value, step):
    return -(-value // step) * step


def normalize(values):
    centre = values - jnp.mean(values, axis=-1, keepdims=True)
    inverse = lax.rsqrt(jnp.mean(centre * centre, axis=-1, keepdims=True) + EPSILON)
    return centre * inverse, inverse


def normalize_back(incoming, unit, inverse, weight):
    scaled = incoming * weight
    first_mean = jnp.mean(scaled, axis=-1, keepdims=True)
    second_mean = jnp.mean(scaled * unit, axis=-1, keepdims=True)
    return inverse * (scaled - first_mean - unit * second_mean)


def gelu_pair(value):
    size = jnp.abs(value)
    t = 1.0 / (1.0 + (0.3275911 * 0.7071067811865476) * size)
    bell = jnp.exp(-0.5 * value * value)
    poly = 0.5 * 1.061405429
    for c in (-1.453152027, 1.421413741, -0.284496736, 0.254829592):
        poly = poly * t + 0.5 * c
    tail = poly * t * bell
    normal = jnp.where(value >= 0, 1.0 - tail, tail)
    return value * normal, normal + value * (bell * 0.3989422804014327)


def call(body, outs, args, scratch=(), outside=(), collective=None):
    where = [
        pl.BlockSpec(memory_space=pl.ANY if i in outside else pltpu.VMEM) for i in range(len(args) + len(outs))
    ]
    return pl.pallas_call(
        body,
        out_shape=[jax.ShapeDtypeStruct(s, d) for s, d in outs],
        in_specs=where[: len(args)],
        out_specs=where[len(args) :],
        scratch_shapes=list(scratch),
        compiler_params=pltpu.CompilerParams(
            vmem_limit_bytes=VMEM_LIMIT, collective_id=collective, has_side_effects=collective is not None
        ),
    )(*args)


def axes():
    return (
        lax.axis_index("expert"), lax.axis_index("shard"), lax.axis_size("expert"), lax.axis_size("shard")
    )


def home(shard, shards):
    core = shard % 2
    return (shard // 2) * (1 - core) + (shards - 1 - shard // 2) * core


def expert_of(member, experts, shards):
    return home(member % shards, shards) * (experts // shards) + member // shards


class Place:
    def __init__(self):
        self.expert, self.shard, self.experts, self.shards = axes()
        self.width = self.experts // self.shards
        self.row = lax.div(self.expert, self.width)
        self.member = lax.rem(self.expert, self.width) * self.shards + self.shard
        self.core = lax.rem(self.shard, 2)
        self.chip = lax.div(self.shard, 2)
        self.root = self.chip * (1 - self.core) + (self.shards - 1 - self.chip) * self.core

    def peer(self, step):
        other = lax.rem(self.member + step, self.experts)
        return other, (self.row * self.width + lax.div(other, self.shards), lax.rem(other, self.shards))

    def along(self, step):
        return (self.expert + step * self.width, self.shard)

    def greet(self):
        barrier = pltpu.get_barrier_semaphore()
        for step in range(1, self.experts):
            tell(barrier, self.peer(step)[1])
        pl.when(self.row > 0)(lambda: tell(barrier, self.along(-1)))
        pl.when(self.row < self.shards - 1)(lambda: tell(barrier, self.along(1)))
        ends = jnp.where(self.row > 0, 1, 0) + jnp.where(self.row < self.shards - 1, 1, 0)
        pl.semaphore_wait(barrier, self.experts - 1 + ends)


    def greet_all(self):
        barrier = pltpu.get_barrier_semaphore()
        for step in range(1, self.experts):
            tell(barrier, self.peer(step)[1])
        for rows in range(1, self.shards):
            for at in range(self.width):
                line = lax.rem(self.row + rows, self.shards) * self.width + at
                tell(barrier, (line, self.shard))
        pl.semaphore_wait(barrier, self.experts - 1 + (self.shards - 1) * self.width)


def tell(semaphore, device):
    pl.semaphore_signal(semaphore, inc=1, device_id=device, device_id_type=pl.DeviceIdType.MESH)


def remote(src, dst, sent, came, device):
    return pltpu.make_async_remote_copy(
        src_ref=src, dst_ref=dst, send_sem=sent, recv_sem=came, device_id=device,
        device_id_type=pl.DeviceIdType.MESH,
    )


def exchange_copies(place, send, recv, sent, came):
    copies = []
    for step in range(1, place.experts):
        other, device = place.peer(step)
        copies.append(remote(send.at[other], recv.at[place.member], sent.at[step], came.at[step], device))
    own = pltpu.make_async_copy(send.at[place.member], recv.at[place.member], sent.at[0])
    return [own, *copies]


def placed(col_in, row_in, col_shape, row_shape):
    tokens = col_in.shape[0]
    down = lax.broadcasted_iota(jnp.int32, (tokens, tokens), 0)
    across = lax.broadcasted_iota(jnp.int32, (tokens, tokens), 1)
    lanes = lax.broadcasted_iota(jnp.int32, col_shape, 1)
    named = (col_in[:, 0:1] == lanes) | (col_in[:, 1:2] == lanes)
    before = (across < down).astype(F32).astype(BF16)
    ranks = mm(before, named.astype(F32).astype(BF16))
    col = jnp.where(named, ranks, -1.0)
    lines = lax.broadcasted_iota(jnp.int32, row_shape, 0)
    named = (row_in[0:1, :] == lines) | (row_in[1:2, :] == lines)
    before = (down < across).astype(F32).astype(BF16)
    ranks = mm(named.astype(F32).astype(BF16), before)
    return col, jnp.where(named, ranks, -1.0)


def chosen(row_ref, expert, slots):
    tokens = row_ref.shape[1]
    index = lax.broadcasted_iota(jnp.int32, (slots, tokens), 0).astype(F32)
    return jnp.where(index == row_ref[expert : expert + 1, :], 1.0, 0.0).astype(BF16)


def taken(col, expert, slots):
    index = lax.broadcasted_iota(jnp.int32, (col.shape[0], slots), 1).astype(F32)
    return jnp.where(index == col[:, expert : expert + 1], 1.0, 0.0).astype(BF16)


def ready_kernel(
    images, real, parts,
    x, cot, gates, routes, routes_row, mats, vecs, up, down, biases,
    rows_in, grads_in, up_out, down_out, biases_out, middle_out, qkv, context, squares, full, rows_of, col,
    send_grads, send_rows, row, vec_all, sent_g, came_g, sent_r, came_r, sent_p, came_p, sent_v, came_v,
    sent_w, came_w,
):
    place = Place()
    tokens, width = x.shape
    lines = tokens // images
    experts, slots, _ = send_rows.shape
    shards = place.shards
    place.greet()

    share = mats.shape[0]
    mine = pl.ds(place.shard * share, share)
    partner = (place.expert, place.shard + 1 - 2 * place.core)
    own = [
        pltpu.make_async_copy(mats, full.at[mine], sent_p.at[0]),
        pltpu.make_async_copy(vecs, vec_all.at[place.shard], sent_v.at[0]),
    ]
    for c in own:
        c.start()
    chips = []
    for step in range(1, shards // 2):
        there = (place.expert, lax.rem(place.chip + step, shards // 2) * 2 + place.core)
        chips.append(remote(mats, full.at[mine], sent_p.at[step], came_p.at[step], there))
        chips.append(remote(vecs, vec_all.at[place.shard], sent_v.at[step], came_v.at[step], there))
    for c in chips:
        c.start()

    def pieces(k, here, there, sent, came, device):
        wide = up.shape[1] // parts
        cols, lots = pl.ds(k * wide, wide), pl.ds(k * wide, wide)
        out = [
            remote(here[0].at[:, cols], there[0].at[:, cols], sent.at[3 * k], came.at[3 * k], device),
            remote(here[1].at[lots, :], there[1].at[lots, :], sent.at[3 * k + 1], came.at[3 * k + 1], device),
        ]
        if k == 0:
            out.append(remote(here[2], there[2], sent.at[3 * k + 2], came.at[3 * k + 2], device))
        return out

    held, landed = (up, down, biases), (up_out, down_out, biases_out)
    rightmost = place.shards - 1
    local = [pltpu.make_async_copy(h, t, sent_w.at[2, i]) for i, (h, t) in enumerate(zip(held, landed))]

    def matrices(k, source, way):
        return pieces(k, source, landed, sent_w.at[(way + 1) // 2], came_w, place.along(way))

    def start_all(copies):
        for c in copies:
            c.start()

    @pl.when(place.row == place.root)
    def _():
        start_all(local)
        for way, more in ((-1, place.row > 0), (1, place.row < rightmost)):

            @pl.when(more)
            def _(way=way):
                for k in range(parts):
                    start_all(matrices(k, held, way))

    def pass_on(k):
        @pl.when(place.row != place.root)
        def _():
            for c in matrices(k, landed, 1):
                c.wait_recv()

        for way, more in (
            (-1, (place.row > 0) & (place.row < place.root)),
            (1, (place.row < rightmost) & (place.row > place.root)),
        ):

            @pl.when(more)
            def _(way=way):
                start_all(matrices(k, landed, way))

    col_all, row_all = placed(routes, routes_row, col.shape, row.shape)
    col[...] = col_all
    row[...] = row_all
    upstream = cot[...].astype(F32)
    for j in range(experts):
        e = expert_of(j, experts, shards)
        gate = jnp.where(routes[:, 0:1] == e, gates[:, 0:1], 0.0) + jnp.where(
            routes[:, 1:2] == e, gates[:, 1:2], 0.0
        )
        send_grads[j] = mm(chosen(row, e, slots), (upstream * gate).astype(BF16)).astype(BF16)
    swap_g = exchange_copies(place, send_grads, grads_in, sent_g, came_g)
    start_all(swap_g)

    over = []
    for step in range(shards // 2):
        source = lax.rem(place.chip + step, shards // 2) * 2 + place.core
        block = pl.ds(source * share, share)
        if step:
            back = shards // 2 - step
            chips[2 * back - 2].wait_recv()
            chips[2 * back - 1].wait_recv()
        else:
            own[0].wait()
            own[1].wait()
        at = shards // 2 + step
        over.append(remote(full.at[block], full.at[block], sent_p.at[at], came_p.at[at], partner))
        over.append(remote(vec_all.at[source], vec_all.at[source], sent_v.at[at], came_v.at[at], partner))
        over[-2].start()
        over[-1].start()
    for c in over:
        c.wait_recv()
    vectors = vec_all[0]
    for s in range(1, shards):
        vectors = vectors + vec_all[s]
    rows_of[...] = vectors
    gain, shift, bias = vectors[0:2], vectors[2:4], vectors[4:7]
    w_in, w_out = full.at[:, : 3 * width], full.at[:, 3 * width :]
    pass_on(0)

    stream = x[...].astype(F32)
    unit, _ = normalize(stream)
    normed = (unit * gain[0:1, :] + shift[0:1, :]).astype(BF16)
    projected = mm(normed, w_in[...])
    qkv[:, :width] = (projected[:, :width] + bias[0:1, :]).astype(BF16)
    qkv[:, width : 2 * width] = projected[:, width : 2 * width].astype(BF16)
    qkv[:, 2 * width :] = (projected[:, 2 * width :] + bias[1:2, :]).astype(BF16)
    valid = lax.broadcasted_iota(jnp.int32, (lines, lines), 0) < real
    half = lax.broadcasted_iota(jnp.int32, (lines, SLAB), 1) < HEAD

    def one_image(i, carry):
        rows = pl.ds(pl.multiple_of(i * lines, 16), lines)
        for s in range(width // SLAB):
            q = qkv[rows, s * SLAB : (s + 1) * SLAB]
            k = qkv[rows, width + s * SLAB : width + (s + 1) * SLAB]
            v = qkv[rows, 2 * width + s * SLAB : 2 * width + (s + 1) * SLAB]
            heads = []
            for h in range(2):
                keep = half if h == 0 else ~half
                scores = mt(jnp.where(keep, k, jnp.zeros_like(k)), q) * (HEAD**-0.5)
                scores = jnp.where(valid, scores, -1e30)
                powers = jnp.exp(scores - jnp.max(scores, axis=0, keepdims=True))
                soft = powers / jnp.sum(powers, axis=0, keepdims=True)
                heads.append(tm(soft.astype(BF16), v))
            context[rows, s * SLAB : (s + 1) * SLAB] = jnp.where(half, heads[0], heads[1]).astype(BF16)
        return carry

    lax.fori_loop(0, images, one_image, 0)
    middle = stream + mm(context[...], w_out[...]) + bias[2:3, :]
    middle_out[...] = middle
    unit, _ = normalize(middle)
    normed = (unit * gain[1:2, :] + shift[1:2, :]).astype(BF16)
    for j in range(experts):
        send_rows[j] = mm(chosen(row, expert_of(j, experts, shards), slots), normed).astype(BF16)
    swap_r = exchange_copies(place, send_rows, rows_in, sent_r, came_r)
    start_all(swap_r)
    index = lax.broadcasted_iota(jnp.int32, (tokens, 1), 0)
    counts = jnp.where(lax.rem(index, lines) < real, 1.0, 0.0)
    squares[0:1, :] = jnp.sum(stream * stream, axis=0, keepdims=True)
    squares[1:2, :] = jnp.sum(middle * middle * counts, axis=0, keepdims=True)

    for k in range(1, parts):
        pass_on(k)
    for c in swap_g + swap_r:
        c.wait()
    for c in chips + over:
        c.wait_send()

    @pl.when(place.row == place.root)
    def _():
        for c in local:
            c.wait()

    for way, more in (
        (-1, (place.row > 0) & (place.row <= place.root)),
        (1, (place.row < rightmost) & (place.row >= place.root)),
    ):

        @pl.when(more)
        def _(way=way):
            for k in range(parts):
                for c in matrices(k, landed, way):
                    c.wait_send()


def finish_kernel(
    images, real, parts,
    back, made, up, down, x, cot, full, vecs, qkv, context, middle, col, gates, routes, squares,
    d_x, out, d_gates, up_out, down_out, shares_out, vec_out,
    back_in, made_in, up_l, down_l, up_r, down_r, d_qkv, d_context, grads, vec, from_core, from_chip, cut, from_all,
    vec_group, vec_rows,
    sent_b, came_b, sent_m, came_m, sent_c, came_l, came_r, sent_d, came_d, sent_o, came_o,
    sent_1, came_1, sent_2, came_2, sent_3, came_3, sent_4, came_4, sent_5, came_5, sent_6, came_6,
):
    place = Place()
    tokens, width = x.shape
    lines = tokens // images
    experts, slots, _ = back_in.shape
    shards = place.shards
    chips = shards // 2
    place.greet_all()

    def go(copies):
        for c in copies:
            c.start()

    swap_b = exchange_copies(place, back, back_in, sent_b, came_b)
    go(swap_b)

    rightmost = shards - 1
    row, root = place.row, place.root
    mine, total = (up, down), (up_out, down_out)
    left, right = (up_l, down_l), (up_r, down_r)
    heights = (up.shape[0] // parts, down.shape[0] // parts)

    def piece(refs, i, k):
        start = k * heights[i]
        if not isinstance(k, int):
            start = pl.multiple_of(start, 16)
        return refs[i].at[pl.ds(start, heights[i])]

    def hop(k, source, target, came, way):
        return [
            remote(piece(source, i, k), piece(target, i, k), sent_c.at[k, i], came.at[k, i], place.along(way))
            for i in range(2)
        ]

    def add(k, target, terms):
        for i in range(2):
            value = piece(terms[0], i, k)[...].astype(F32)
            for t in terms[1:]:
                value += piece(t, i, k)[...].astype(F32)
            piece(target, i, k)[...] = value.astype(BF16)

    def arrived(k, buffer, came):
        for c in hop(k, buffer, buffer, came, 1):
            c.wait_recv()

    def left_free(k):
        for c in hop(k, left, left, came_l, 1):
            c.wait_send()

    def chain(k):
        @pl.when((row > 0) & (row < root))
        def _():
            arrived(k, left, came_l)
            add(k, left, [mine, left])

        @pl.when((row < rightmost) & (row > root))
        def _():
            arrived(k, right, came_r)
            add(k, right, [mine, right])

        if not isinstance(k, int) or k >= 2:
            pl.when(row != root)(lambda: left_free(k - 2))
        pl.when((row == 0) & (row < root))(lambda: go(hop(k, mine, left, came_l, 1)))
        pl.when((row == rightmost) & (row > root))(lambda: go(hop(k, mine, right, came_r, -1)))
        pl.when((row > 0) & (row < root))(lambda: go(hop(k, left, left, came_l, 1)))
        pl.when((row < rightmost) & (row > root))(lambda: go(hop(k, right, right, came_r, -1)))

        @pl.when(row == root)
        def _():
            @pl.when(row > 0)
            def _():
                arrived(k, left, came_l)
                add(k, total, [mine, left])

            @pl.when(row == 0)
            def _():
                arrived(k, right, came_r)
                add(k, total, [mine, right])

            @pl.when((row > 0) & (row < rightmost))
            def _():
                arrived(k, right, came_r)
                add(k, total, [total, right])

            for step in range(1, chips):
                go(spread(k, step))
            go(cross(k))

    root_core = jnp.where(row < chips, 0, 1)
    root_chip = jnp.where(row < chips, row, rightmost - row)
    partner = (place.expert, place.shard + 1 - 2 * place.core)

    def chip_at(step):
        return lax.rem(place.chip + step, chips)

    def spread(k, step):
        there = (place.expert, chip_at(step) * 2 + place.core)
        return [
            remote(piece(total, i, k), piece(total, i, k), sent_d.at[step - 1, k, i], came_d.at[k, i], there)
            for i in range(2)
        ]

    def cross(k):
        return [
            remote(piece(total, i, k), piece(total, i, k), sent_o.at[k, i], came_o.at[k, i], partner)
            for i in range(2)
        ]

    def hand_out(k):
        @pl.when((place.core == root_core) & (place.chip != root_chip))
        def _():
            for c in spread(k, 1):
                c.wait_recv()
            go(cross(k))

        @pl.when(place.core != root_core)
        def _():
            for c in cross(k):
                c.wait_recv()

    for k in range(4):
        chain(k)
    for c in swap_b:
        c.wait()
    swap_m = exchange_copies(place, made, made_in, sent_m, came_m)
    go(swap_m)

    gain, shift = vecs[0:2], vecs[2:4]
    w_in, w_out = full.at[:, : 3 * width], full.at[:, 3 * width :]
    back_two = jnp.zeros((tokens, width), F32)
    for j in range(experts):
        back_two += mm(taken(col, expert_of(j, experts, shards), slots), back_in[j])
    unit, inverse = normalize(middle[...])
    vec[1:2, :] = jnp.sum(back_two * unit, axis=0, keepdims=True)
    vec[3:4, :] = jnp.sum(back_two, axis=0, keepdims=True)
    back_middle = cot[...].astype(F32) + normalize_back(back_two, unit, inverse, gain[1:2, :])
    d_x[...] = back_middle
    branch = back_middle.astype(BF16)
    vec[6:7, :] = jnp.sum(branch.astype(F32), axis=0, keepdims=True)
    grads[:, 3 * width :] = tm(context[...], branch).astype(BF16)
    d_context[...] = mt(branch, w_out[...]).astype(BF16)
    valid = lax.broadcasted_iota(jnp.int32, (lines, lines), 0) < real
    half = lax.broadcasted_iota(jnp.int32, (lines, SLAB), 1) < HEAD
    scale = HEAD**-0.5
    vec[4:6, :] = jnp.zeros((2, width), F32)
    chain(4)

    def one_image(i, carry):
        rows = pl.ds(pl.multiple_of(i * lines, 16), lines)
        for s in range(width // SLAB):
            cols = [slice(a * width + s * SLAB, a * width + (s + 1) * SLAB) for a in range(3)]
            q, k, v = (qkv[rows, c] for c in cols)
            given = d_context[rows, cols[0]]
            heads = []
            for h in range(2):
                keep = half if h == 0 else ~half
                zero = jnp.zeros_like(k)
                scores = mt(jnp.where(keep, k, zero), q) * scale
                scores = jnp.where(valid, scores, -1e30)
                powers = jnp.exp(scores - jnp.max(scores, axis=0, keepdims=True))
                soft = powers / jnp.sum(powers, axis=0, keepdims=True)
                back_soft = mt(jnp.where(keep, v, zero), given)
                shared = jnp.sum(back_soft * soft, axis=0, keepdims=True)
                back_scores = (soft * (back_soft - shared)).astype(BF16)
                heads.append((tm(back_scores, k), mm(back_scores, q), mm(soft.astype(BF16), given)))
            both = [jnp.where(half, a, b) for a, b in zip(*heads)]
            both = [both[0] * scale, both[1] * scale, both[2]]
            vec[4:5, cols[0]] += jnp.sum(both[0], axis=0, keepdims=True)
            vec[5:6, cols[0]] += jnp.sum(both[2], axis=0, keepdims=True)
            for c, grad in zip(cols, both):
                d_qkv[rows, c] = grad.astype(BF16)
        pl.when(i < parts - 5)(lambda: chain(i + 5))
        return carry

    lax.fori_loop(0, images, one_image, 0)
    for k in range(images + 5, parts):
        chain(k)
    unit, inverse = normalize(x[...].astype(F32))
    normed = (unit * gain[0:1, :] + shift[0:1, :]).astype(BF16)
    grads[:, : 3 * width] = tm(normed, d_qkv[...]).astype(BF16)

    share = width // shards
    halves = [
        remote(
            grads.at[pl.ds(pl.multiple_of((2 * c + 1 - place.core) * share, 16), share)], from_core.at[c],
            sent_1.at[c], came_1.at[c], partner,
        )
        for c in range(chips)
    ]
    go(halves)
    back_one = mt(d_qkv[...], w_in[...])
    vec[0:1, :] = jnp.sum(back_one * unit, axis=0, keepdims=True)
    vec[2:3, :] = jnp.sum(back_one, axis=0, keepdims=True)
    d_x[...] += normalize_back(back_one, unit, inverse, gain[0:1, :])
    for c in range(chips):
        halves[c].wait_recv()
        block = pl.ds(pl.multiple_of((2 * c + place.core) * share, 16), share)
        from_core[c] = (from_core[c].astype(F32) + grads[block, :].astype(F32)).astype(BF16)
    quarters = [
        remote(
            from_core.at[chip_at(step)], from_chip.at[place.chip], sent_2.at[step], came_2.at[step],
            (place.expert, chip_at(step) * 2 + place.core),
        )
        for step in range(1, chips)
    ]
    go(quarters)
    for k in range(4):
        hand_out(k)

    for c in swap_m:
        c.wait()
    upstream = cot[...].astype(F32)
    stream = middle[...]

    def gathered(r):
        found = jnp.zeros((tokens, width), F32)
        for j in range(experts):
            e = expert_of(j, experts, shards)
            slot = jnp.where(routes[:, r : r + 1] == e, col[:, e : e + 1], -1.0)
            found += mm(taken(slot, 0, slots), made_in[j])
        d_gates[:, r : r + 1] = jnp.sum(found * upstream, axis=1, keepdims=True)
        return found * gates[:, r : r + 1]

    stream += gathered(0)
    for c in quarters:
        c.wait_recv()
    whole = from_core[place.chip].astype(F32)
    for step in range(1, chips):
        whole += from_chip[chip_at(step)].astype(F32)
    whole = whole.astype(BF16)
    down_n = share // 16
    across_n = experts // down_n
    wide = cut.shape[2]
    for r in range(down_n):
        for c in range(across_n):
            cut[r * across_n + c] = whole[r * 16 : (r + 1) * 16, c * wide : (c + 1) * wide]

    def other(step):
        return lax.rem(place.expert + step, experts)

    pieces = [
        remote(
            cut.at[other(step)], from_all.at[place.expert], sent_3.at[step], came_3.at[step],
            (other(step), place.shard),
        )
        for step in range(1, experts)
    ]
    go(pieces)
    stream += gathered(1)
    out[...] = stream.astype(BF16)
    index = lax.broadcasted_iota(jnp.int32, (tokens, 1), 0)
    counts = jnp.where(lax.rem(index, lines) < real, 1.0, 0.0)
    vec[7:8, :] = jnp.zeros((1, width), F32)
    vec[8:10, :] = squares[...]
    vec[10:11, :] = jnp.sum(stream * stream * counts, axis=0, keepdims=True)
    vec[11:16, :] = jnp.zeros((5, width), F32)
    vec_group[place.member] = vec[...]
    lists = [
        remote(vec, vec_group.at[place.member], sent_5.at[step], came_5.at[step], place.peer(step)[1])
        for step in range(1, experts)
    ]
    go(lists)
    for c in pieces:
        c.wait_recv()
    whole = cut[place.expert].astype(F32)
    for step in range(1, experts):
        whole += from_all[other(step)].astype(F32)
    shares_out[place.expert] = whole.astype(BF16)
    spreads = [
        remote(
            shares_out.at[place.expert], shares_out.at[place.expert], sent_4.at[step], came_4.at[step],
            (other(step), place.shard),
        )
        for step in range(1, experts)
    ]
    go(spreads)
    for c in lists:
        c.wait_recv()
    whole = vec_group[0]
    for j in range(1, experts):
        whole += vec_group[j]
    vec_rows[row] = whole
    downs = [
        remote(
            vec_rows.at[row], vec_rows.at[row], sent_6.at[step], came_6.at[step],
            (lax.rem(place.expert + step * place.width, experts), place.shard),
        )
        for step in range(1, shards)
    ]
    go(downs)
    for k in range(4, parts):
        hand_out(k)
    for c in downs:
        c.wait_recv()
    whole = vec_rows[0]
    for j in range(1, shards):
        whole += vec_rows[j]
    vec_out[...] = whole
    for c in spreads:
        c.wait_recv()
    for c in halves + quarters + pieces + spreads + lists + downs:
        c.wait_send()
    for k in range(parts - 2, parts):
        pl.when(row != root)(lambda k=k: left_free(k))

    def sends(k, carry):
        @pl.when(row == root)
        def _():
            for step in range(1, chips):
                for c in spread(k, step):
                    c.wait_send()

        @pl.when(place.core == root_core)
        def _():
            for c in cross(k):
                c.wait_send()

        return carry

    lax.fori_loop(0, parts, sends, 0)


def expert_kernel(
    chunk, rows, grads, up, hidden_bias, down, out_bias, made, back, d_up, d_down, sum_up, sum_down, d_hidden, d_out
):
    step, steps = pl.program_id(0), pl.num_programs(0)

    @pl.when(step == 0)
    def _():
        sum_up[...] = jnp.zeros_like(sum_up)
        sum_down[...] = jnp.zeros_like(sum_down)
        d_hidden[...] = jnp.zeros_like(d_hidden)
        d_out[...] = jnp.zeros_like(d_out)

    x, g = rows[...], grads[...]
    produced = jnp.zeros(x.shape, F32)
    routed = jnp.zeros(x.shape, F32)
    for j in range(up.shape[1] // chunk):
        cols = slice(j * chunk, (j + 1) * chunk)
        hidden = mm(x, up[:, cols]) + hidden_bias[:, cols]
        back_active = mt(g, down[cols, :])
        active, slope = gelu_pair(hidden)
        active = active.astype(BF16)
        back_hidden = back_active * slope
        d_hidden[:, cols] += jnp.sum(back_hidden, axis=0, keepdims=True)
        back_hidden = back_hidden.astype(BF16)
        produced += mm(active, down[cols, :])
        routed += mt(back_hidden, up[:, cols])
        sum_up[:, cols] += tm(x, back_hidden)
        sum_down[:, cols] += tm(g, active)
    d_out[...] += jnp.sum(g.astype(F32), axis=0, keepdims=True)
    made[...] = (produced + out_bias[...]).astype(BF16)
    back[...] = routed.astype(BF16)

    @pl.when(step == steps - 1)
    def _():
        d_up[...] = sum_up[...].astype(BF16)
        units, width = down.shape
        d_down[:units, :] = sum_down[...].T.astype(BF16)
        d_down[units:, :] = jnp.zeros((d_down.shape[0] - units, width), BF16)
        for i in range(units // width):
            d_down[units + i : units + i + 1, :] = d_hidden[:, i * width : (i + 1) * width].astype(BF16)
        i = units + units // width
        d_down[i : i + 1, :] = d_out[...].astype(BF16)


def local(
    images, attention_in, attention_out, layer_gain, layer_shift, attention_bias, expert_up, hidden_bias,
    expert_down, expert_bias, routes, gates, cotangent,
):
    count, real, width = images.shape
    lines = up_to(real, 16)
    tokens = count * lines
    experts = lax.axis_size("expert")
    shards = lax.axis_size("shard")
    slots = up_to(max(2, 4 * count * real // experts), 16)
    hidden_units = expert_up.shape[2]

    def padded(values, fill=0):
        wide = jnp.pad(values, ((0, 0), (0, lines - real), (0, 0)), constant_values=fill)
        return wide.reshape(tokens, values.shape[2])

    mats = jnp.concatenate([attention_in, attention_out], axis=1)
    vectors = jnp.concatenate([layer_gain, layer_shift, attention_bias], axis=0).astype(F32)
    vectors = lax.dynamic_update_slice(
        jnp.zeros((8, width), F32), vectors, (0, lax.axis_index("shard") * vectors.shape[1])
    )
    biases = jnp.concatenate([hidden_bias, expert_bias], axis=1).astype(F32)

    x, cot = padded(images), padded(cotangent)
    route_col, gate_col = padded(routes, -1), padded(gates)
    block = (experts, slots, width)
    parts = 4
    dma = pltpu.SemaphoreType.DMA
    rows, grads, up_held, down_held, bias_held, middle, qkv, context, squares, full, vecs, col = call(
        functools.partial(ready_kernel, count, real, parts),
        [
            (block, BF16), (block, BF16), ((width, hidden_units), BF16), ((hidden_units, width), BF16),
            ((1, hidden_units + width), F32), ((tokens, width), F32), ((tokens, 3 * width), BF16),
            ((tokens, width), BF16), ((2, width), F32), ((width, 4 * width), BF16), ((8, width), F32),
            ((tokens, up_to(experts, 128)), F32),
        ],
        [
            x, cot, gate_col, route_col, route_col.T, mats, vectors, expert_up[0], expert_down[0], biases,
        ],
        [
            pltpu.VMEM(block, BF16), pltpu.VMEM(block, BF16), pltpu.VMEM((up_to(experts, 8), tokens), F32),
            pltpu.VMEM((shards, 8, width), F32),
            dma((experts,)), dma((experts,)), dma((experts,)), dma((experts,)),
            dma((shards,)), dma((shards,)), dma((shards,)), dma((shards,)),
            dma((3, 3 * parts)), dma((3 * parts,)),
        ],
        outside=(7, 8, 9, 12, 13, 14),
        collective=0,
    )
    full_in, full_out = full[:, : 3 * width], full[:, 3 * width :]
    gain, shift, bias = vecs[0:2], vecs[2:4], vecs[4:7]

    every = experts * slots
    steps = 8
    size = every // steps
    tile = lambda: pl.BlockSpec((size, width), lambda i: (i, 0))
    fixed = lambda *shape: pl.BlockSpec(shape, lambda i: (0, 0))
    parts = 8
    low = hidden_units + 16 * parts
    made, back, d_up, d_down = pl.pallas_call(
        functools.partial(expert_kernel, 512),
        grid=(steps,),
        out_shape=[
            jax.ShapeDtypeStruct((every, width), BF16),
            jax.ShapeDtypeStruct((every, width), BF16),
            jax.ShapeDtypeStruct((width, hidden_units), BF16),
            jax.ShapeDtypeStruct((low, width), BF16),
        ],
        in_specs=[
            tile(), tile(), fixed(width, hidden_units), fixed(1, hidden_units), fixed(hidden_units, width),
            fixed(1, width),
        ],
        out_specs=[tile(), tile(), fixed(width, hidden_units), fixed(low, width)],
        scratch_shapes=[
            pltpu.VMEM((width, hidden_units), F32), pltpu.VMEM((width, hidden_units), F32),
            pltpu.VMEM((1, hidden_units), F32), pltpu.VMEM((1, width), F32),
        ],
        compiler_params=pltpu.CompilerParams(vmem_limit_bytes=VMEM_LIMIT),
    )(
        rows.reshape(every, width), grads.reshape(every, width), up_held, bias_held[:, :hidden_units],
        down_held, bias_held[:, hidden_units:],
    )
    share = width // shards
    across = experts // (share // 16)
    wide = 4 * width // across
    vmem = lambda *shape: pltpu.VMEM(shape, BF16)
    d_x, out, d_gates, up_total, down_total, owned, vector_sums = call(
        functools.partial(finish_kernel, count, real, parts),
        [
            ((tokens, width), F32), ((tokens, width), BF16), ((tokens, TOP), F32), (d_up.shape, BF16),
            (d_down.shape, BF16), ((experts, 16, wide), BF16), ((16, width), F32),
        ],
        [
            back.reshape(block), made.reshape(block), d_up, d_down, x, cot, full, vecs, qkv, context, middle, col,
            gate_col, route_col, squares,
        ],
        [
            vmem(*block), vmem(*block), vmem(*d_up.shape), vmem(*d_down.shape), vmem(*d_up.shape),
            vmem(*d_down.shape), vmem(tokens, 3 * width), vmem(tokens, width), vmem(width, 4 * width),
            pltpu.VMEM((16, width), F32), vmem(shards // 2, share, 4 * width), vmem(shards // 2, share, 4 * width),
            vmem(experts, 16, wide), vmem(experts, 16, wide), pltpu.VMEM((experts, 16, width), F32),
            pltpu.VMEM((shards, 16, width), F32),
            dma((experts,)), dma((experts,)), dma((experts,)), dma((experts,)),
            dma((parts, 2)), dma((parts, 2)), dma((parts, 2)),
            dma((shards // 2, parts, 2)), dma((parts, 2)), dma((parts, 2)), dma((parts, 2)),
            dma((shards,)), dma((shards,)), dma((shards,)), dma((shards,)),
            dma((experts,)), dma((experts,)), dma((experts,)), dma((experts,)),
            dma((experts,)), dma((experts,)), dma((shards,)), dma((shards,)),
        ],
        outside=(0, 1),
        collective=1,
    )
    entries = float(count * real * width * experts * shards)
    magnitude = jnp.sqrt(jnp.sum(vector_sums[8:11], axis=1) / entries)
    owned = owned.reshape(share // 16, across, 16, wide).transpose(0, 2, 1, 3).reshape(share, 4 * width)
    owned = owned.astype(F32)
    vectors = lax.dynamic_slice(vector_sums, (0, lax.axis_index("shard") * share), (7, share))
    small = down_total[hidden_units:].astype(F32)

    def cut(values):
        return values.reshape(count, lines, values.shape[1])[:, :real]

    return (
        cut(out),
        cut(d_x),
        owned[:, : 3 * width],
        owned[:, 3 * width : 4 * width],
        vectors[0:2],
        vectors[2:4],
        vectors[4:7],
        up_total.astype(F32)[None],
        small[: hidden_units // width].reshape(1, hidden_units),
        down_total[:hidden_units].astype(F32)[None],
        small[hidden_units // width : hidden_units // width + 1],
        cut(d_gates),
        magnitude,
    )


def solution(mesh):
    every = P(("expert", "shard"), None, None)
    return jax.shard_map(
        local,
        mesh=mesh,
        in_specs=(
            every, P("shard", None), P("shard", None), P(None, "shard"), P(None, "shard"), P(None, "shard"),
            P("expert", None, None), P("expert", None), P("expert", None, None), P("expert", None),
            every, every, every,
        ),
        out_specs=(
            every, every, P("shard", None), P("shard", None), P(None, "shard"), P(None, "shard"),
            P(None, "shard"), P("expert", None, None), P("expert", None), P("expert", None, None),
            P("expert", None), every, P(),
        ),
        check_vma=False,
    )
```

```python
import functools

import jax
import jax.numpy as jnp
from jax import lax
from jax.experimental import pallas as pl
from jax.experimental.pallas import tpu as pltpu
from jax.sharding import PartitionSpec as P

HEAD = 64
SLAB = 2 * HEAD
TOP = 2
EPSILON = 1e-06
F32, BF16 = jnp.float32, jnp.bfloat16
VMEM_LIMIT = 60 * 1024 * 1024


def dot_of(contract):
    def run(left, right):
        return lax.dot_general(
            left, right, (contract, ((), ())), preferred_element_type=F32
        )

    return run


mm = dot_of(((1,), (0,)))
mt = dot_of(((1,), (1,)))
tm = dot_of(((0,), (0,)))


def up_to(value, step):
    return -(-value // step) * step


def normalize(values):
    centre = values - jnp.mean(values, axis=-1, keepdims=True)
    inverse = lax.rsqrt(jnp.mean(centre * centre, axis=-1, keepdims=True) + EPSILON)
    return centre * inverse, inverse


def normalize_back(incoming, unit, inverse, weight):
    scaled = incoming * weight
    first_mean = jnp.mean(scaled, axis=-1, keepdims=True)
    second_mean = jnp.mean(scaled * unit, axis=-1, keepdims=True)
    return inverse * (scaled - first_mean - unit * second_mean)


def gelu_pair(value):
    size = jnp.abs(value)
    t = 1.0 / (1.0 + (0.3275911 * 0.7071067811865476) * size)
    bell = jnp.exp(-0.5 * value * value)
    poly = 0.5 * 1.061405429
    for c in (-1.453152027, 1.421413741, -0.284496736, 0.254829592):
        poly = poly * t + 0.5 * c
    tail = poly * t * bell
    normal = jnp.where(value >= 0, 1.0 - tail, tail)
    return value * normal, normal + value * (bell * 0.3989422804014327)


def call(body, outs, args, scratch=(), outside=(), collective=None):
    where = [
        pl.BlockSpec(memory_space=pl.ANY if i in outside else pltpu.VMEM) for i in range(len(args) + len(outs))
    ]
    return pl.pallas_call(
        body,
        out_shape=[jax.ShapeDtypeStruct(s, d) for s, d in outs],
        in_specs=where[: len(args)],
        out_specs=where[len(args) :],
        scratch_shapes=list(scratch),
        compiler_params=pltpu.CompilerParams(
            vmem_limit_bytes=VMEM_LIMIT, collective_id=collective, has_side_effects=collective is not None
        ),
    )(*args)


def axes():
    return (
        lax.axis_index("expert"), lax.axis_index("shard"), lax.axis_size("expert"), lax.axis_size("shard")
    )


class Place:
    def __init__(self):
        self.expert, self.shard, self.experts, self.shards = axes()
        self.width = self.experts // self.shards
        self.row = lax.div(self.expert, self.width)
        self.member = lax.rem(self.expert, self.width) * self.shards + self.shard
        self.core = lax.rem(self.shard, 2)
        self.chip = lax.div(self.shard, 2)
        self.root = self.chip * (1 - self.core) + (self.shards - 1 - self.chip) * self.core

    def peer(self, step):
        other = lax.rem(self.member + step, self.experts)
        return other, (self.row * self.width + lax.div(other, self.shards), lax.rem(other, self.shards))

    def expert_at(self, number):
        many = self.experts // 2
        chips = self.shards // 2
        half, spot = divmod(number, many)
        core = self.core * (1 - half) + (1 - self.core) * half
        chip = spot % chips
        return (chip * (1 - core) + (self.shards - 1 - chip) * core) * self.width + spot // chips

    def expert_at_all(self, shape, axis):
        at = lax.broadcasted_iota(jnp.int32, shape, axis)
        experts = jnp.full(shape, -9, jnp.int32)
        for number in range(self.experts):
            experts = jnp.where(at == number, self.expert_at(number), experts)
        return experts

    def swap(self, half, send, recv, sent, came):
        many = self.experts // 2
        chips = self.shards // 2
        spot = lax.div(self.member, 2)
        core = self.core if half == 0 else 1 - self.core
        copies = []
        if half == 0:
            copies.append(pltpu.make_async_copy(send.at[spot], recv.at[spot], sent.at[0]))
        for step in range(1 - half, many):
            other = lax.rem(spot + step, many)
            device = (self.row * self.width + lax.div(other, chips), lax.rem(other, chips) * 2 + core)
            copies.append(remote(send.at[other], recv.at[spot], sent.at[step], came.at[step], device))
        return copies

    def along(self, step):
        return (self.expert + step * self.width, self.shard)

    def greet(self):
        barrier = pltpu.get_barrier_semaphore()
        for step in range(1, self.experts):
            tell(barrier, self.peer(step)[1])
        pl.when(self.row > 0)(lambda: tell(barrier, self.along(-1)))
        pl.when(self.row < self.shards - 1)(lambda: tell(barrier, self.along(1)))
        ends = jnp.where(self.row > 0, 1, 0) + jnp.where(self.row < self.shards - 1, 1, 0)
        pl.semaphore_wait(barrier, self.experts - 1 + ends)


    def greet_all(self):
        barrier = pltpu.get_barrier_semaphore()
        for step in range(1, self.experts):
            tell(barrier, self.peer(step)[1])
        for rows in range(1, self.shards):
            for at in range(self.width):
                line = lax.rem(self.row + rows, self.shards) * self.width + at
                tell(barrier, (line, self.shard))
        pl.semaphore_wait(barrier, self.experts - 1 + (self.shards - 1) * self.width)


def tell(semaphore, device):
    pl.semaphore_signal(semaphore, inc=1, device_id=device, device_id_type=pl.DeviceIdType.MESH)


def remote(src, dst, sent, came, device):
    return pltpu.make_async_remote_copy(
        src_ref=src, dst_ref=dst, send_sem=sent, recv_sem=came, device_id=device,
        device_id_type=pl.DeviceIdType.MESH,
    )


def placed(place, col_in, row_in, col_shape, row_shape):
    tokens = col_in.shape[0]
    down = lax.broadcasted_iota(jnp.int32, (tokens, tokens), 0)
    across = lax.broadcasted_iota(jnp.int32, (tokens, tokens), 1)
    lanes = place.expert_at_all(col_shape, 1)
    named = (col_in[:, 0:1] == lanes) | (col_in[:, 1:2] == lanes)
    before = (across < down).astype(F32).astype(BF16)
    ranks = mm(before, named.astype(F32).astype(BF16))
    col = jnp.where(named, ranks, -1.0)
    lines = place.expert_at_all(row_shape, 0)
    named = (row_in[0:1, :] == lines) | (row_in[1:2, :] == lines)
    before = (down < across).astype(F32).astype(BF16)
    ranks = mm(named.astype(F32).astype(BF16), before)
    return col, jnp.where(named, ranks, -1.0)


def chosen(row_ref, expert, slots):
    tokens = row_ref.shape[1]
    index = lax.broadcasted_iota(jnp.int32, (slots, tokens), 0).astype(F32)
    return jnp.where(index == row_ref[expert : expert + 1, :], 1.0, 0.0).astype(BF16)


def taken(col, expert, slots):
    index = lax.broadcasted_iota(jnp.int32, (col.shape[0], slots), 1).astype(F32)
    return jnp.where(index == col[:, expert : expert + 1], 1.0, 0.0).astype(BF16)


def expert_step(x, g, up, down, bias):
    hidden = mm(x, up) + bias
    back_active = mt(g, down)
    active, slope = gelu_pair(hidden)
    active = active.astype(BF16)
    back_hidden = back_active * slope
    sums = jnp.sum(back_hidden, axis=0, keepdims=True)
    back_hidden = back_hidden.astype(BF16)
    return mm(active, down), mt(back_hidden, up), tm(x, back_hidden), tm(active, g), sums


def forward_kernel(
    images, real, parts, chunks,
    x, cot, gates, routes, routes_row, mats, vecs, up, down, biases,
    back_a, made_a, back_b, made_b, d_up, d_down, middle_out, qkv, context, squares, full, rows_of, col,
    send_g, send_r, rows_in, grads_in, up_in, down_in, biases_in, made_sum, back_sum, sum_up, sum_down, sum_small,
    row, vec_all,
    sent_g, came_g, sent_r, came_r, sent_p, came_p, sent_v, came_v, sent_w, came_w, sent_b, came_b, sent_m, came_m,
):
    place = Place()
    tokens, width = x.shape
    lines = tokens // images
    _, many, slots, _ = send_r.shape
    shards = place.shards
    chips_n = shards // 2
    place.greet()

    def go(copies):
        for c in copies:
            c.start()

    share = mats.shape[0]
    mine = pl.ds(pl.multiple_of(place.shard * share, 16), share)
    partner = (place.expert, place.shard + 1 - 2 * place.core)
    own = [
        pltpu.make_async_copy(mats, full.at[mine], sent_p.at[0]),
        pltpu.make_async_copy(vecs, vec_all.at[place.shard], sent_v.at[0]),
    ]
    go(own)
    chips = []
    for step in range(1, chips_n):
        there = (place.expert, lax.rem(place.chip + step, chips_n) * 2 + place.core)
        chips.append(remote(mats, full.at[mine], sent_p.at[step], came_p.at[step], there))
        chips.append(remote(vecs, vec_all.at[place.shard], sent_v.at[step], came_v.at[step], there))
    go(chips)

    held, landed = (up, down, biases), (up_in, down_in, biases_in)
    rightmost = shards - 1
    units = up.shape[1]
    thin = units // parts

    def part_of(ref, i, k):
        if i == 2:
            return ref
        span = pl.ds(k * thin, thin) if isinstance(k, int) else pl.ds(pl.multiple_of(k * thin, 128), thin)
        return ref.at[:, span] if i == 0 else ref.at[span, :]

    def matrices(k, source, way):
        kinds = range(3) if isinstance(k, int) and k == 0 else range(2)
        return [
            remote(
                part_of(source[i], i, k), part_of(landed[i], i, k), sent_w.at[(way + 1) // 2, k, i],
                came_w.at[k, i], place.along(way),
            )
            for i in kinds
        ]

    local = [pltpu.make_async_copy(h, t, sent_w.at[2, 0, i]) for i, (h, t) in enumerate(zip(held, landed))]

    def owner_part(k):
        for way, more in ((-1, place.row > 0), (1, place.row < rightmost)):

            @pl.when((place.row == place.root) & more)
            def _(way=way):
                if not isinstance(k, int) or k >= 2:
                    for c in matrices(k - 2, landed, way):
                        c.wait_send()
                go(matrices(k, held, way))

    def pass_part(k):
        @pl.when(place.row != place.root)
        def _():
            for c in matrices(k, landed, 1):
                c.wait_recv()

        for way, more in (
            (-1, (place.row > 0) & (place.row < place.root)),
            (1, (place.row < rightmost) & (place.row > place.root)),
        ):

            @pl.when(more)
            def _(way=way):
                if k >= 2:
                    for c in matrices(k - 2, landed, way):
                        c.wait_send()
                go(matrices(k, landed, way))

    pl.when(place.row == place.root)(lambda: go(local))
    owner_part(0)
    owner_part(1)

    col_all, row_all = placed(place, routes, routes_row, col.shape, row.shape)
    col[...] = col_all
    row[...] = row_all
    upstream = cot[...].astype(F32)

    def send_grads(half):
        for i in range(many):
            e = place.expert_at(half * many + i)
            gate = jnp.where(routes[:, 0:1] == e, gates[:, 0:1], 0.0) + jnp.where(
                routes[:, 1:2] == e, gates[:, 1:2], 0.0
            )
            scaled = (upstream * gate).astype(BF16)
            send_g[half, i] = mm(chosen(row, half * many + i, slots), scaled).astype(BF16)

    def swap_of(half, send, recv, sent, came):
        return place.swap(half, send.at[half], recv.at[half], sent.at[half], came.at[half])

    send_grads(0)
    swap_ga = swap_of(0, send_g, grads_in, sent_g, came_g)
    go(swap_ga)
    send_grads(1)

    over = []
    for step in range(chips_n):
        source = lax.rem(place.chip + step, chips_n) * 2 + place.core
        block = pl.ds(pl.multiple_of(source * share, 16), share)
        if step:
            back = chips_n - step
            chips[2 * back - 2].wait_recv()
            chips[2 * back - 1].wait_recv()
        else:
            own[0].wait()
            own[1].wait()
        at = chips_n + step
        over.append(remote(full.at[block], full.at[block], sent_p.at[at], came_p.at[at], partner))
        over.append(remote(vec_all.at[source], vec_all.at[source], sent_v.at[at], came_v.at[at], partner))
        go(over[-2:])
    for c in over:
        c.wait_recv()
    vectors = vec_all[0]
    for s in range(1, shards):
        vectors = vectors + vec_all[s]
    rows_of[...] = vectors
    gain, shift, bias = vectors[0:2], vectors[2:4], vectors[4:7]
    w_in, w_out = full.at[:, : 3 * width], full.at[:, 3 * width :]

    stream = x[...].astype(F32)
    unit, _ = normalize(stream)
    normed = (unit * gain[0:1, :] + shift[0:1, :]).astype(BF16)
    projected = mm(normed, w_in[...])
    qkv[:, :width] = (projected[:, :width] + bias[0:1, :]).astype(BF16)
    qkv[:, width : 2 * width] = projected[:, width : 2 * width].astype(BF16)
    qkv[:, 2 * width :] = (projected[:, 2 * width :] + bias[1:2, :]).astype(BF16)
    valid = lax.broadcasted_iota(jnp.int32, (lines, lines), 0) < real
    half_lanes = lax.broadcasted_iota(jnp.int32, (lines, SLAB), 1) < HEAD

    def one_image(i, carry):
        rows = pl.ds(pl.multiple_of(i * lines, 16), lines)
        for s in range(width // SLAB):
            q = qkv[rows, s * SLAB : (s + 1) * SLAB]
            k = qkv[rows, width + s * SLAB : width + (s + 1) * SLAB]
            v = qkv[rows, 2 * width + s * SLAB : 2 * width + (s + 1) * SLAB]
            heads = []
            for h in range(2):
                keep = half_lanes if h == 0 else ~half_lanes
                scores = mt(jnp.where(keep, k, jnp.zeros_like(k)), q) * (HEAD**-0.5)
                scores = jnp.where(valid, scores, -1e30)
                powers = jnp.exp(scores - jnp.max(scores, axis=0, keepdims=True))
                soft = powers / jnp.sum(powers, axis=0, keepdims=True)
                heads.append(tm(soft.astype(BF16), v))
            context[rows, s * SLAB : (s + 1) * SLAB] = jnp.where(half_lanes, heads[0], heads[1]).astype(BF16)
        return carry

    lax.fori_loop(0, images, one_image, 0)
    owner_part(2)
    pass_part(0)
    middle = stream + mm(context[...], w_out[...]) + bias[2:3, :]
    middle_out[...] = middle
    unit, _ = normalize(middle)
    normed = (unit * gain[1:2, :] + shift[1:2, :]).astype(BF16)

    def send_tokens(half):
        for i in range(many):
            send_r[half, i] = mm(chosen(row, half * many + i, slots), normed).astype(BF16)

    send_tokens(0)
    swap_ra = swap_of(0, send_r, rows_in, sent_r, came_r)
    go(swap_ra)
    owner_part(3)
    pass_part(1)
    send_tokens(1)
    index = lax.broadcasted_iota(jnp.int32, (tokens, 1), 0)
    counts = jnp.where(lax.rem(index, lines) < real, 1.0, 0.0)
    squares[0:1, :] = jnp.sum(stream * stream, axis=0, keepdims=True)
    squares[1:2, :] = jnp.sum(middle * middle * counts, axis=0, keepdims=True)
    owner_part(4)
    pass_part(2)
    for c in swap_ga + swap_ra:
        c.wait()
    swap_gb = swap_of(1, send_g, grads_in, sent_g, came_g)
    swap_rb = swap_of(1, send_r, rows_in, sent_r, came_r)
    go(swap_gb + swap_rb)
    owner_part(5)
    pass_part(3)

    wide = units // chunks
    each = parts // chunks
    pl.when(place.row == place.root)(lambda: [c.wait() for c in local] and None)
    made_to, back_to = (rows_in.at[0], made_b), (grads_in.at[0], back_b)

    def work(half, j):
        cols = slice(j * wide, (j + 1) * wide)
        sum_up[...] = jnp.zeros_like(sum_up)
        sum_down[...] = jnp.zeros_like(sum_down)
        if half == 0:
            sum_small[:, cols] = jnp.zeros((1, wide), F32)
            if j == 0:
                sum_small[:, units:] = jnp.zeros((1, width), F32)

        def block(i, carry):
            rows, given = rows_in[half, i], grads_in[half, i]
            made, back, part_up, part_down, small = expert_step(
                rows, given, up_in[:, cols], down_in[cols, :], biases_in[:, cols]
            )
            sum_up[...] += part_up
            sum_down[...] += part_down
            sum_small[:, cols] += small
            if j == 0:
                made += biases_in[:, units:]
                sum_small[:, units:] += jnp.sum(given.astype(F32), axis=0, keepdims=True)
            else:
                made += made_sum[i]
                back += back_sum[i]
            if j < chunks - 1:
                made_sum[i] = made
                back_sum[i] = back
            else:
                made_to[half][i] = made.astype(BF16)
                back_to[half][i] = back.astype(BF16)
            return carry

        lax.fori_loop(0, many, block, 0)
        if half == 0:
            d_up[:, cols] = sum_up[...].astype(BF16)
            d_down[cols, :] = sum_down[...].astype(BF16)
        else:
            d_up[:, cols] = (sum_up[...] + d_up[:, cols].astype(F32)).astype(BF16)
            d_down[cols, :] = (sum_down[...] + d_down[cols, :].astype(F32)).astype(BF16)

    for j in range(chunks):
        for k in range(max(4, j * each), (j + 1) * each):
            if k + 2 < parts:
                owner_part(k + 2)
            pass_part(k)
        work(0, j)
    swap_b = place.swap(0, grads_in.at[0], back_a, sent_b, came_b)
    go(swap_b)
    for c in swap_gb + swap_rb:
        c.wait()
    for j in range(chunks):
        work(1, j)
        if j == chunks // 2:
            for c in swap_b:
                c.wait()
            swap_m = place.swap(0, rows_in.at[0], made_a, sent_m, came_m)
            go(swap_m)
    d_down[units:, :] = jnp.zeros((d_down.shape[0] - units, width), BF16)
    for i in range(units // width + 1):
        d_down[units + i : units + i + 1, :] = sum_small[:, i * width : (i + 1) * width].astype(BF16)

    for c in chips + over:
        c.wait_send()
    for way, more in (
        (-1, (place.row > 0) & (place.row <= place.root)),
        (1, (place.row < rightmost) & (place.row >= place.root)),
    ):

        @pl.when(more)
        def _(way=way):
            for k in range(parts - 2, parts):
                for c in matrices(k, landed, way):
                    c.wait_send()

    for c in swap_m:
        c.wait()


def finish_kernel(
    images, real, parts,
    back, made, back_a, made_a, up, down, x, cot, full, vecs, qkv, context, middle, col, gates, routes, squares,
    d_x, out, d_gates, up_out, down_out, shares_out, vec_out,
    back_b, made_b, up_l, down_l, up_r, down_r, d_qkv, d_context, grads, vec, from_core, from_chip, cut, from_all,
    vec_group, vec_rows,
    sent_b, came_b, sent_m, came_m, sent_c, came_l, came_r, sent_d, came_d, sent_o, came_o,
    sent_1, came_1, sent_2, came_2, sent_3, came_3, sent_4, came_4, sent_5, came_5, sent_6, came_6,
):
    place = Place()
    tokens, width = x.shape
    lines = tokens // images
    many, slots, _ = back_b.shape
    experts = 2 * many
    shards = place.shards
    chips = shards // 2
    back_in, made_in = (back_a, back_b), (made_a, made_b)
    place.greet_all()

    def go(copies):
        for c in copies:
            c.start()

    swap_b = place.swap(1, back, back_b, sent_b, came_b)
    go(swap_b)

    rightmost = shards - 1
    row, root = place.row, place.root
    mine, total = (up, down), (up_out, down_out)
    left, right = (up_l, down_l), (up_r, down_r)
    heights = (up.shape[0] // parts, down.shape[0] // parts)

    def piece(refs, i, k):
        start = k * heights[i]
        if not isinstance(k, int):
            start = pl.multiple_of(start, 16)
        return refs[i].at[pl.ds(start, heights[i])]

    def hop(k, source, target, came, way):
        return [
            remote(piece(source, i, k), piece(target, i, k), sent_c.at[k, i], came.at[k, i], place.along(way))
            for i in range(2)
        ]

    def add(k, target, terms):
        for i in range(2):
            value = piece(terms[0], i, k)[...].astype(F32)
            for t in terms[1:]:
                value += piece(t, i, k)[...].astype(F32)
            piece(target, i, k)[...] = value.astype(BF16)

    def arrived(k, buffer, came):
        for c in hop(k, buffer, buffer, came, 1):
            c.wait_recv()

    def left_free(k):
        for c in hop(k, left, left, came_l, 1):
            c.wait_send()

    def chain(k):
        @pl.when((row > 0) & (row < root))
        def _():
            arrived(k, left, came_l)
            add(k, left, [mine, left])

        @pl.when((row < rightmost) & (row > root))
        def _():
            arrived(k, right, came_r)
            add(k, right, [mine, right])

        if not isinstance(k, int) or k >= 2:
            pl.when(row != root)(lambda: left_free(k - 2))
        pl.when((row == 0) & (row < root))(lambda: go(hop(k, mine, left, came_l, 1)))
        pl.when((row == rightmost) & (row > root))(lambda: go(hop(k, mine, right, came_r, -1)))
        pl.when((row > 0) & (row < root))(lambda: go(hop(k, left, left, came_l, 1)))
        pl.when((row < rightmost) & (row > root))(lambda: go(hop(k, right, right, came_r, -1)))

        @pl.when(row == root)
        def _():
            @pl.when(row > 0)
            def _():
                arrived(k, left, came_l)
                add(k, total, [mine, left])

            @pl.when(row == 0)
            def _():
                arrived(k, right, came_r)
                add(k, total, [mine, right])

            @pl.when((row > 0) & (row < rightmost))
            def _():
                arrived(k, right, came_r)
                add(k, total, [total, right])

            for step in range(1, chips):
                go(spread(k, step))
            go(cross(k))

    root_core = jnp.where(row < chips, 0, 1)
    root_chip = jnp.where(row < chips, row, rightmost - row)
    partner = (place.expert, place.shard + 1 - 2 * place.core)

    def chip_at(step):
        return lax.rem(place.chip + step, chips)

    def spread(k, step):
        there = (place.expert, chip_at(step) * 2 + place.core)
        return [
            remote(piece(total, i, k), piece(total, i, k), sent_d.at[step - 1, k, i], came_d.at[k, i], there)
            for i in range(2)
        ]

    def cross(k):
        return [
            remote(piece(total, i, k), piece(total, i, k), sent_o.at[k, i], came_o.at[k, i], partner)
            for i in range(2)
        ]

    def hand_out(k):
        @pl.when((place.core == root_core) & (place.chip != root_chip))
        def _():
            for c in spread(k, 1):
                c.wait_recv()
            go(cross(k))

        @pl.when(place.core != root_core)
        def _():
            for c in cross(k):
                c.wait_recv()

    for k in range(4):
        chain(k)
    for c in swap_b:
        c.wait()
    swap_m = place.swap(1, made, made_b, sent_m, came_m)
    go(swap_m)

    gain, shift = vecs[0:2], vecs[2:4]
    w_in, w_out = full.at[:, : 3 * width], full.at[:, 3 * width :]
    back_two = jnp.zeros((tokens, width), F32)
    for j in range(experts):
        back_two += mm(taken(col, j, slots), back_in[j // many][j % many])
    unit, inverse = normalize(middle[...])
    vec[1:2, :] = jnp.sum(back_two * unit, axis=0, keepdims=True)
    vec[3:4, :] = jnp.sum(back_two, axis=0, keepdims=True)
    back_middle = cot[...].astype(F32) + normalize_back(back_two, unit, inverse, gain[1:2, :])
    d_x[...] = back_middle
    branch = back_middle.astype(BF16)
    vec[6:7, :] = jnp.sum(branch.astype(F32), axis=0, keepdims=True)
    grads[:, 3 * width :] = tm(context[...], branch).astype(BF16)
    d_context[...] = mt(branch, w_out[...]).astype(BF16)
    valid = lax.broadcasted_iota(jnp.int32, (lines, lines), 0) < real
    half = lax.broadcasted_iota(jnp.int32, (lines, SLAB), 1) < HEAD
    scale = HEAD**-0.5
    vec[4:6, :] = jnp.zeros((2, width), F32)
    chain(4)

    def one_image(i, carry):
        rows = pl.ds(pl.multiple_of(i * lines, 16), lines)
        for s in range(width // SLAB):
            cols = [slice(a * width + s * SLAB, a * width + (s + 1) * SLAB) for a in range(3)]
            q, k, v = (qkv[rows, c] for c in cols)
            given = d_context[rows, cols[0]]
            heads = []
            for h in range(2):
                keep = half if h == 0 else ~half
                zero = jnp.zeros_like(k)
                scores = mt(jnp.where(keep, k, zero), q) * scale
                scores = jnp.where(valid, scores, -1e30)
                powers = jnp.exp(scores - jnp.max(scores, axis=0, keepdims=True))
                soft = powers / jnp.sum(powers, axis=0, keepdims=True)
                back_soft = mt(jnp.where(keep, v, zero), given)
                shared = jnp.sum(back_soft * soft, axis=0, keepdims=True)
                back_scores = (soft * (back_soft - shared)).astype(BF16)
                heads.append((tm(back_scores, k), mm(back_scores, q), mm(soft.astype(BF16), given)))
            both = [jnp.where(half, a, b) for a, b in zip(*heads)]
            both = [both[0] * scale, both[1] * scale, both[2]]
            vec[4:5, cols[0]] += jnp.sum(both[0], axis=0, keepdims=True)
            vec[5:6, cols[0]] += jnp.sum(both[2], axis=0, keepdims=True)
            for c, grad in zip(cols, both):
                d_qkv[rows, c] = grad.astype(BF16)
        pl.when(i < parts - 5)(lambda: chain(i + 5))
        return carry

    lax.fori_loop(0, images, one_image, 0)
    for k in range(images + 5, parts):
        chain(k)
    unit, inverse = normalize(x[...].astype(F32))
    normed = (unit * gain[0:1, :] + shift[0:1, :]).astype(BF16)
    grads[:, : 3 * width] = tm(normed, d_qkv[...]).astype(BF16)

    share = width // shards
    halves = [
        remote(
            grads.at[pl.ds(pl.multiple_of((2 * c + 1 - place.core) * share, 16), share)], from_core.at[c],
            sent_1.at[c], came_1.at[c], partner,
        )
        for c in range(chips)
    ]
    go(halves)
    back_one = mt(d_qkv[...], w_in[...])
    vec[0:1, :] = jnp.sum(back_one * unit, axis=0, keepdims=True)
    vec[2:3, :] = jnp.sum(back_one, axis=0, keepdims=True)
    d_x[...] += normalize_back(back_one, unit, inverse, gain[0:1, :])
    for c in range(chips):
        halves[c].wait_recv()
        block = pl.ds(pl.multiple_of((2 * c + place.core) * share, 16), share)
        from_core[c] = (from_core[c].astype(F32) + grads[block, :].astype(F32)).astype(BF16)
    quarters = [
        remote(
            from_core.at[chip_at(step)], from_chip.at[place.chip], sent_2.at[step], came_2.at[step],
            (place.expert, chip_at(step) * 2 + place.core),
        )
        for step in range(1, chips)
    ]
    go(quarters)
    for k in range(4):
        hand_out(k)

    for c in swap_m:
        c.wait()
    upstream = cot[...].astype(F32)
    stream = middle[...]

    def gathered(r):
        found = jnp.zeros((tokens, width), F32)
        for j in range(experts):
            slot = jnp.where(routes[:, r : r + 1] == place.expert_at(j), col[:, j : j + 1], -1.0)
            found += mm(taken(slot, 0, slots), made_in[j // many][j % many])
        d_gates[:, r : r + 1] = jnp.sum(found * upstream, axis=1, keepdims=True)
        return found * gates[:, r : r + 1]

    stream += gathered(0)
    for c in quarters:
        c.wait_recv()
    whole = from_core[place.chip].astype(F32)
    for step in range(1, chips):
        whole += from_chip[chip_at(step)].astype(F32)
    whole = whole.astype(BF16)
    down_n = share // 16
    across_n = experts // down_n
    wide = cut.shape[2]
    for r in range(down_n):
        for c in range(across_n):
            cut[r * across_n + c] = whole[r * 16 : (r + 1) * 16, c * wide : (c + 1) * wide]

    def other(step):
        return lax.rem(place.expert + step, experts)

    pieces = [
        remote(
            cut.at[other(step)], from_all.at[place.expert], sent_3.at[step], came_3.at[step],
            (other(step), place.shard),
        )
        for step in range(1, experts)
    ]
    go(pieces)
    stream += gathered(1)
    out[...] = stream.astype(BF16)
    index = lax.broadcasted_iota(jnp.int32, (tokens, 1), 0)
    counts = jnp.where(lax.rem(index, lines) < real, 1.0, 0.0)
    vec[7:8, :] = jnp.zeros((1, width), F32)
    vec[8:10, :] = squares[...]
    vec[10:11, :] = jnp.sum(stream * stream * counts, axis=0, keepdims=True)
    vec[11:16, :] = jnp.zeros((5, width), F32)
    vec_group[place.member] = vec[...]
    lists = [
        remote(vec, vec_group.at[place.member], sent_5.at[step], came_5.at[step], place.peer(step)[1])
        for step in range(1, experts)
    ]
    go(lists)
    for c in pieces:
        c.wait_recv()
    whole = cut[place.expert].astype(F32)
    for step in range(1, experts):
        whole += from_all[other(step)].astype(F32)
    shares_out[place.expert] = whole.astype(BF16)
    spreads = [
        remote(
            shares_out.at[place.expert], shares_out.at[place.expert], sent_4.at[step], came_4.at[step],
            (other(step), place.shard),
        )
        for step in range(1, experts)
    ]
    go(spreads)
    for c in lists:
        c.wait_recv()
    whole = vec_group[0]
    for j in range(1, experts):
        whole += vec_group[j]
    vec_rows[row] = whole
    downs = [
        remote(
            vec_rows.at[row], vec_rows.at[row], sent_6.at[step], came_6.at[step],
            (lax.rem(place.expert + step * place.width, experts), place.shard),
        )
        for step in range(1, shards)
    ]
    go(downs)
    for k in range(4, parts):
        hand_out(k)
    for c in downs:
        c.wait_recv()
    whole = vec_rows[0]
    for j in range(1, shards):
        whole += vec_rows[j]
    vec_out[...] = whole
    for c in spreads:
        c.wait_recv()
    for c in halves + quarters + pieces + spreads + lists + downs:
        c.wait_send()
    for k in range(parts - 2, parts):
        pl.when(row != root)(lambda k=k: left_free(k))

    def sends(k, carry):
        @pl.when(row == root)
        def _():
            for step in range(1, chips):
                for c in spread(k, step):
                    c.wait_send()

        @pl.when(place.core == root_core)
        def _():
            for c in cross(k):
                c.wait_send()

        return carry

    lax.fori_loop(0, parts, sends, 0)


def local(
    images, attention_in, attention_out, layer_gain, layer_shift, attention_bias, expert_up, hidden_bias,
    expert_down, expert_bias, routes, gates, cotangent,
):
    count, real, width = images.shape
    lines = up_to(real, 16)
    tokens = count * lines
    experts = lax.axis_size("expert")
    shards = lax.axis_size("shard")
    slots = up_to(max(2, 4 * count * real // experts), 16)
    hidden_units = expert_up.shape[2]

    def padded(values, fill=0):
        wide = jnp.pad(values, ((0, 0), (0, lines - real), (0, 0)), constant_values=fill)
        return wide.reshape(tokens, values.shape[2])

    mats = jnp.concatenate([attention_in, attention_out], axis=1)
    vectors = jnp.concatenate([layer_gain, layer_shift, attention_bias], axis=0).astype(F32)
    vectors = lax.dynamic_update_slice(
        jnp.zeros((8, width), F32), vectors, (0, lax.axis_index("shard") * vectors.shape[1])
    )
    biases = jnp.concatenate([hidden_bias, expert_bias], axis=1).astype(F32)

    x, cot = padded(images), padded(cotangent)
    route_col, gate_col = padded(routes, -1), padded(gates)
    parts, chunks = 8, 4
    many = experts // 2
    low = hidden_units + 16 * parts
    half_block = (many, slots, width)
    dma = pltpu.SemaphoreType.DMA
    vmem = lambda *shape: pltpu.VMEM(shape, BF16)
    wide_vmem = lambda *shape: pltpu.VMEM(shape, F32)
    (
        back_a, made_a, back, made, d_up, d_down, middle, qkv, context, squares, full, vecs, col,
    ) = call(
        functools.partial(forward_kernel, count, real, parts, chunks),
        [
            (half_block, BF16), (half_block, BF16), (half_block, BF16), (half_block, BF16),
            ((width, hidden_units), BF16), ((low, width), BF16), ((tokens, width), F32),
            ((tokens, 3 * width), BF16), ((tokens, width), BF16), ((2, width), F32), ((width, 4 * width), BF16),
            ((8, width), F32), ((tokens, up_to(experts, 128)), F32),
        ],
        [
            x, cot, gate_col, route_col, route_col.T, mats, vectors, expert_up[0], expert_down[0], biases,
        ],
        [
            vmem(2, *half_block), vmem(2, *half_block), vmem(2, *half_block), vmem(2, *half_block),
            vmem(width, hidden_units), vmem(hidden_units, width), wide_vmem(1, hidden_units + width),
            wide_vmem(*half_block), wide_vmem(*half_block), wide_vmem(width, hidden_units // chunks),
            wide_vmem(hidden_units // chunks, width), wide_vmem(1, hidden_units + width),
            wide_vmem(up_to(experts, 8), tokens), wide_vmem(shards, 8, width),
            dma((2, many)), dma((2, many)), dma((2, many)), dma((2, many)),
            dma((shards,)), dma((shards,)), dma((shards,)), dma((shards,)),
            dma((3, parts, 3)), dma((parts, 3)),
            dma((many,)), dma((many,)), dma((many,)), dma((many,)),
        ],
        outside=(7, 8, 9),
        collective=0,
    )

    share = width // shards
    across = experts // (share // 16)
    wide = 4 * width // across
    d_x, out, d_gates, up_total, down_total, owned, vector_sums = call(
        functools.partial(finish_kernel, count, real, parts),
        [
            ((tokens, width), F32), ((tokens, width), BF16), ((tokens, TOP), F32), (d_up.shape, BF16),
            (d_down.shape, BF16), ((experts, 16, wide), BF16), ((16, width), F32),
        ],
        [
            back, made, back_a, made_a, d_up, d_down, x, cot, full, vecs, qkv, context, middle, col,
            gate_col, route_col, squares,
        ],
        [
            vmem(*half_block), vmem(*half_block), vmem(*d_up.shape), vmem(*d_down.shape), vmem(*d_up.shape),
            vmem(*d_down.shape), vmem(tokens, 3 * width), vmem(tokens, width), vmem(width, 4 * width),
            pltpu.VMEM((16, width), F32), vmem(shards // 2, share, 4 * width), vmem(shards // 2, share, 4 * width),
            vmem(experts, 16, wide), vmem(experts, 16, wide), pltpu.VMEM((experts, 16, width), F32),
            pltpu.VMEM((shards, 16, width), F32),
            dma((many,)), dma((many,)), dma((many,)), dma((many,)),
            dma((parts, 2)), dma((parts, 2)), dma((parts, 2)),
            dma((shards // 2, parts, 2)), dma((parts, 2)), dma((parts, 2)), dma((parts, 2)),
            dma((shards,)), dma((shards,)), dma((shards,)), dma((shards,)),
            dma((experts,)), dma((experts,)), dma((experts,)), dma((experts,)),
            dma((experts,)), dma((experts,)), dma((shards,)), dma((shards,)),
        ],
        outside=(0, 1),
        collective=1,
    )
    entries = float(count * real * width * experts * shards)
    magnitude = jnp.sqrt(jnp.sum(vector_sums[8:11], axis=1) / entries)
    owned = owned.reshape(share // 16, across, 16, wide).transpose(0, 2, 1, 3).reshape(share, 4 * width)
    owned = owned.astype(F32)
    vectors = lax.dynamic_slice(vector_sums, (0, lax.axis_index("shard") * share), (7, share))
    small = down_total[hidden_units:].astype(F32)

    def cut(values):
        return values.reshape(count, lines, values.shape[1])[:, :real]

    return (
        cut(out),
        cut(d_x),
        owned[:, : 3 * width],
        owned[:, 3 * width : 4 * width],
        vectors[0:2],
        vectors[2:4],
        vectors[4:7],
        up_total.astype(F32)[None],
        small[: hidden_units // width].reshape(1, hidden_units),
        down_total[:hidden_units].astype(F32)[None],
        small[hidden_units // width : hidden_units // width + 1],
        cut(d_gates),
        magnitude,
    )


def solution(mesh):
    every = P(("expert", "shard"), None, None)
    return jax.shard_map(
        local,
        mesh=mesh,
        in_specs=(
            every, P("shard", None), P("shard", None), P(None, "shard"), P(None, "shard"), P(None, "shard"),
            P("expert", None, None), P("expert", None), P("expert", None, None), P("expert", None),
            every, every, every,
        ),
        out_specs=(
            every, every, P("shard", None), P("shard", None), P(None, "shard"), P(None, "shard"),
            P(None, "shard"), P("expert", None, None), P("expert", None), P("expert", None, None),
            P("expert", None), every, P(),
        ),
        check_vma=False,
    )
```

```python
import functools

import jax
import jax.numpy as jnp
from jax import lax
from jax.experimental import pallas as pl
from jax.experimental.pallas import tpu as pltpu
from jax.sharding import PartitionSpec as P

HEAD = 64
SLAB = 2 * HEAD
TOP = 2
EPSILON = 1e-06
F32, BF16 = jnp.float32, jnp.bfloat16
VMEM_LIMIT = 60 * 1024 * 1024


def dot_of(contract):
    def run(left, right):
        return lax.dot_general(
            left, right, (contract, ((), ())), preferred_element_type=F32
        )

    return run


mm = dot_of(((1,), (0,)))
mt = dot_of(((1,), (1,)))
tm = dot_of(((0,), (0,)))


def up_to(value, step):
    return -(-value // step) * step


def normalize(values):
    centre = values - jnp.mean(values, axis=-1, keepdims=True)
    inverse = lax.rsqrt(jnp.mean(centre * centre, axis=-1, keepdims=True) + EPSILON)
    return centre * inverse, inverse


def normalize_back(incoming, unit, inverse, weight):
    scaled = incoming * weight
    first_mean = jnp.mean(scaled, axis=-1, keepdims=True)
    second_mean = jnp.mean(scaled * unit, axis=-1, keepdims=True)
    return inverse * (scaled - first_mean - unit * second_mean)


def gelu_pair(value):
    size = jnp.abs(value)
    t = 1.0 / (1.0 + (0.3275911 * 0.7071067811865476) * size)
    bell = jnp.exp(-0.5 * value * value)
    poly = 0.5 * 1.061405429
    for c in (-1.453152027, 1.421413741, -0.284496736, 0.254829592):
        poly = poly * t + 0.5 * c
    tail = poly * t * bell
    normal = jnp.where(value >= 0, 1.0 - tail, tail)
    return value * normal, normal + value * (bell * 0.3989422804014327)


def call(body, outs, args, scratch=(), outside=(), collective=None):
    where = [
        pl.BlockSpec(memory_space=pl.ANY if i in outside else pltpu.VMEM) for i in range(len(args) + len(outs))
    ]
    return pl.pallas_call(
        body,
        out_shape=[jax.ShapeDtypeStruct(s, d) for s, d in outs],
        in_specs=where[: len(args)],
        out_specs=where[len(args) :],
        scratch_shapes=list(scratch),
        compiler_params=pltpu.CompilerParams(
            vmem_limit_bytes=VMEM_LIMIT, collective_id=collective, has_side_effects=collective is not None
        ),
    )(*args)


def axes():
    return (
        lax.axis_index("expert"), lax.axis_index("shard"), lax.axis_size("expert"), lax.axis_size("shard")
    )


class Place:
    def __init__(self):
        self.expert, self.shard, self.experts, self.shards = axes()
        self.width = self.experts // self.shards
        self.row = lax.div(self.expert, self.width)
        self.member = lax.rem(self.expert, self.width) * self.shards + self.shard
        self.core = lax.rem(self.shard, 2)
        self.chip = lax.div(self.shard, 2)
        self.root = self.chip * (1 - self.core) + (self.shards - 1 - self.chip) * self.core

    def peer(self, step):
        other = lax.rem(self.member + step, self.experts)
        return other, (self.row * self.width + lax.div(other, self.shards), lax.rem(other, self.shards))

    def expert_at(self, number):
        many = self.experts // 2
        chips = self.shards // 2
        half, spot = divmod(number, many)
        core = self.core * (1 - half) + (1 - self.core) * half
        chip = spot % chips
        return (chip * (1 - core) + (self.shards - 1 - chip) * core) * self.width + spot // chips

    def expert_at_all(self, shape, axis):
        at = lax.broadcasted_iota(jnp.int32, shape, axis)
        experts = jnp.full(shape, -9.0, F32)
        for number in range(self.experts):
            experts = jnp.where(at == number, self.expert_at(number).astype(F32), experts)
        return experts

    def swap(self, half, send, recv, sent, came):
        many = self.experts // 2
        chips = self.shards // 2
        spot = lax.div(self.member, 2)
        core = self.core if half == 0 else 1 - self.core
        copies = []
        if half == 0:
            copies.append(pltpu.make_async_copy(send.at[spot], recv.at[spot], sent.at[0]))
        for step in range(1 - half, many):
            other = lax.rem(spot + step, many)
            device = (self.row * self.width + lax.div(other, chips), lax.rem(other, chips) * 2 + core)
            copies.append(remote(send.at[other], recv.at[spot], sent.at[step], came.at[step], device))
        return copies

    def along(self, step):
        return (self.expert + step * self.width, self.shard)

    def greet(self):
        barrier = pltpu.get_barrier_semaphore()
        for step in range(1, self.experts):
            tell(barrier, self.peer(step)[1])
        pl.when(self.row > 0)(lambda: tell(barrier, self.along(-1)))
        pl.when(self.row < self.shards - 1)(lambda: tell(barrier, self.along(1)))
        ends = jnp.where(self.row > 0, 1, 0) + jnp.where(self.row < self.shards - 1, 1, 0)
        pl.semaphore_wait(barrier, self.experts - 1 + ends)


    def greet_all(self):
        barrier = pltpu.get_barrier_semaphore()
        for step in range(1, self.experts):
            tell(barrier, self.peer(step)[1])
        for rows in range(1, self.shards):
            for at in range(self.width):
                line = lax.rem(self.row + rows, self.shards) * self.width + at
                tell(barrier, (line, self.shard))
        pl.semaphore_wait(barrier, self.experts - 1 + (self.shards - 1) * self.width)


def tell(semaphore, device):
    pl.semaphore_signal(semaphore, inc=1, device_id=device, device_id_type=pl.DeviceIdType.MESH)


def remote(src, dst, sent, came, device):
    return pltpu.make_async_remote_copy(
        src_ref=src, dst_ref=dst, send_sem=sent, recv_sem=came, device_id=device,
        device_id_type=pl.DeviceIdType.MESH,
    )


def placed(place, col_in, row_in, col_shape, row_shape):
    tokens = col_in.shape[0]
    down = lax.broadcasted_iota(jnp.int32, (tokens, tokens), 0)
    across = lax.broadcasted_iota(jnp.int32, (tokens, tokens), 1)
    lanes = place.expert_at_all(col_shape, 1)
    named = (col_in[:, 0:1] == lanes) | (col_in[:, 1:2] == lanes)
    before = (across < down).astype(F32).astype(BF16)
    ranks = mm(before, named.astype(F32).astype(BF16))
    col = jnp.where(named, ranks, -1.0)
    lines = place.expert_at_all(row_shape, 0)
    named = (row_in[0:1, :] == lines) | (row_in[1:2, :] == lines)
    before = (down < across).astype(F32).astype(BF16)
    ranks = mm(named.astype(F32).astype(BF16), before)
    return col, jnp.where(named, ranks, -1.0)


def chosen(row_ref, expert, slots):
    tokens = row_ref.shape[1]
    index = lax.broadcasted_iota(jnp.int32, (slots, tokens), 0).astype(F32)
    return jnp.where(index == row_ref[expert : expert + 1, :], 1.0, 0.0).astype(BF16)


def taken(col, expert, slots):
    index = lax.broadcasted_iota(jnp.int32, (col.shape[0], slots), 1).astype(F32)
    return jnp.where(index == col[:, expert : expert + 1], 1.0, 0.0).astype(BF16)


def expert_step(x, g, up, down, bias):
    hidden = mm(x, up) + bias
    back_active = mt(g, down)
    active, slope = gelu_pair(hidden)
    active = active.astype(BF16)
    back_hidden = back_active * slope
    sums = jnp.sum(back_hidden, axis=0, keepdims=True)
    back_hidden = back_hidden.astype(BF16)
    return mm(active, down), mt(back_hidden, up), tm(x, back_hidden), tm(active, g), sums


def forward_kernel(
    images, real, parts, chunks,
    x, cot, both, both_row, mats, vecs, up, down, biases,
    back_a, grads_in, rows_in, d_up, d_down, d_small, middle_out, qkv, context, squares, full, rows_of, col,
    send_g, send_r, up_in, down_in, biases_in, made_sum, back_sum, sum_up, sum_down, sum_small,
    row, vec_all,
    sent_g, came_g, sent_r, came_r, sent_p, came_p, sent_v, came_v, sent_w, came_w, sent_b, came_b,
):
    place = Place()
    tokens, width = x.shape
    routes, routes_row = both[:, 0:TOP] - 1.0, both_row[0:TOP, :] - 1.0
    gates = both[:, TOP:]
    lines = tokens // images
    _, many, slots, _ = send_r.shape
    shards = place.shards
    chips_n = shards // 2
    place.greet()

    def go(copies):
        for c in copies:
            c.start()

    share = mats.shape[0]
    mine = pl.ds(pl.multiple_of(place.shard * share, 16), share)
    partner = (place.expert, place.shard + 1 - 2 * place.core)
    own = [
        pltpu.make_async_copy(mats, full.at[mine], sent_p.at[0]),
        pltpu.make_async_copy(vecs, vec_all.at[place.shard], sent_v.at[0]),
    ]
    go(own)
    chips = []
    for step in range(1, chips_n):
        there = (place.expert, lax.rem(place.chip + step, chips_n) * 2 + place.core)
        chips.append(remote(mats, full.at[mine], sent_p.at[step], came_p.at[step], there))
        chips.append(remote(vecs, vec_all.at[place.shard], sent_v.at[step], came_v.at[step], there))
    go(chips)

    held, landed = (up, down, biases), (up_in, down_in, biases_in)
    rightmost = shards - 1
    flight = 3
    units = up.shape[1]
    thin = units // parts

    hops = jnp.abs(place.row - place.root)
    sides = ((-1, place.row > 0), (1, place.row < rightmost))

    def part_of(ref, i, k):
        span = pl.ds(k * thin, thin) if isinstance(k, int) else pl.ds(pl.multiple_of(k * thin, 128), thin)
        return ref.at[:, span] if i == 0 else ref.at[span, :]

    def matrices(k, source, way):
        return [
            remote(
                part_of(source[i], i, k), part_of(landed[i], i, k), sent_w.at[(way + 1) // 2, k, i],
                came_w.at[k, i], place.along(way),
            )
            for i in range(2)
        ]

    def bias_copy(source, way):
        return remote(source[2], landed[2], sent_w.at[(way + 1) // 2, 0, 2], came_w.at[0, 2], place.along(way))

    local = [pltpu.make_async_copy(h, t, sent_w.at[2, 0, i]) for i, (h, t) in enumerate(zip(held, landed))]

    def onward(way):
        return (place.row > 0) & (place.row < place.root) if way < 0 else (place.row < rightmost) & (place.row > place.root)

    def owner_part(k):
        for way, more in sides:

            @pl.when((place.row == place.root) & more)
            def _(way=way):
                if not isinstance(k, int) or k >= flight:
                    for c in matrices(k - flight, landed, way):
                        c.wait_send()
                go(matrices(k, held, way))

    def pass_part(k):
        for c in matrices(k, landed, 1):
            c.wait_recv()
        for way in (-1, 1):

            @pl.when(onward(way))
            def _(way=way):
                @pl.when(k >= flight)
                def _():
                    for c in matrices(k - flight, landed, way):
                        c.wait_send()

                go(matrices(k, landed, way))

    steps_done, sure = [0], [0]

    def matrix_step(p, owner=True):
        if owner:
            pl.when(p + flight < parts)(lambda: owner_part(p + flight)) if not isinstance(p, int) else (
                owner_part(p + flight) if p + flight < parts else None
            )
        k = p - 2 * (hops - 1)
        pl.when((hops > 0) & (k >= sure[0]) & (k < parts))(lambda: pass_part(k))

    def move_on(count, owner=True):
        for _ in range(count):
            matrix_step(steps_done[0], owner)
            steps_done[0] += 1

    def ensure(count):
        for k in range(sure[0], count):
            pl.when((hops > 0) & (k >= steps_done[0] - 2 * (hops - 1)))(lambda k=k: pass_part(k))
        sure[0] = max(sure[0], count)

    pl.when(place.row == place.root)(lambda: go(local))
    for way, more in sides:
        pl.when((place.row == place.root) & more)(lambda way=way: bias_copy(held, way).start())
    for k in range(flight):
        owner_part(k)

    col_all, row_all = placed(place, routes, routes_row, col.shape, row.shape)
    col[...] = col_all
    row[...] = row_all
    upstream = cot[...].astype(F32)

    def send_grads(half):
        for i in range(many):
            e = place.expert_at(half * many + i).astype(F32)
            gate = jnp.where(routes[:, 0:1] == e, gates[:, 0:1], 0.0) + jnp.where(
                routes[:, 1:2] == e, gates[:, 1:2], 0.0
            )
            scaled = (upstream * gate).astype(BF16)
            send_g[half, i] = mm(chosen(row, half * many + i, slots), scaled).astype(BF16)

    def swap_of(half, send, recv, sent, came):
        return place.swap(half, send.at[half], recv.at[half], sent.at[half], came.at[half])

    send_grads(0)
    swap_ga = swap_of(0, send_g, grads_in, sent_g, came_g)
    go(swap_ga)
    send_grads(1)

    over = []
    for step in range(chips_n):
        source = lax.rem(place.chip + step, chips_n) * 2 + place.core
        block = pl.ds(pl.multiple_of(source * share, 16), share)
        if step:
            back = chips_n - step
            chips[2 * back - 2].wait_recv()
            chips[2 * back - 1].wait_recv()
        else:
            own[0].wait()
            own[1].wait()
        at = chips_n + step
        over.append(remote(full.at[block], full.at[block], sent_p.at[at], came_p.at[at], partner))
        over.append(remote(vec_all.at[source], vec_all.at[source], sent_v.at[at], came_v.at[at], partner))
        go(over[-2:])
    for c in over:
        c.wait_recv()
    vectors = vec_all[0]
    for s in range(1, shards):
        vectors = vectors + vec_all[s]
    rows_of[...] = vectors
    gain, shift, bias = vectors[0:2], vectors[2:4], vectors[4:7]
    w_in, w_out = full.at[:, : 3 * width], full.at[:, 3 * width :]

    stream = x[...].astype(F32)
    unit, _ = normalize(stream)
    normed = (unit * gain[0:1, :] + shift[0:1, :]).astype(BF16)
    projected = mm(normed, w_in[...])
    qkv[:, :width] = (projected[:, :width] + bias[0:1, :]).astype(BF16)
    qkv[:, width : 2 * width] = projected[:, width : 2 * width].astype(BF16)
    qkv[:, 2 * width :] = (projected[:, 2 * width :] + bias[1:2, :]).astype(BF16)
    valid = lax.broadcasted_iota(jnp.int32, (lines, lines), 0) < real
    half_lanes = lax.broadcasted_iota(jnp.int32, (lines, SLAB), 1) < HEAD

    def one_image(i, carry):
        rows = pl.ds(pl.multiple_of(i * lines, 16), lines)
        for s in range(width // SLAB):
            q = qkv[rows, s * SLAB : (s + 1) * SLAB]
            k = qkv[rows, width + s * SLAB : width + (s + 1) * SLAB]
            v = qkv[rows, 2 * width + s * SLAB : 2 * width + (s + 1) * SLAB]
            heads = []
            for h in range(2):
                keep = half_lanes if h == 0 else ~half_lanes
                scores = mt(jnp.where(keep, k, jnp.zeros_like(k)), q) * (HEAD**-0.5)
                scores = jnp.where(valid, scores, -1e30)
                powers = jnp.exp(scores - jnp.max(scores, axis=0, keepdims=True))
                soft = powers / jnp.sum(powers, axis=0, keepdims=True)
                heads.append(tm(soft.astype(BF16), v))
            context[rows, s * SLAB : (s + 1) * SLAB] = jnp.where(half_lanes, heads[0], heads[1]).astype(BF16)

        @pl.when((i > 0) & (i <= flight))
        def _():
            owner_part(i + flight - 1)

        return carry

    lax.fori_loop(0, images, one_image, 0)
    started = min(images - 1, flight)
    pl.when(place.row != place.root)(lambda: bias_copy(landed, 1).wait_recv())
    for way, more in sides:
        pl.when(onward(way))(lambda way=way: bias_copy(landed, way).start())
    move_on(started, owner=False)
    middle = stream + mm(context[...], w_out[...]) + bias[2:3, :]
    middle_out[...] = middle
    unit, _ = normalize(middle)
    normed = (unit * gain[1:2, :] + shift[1:2, :]).astype(BF16)

    def send_tokens(half):
        for i in range(many):
            send_r[half, i] = mm(chosen(row, half * many + i, slots), normed).astype(BF16)

    send_tokens(0)
    swap_ra = swap_of(0, send_r, rows_in, sent_r, came_r)
    go(swap_ra)
    move_on(1)
    send_tokens(1)
    index = lax.broadcasted_iota(jnp.int32, (tokens, 1), 0)
    counts = jnp.where(lax.rem(index, lines) < real, 1.0, 0.0)
    squares[0:1, :] = jnp.sum(stream * stream, axis=0, keepdims=True)
    squares[1:2, :] = jnp.sum(middle * middle * counts, axis=0, keepdims=True)
    move_on(2)
    for c in swap_ga + swap_ra:
        c.wait()
    swap_gb = swap_of(1, send_g, grads_in, sent_g, came_g)
    swap_rb = swap_of(1, send_r, rows_in, sent_r, came_r)
    few = many // 2
    go(swap_gb[:few] + swap_rb[:few])
    move_on(1)

    wide = units // chunks
    each = parts // chunks
    pl.when(place.row == place.root)(lambda: [c.wait() for c in local] and None)

    spot = lax.div(place.member, 2)

    def work(half, j, first=0, last=many, stride=0):
        base = steps_done[0]
        cols = slice(j * wide, (j + 1) * wide)
        if half == 0:
            sum_up[j % (chunks - 1)] = jnp.zeros(sum_up.shape[1:], F32)
            sum_down[j % (chunks - 1)] = jnp.zeros(sum_down.shape[1:], F32)
            sum_small[:, cols] = jnp.zeros((1, wide), F32)
            if j == 0:
                sum_small[:, units:] = jnp.zeros((1, width), F32)

        def block(step_at, carry):
            i = lax.rem(spot + many - step_at, many)
            rows, given = rows_in[half, i], grads_in[half, i]
            made, back, part_up, part_down, small = expert_step(
                rows, given, up_in[:, cols], down_in[cols, :], biases_in[:, cols]
            )
            sum_up[j % (chunks - 1)] += part_up
            sum_down[j % (chunks - 1)] += part_down
            sum_small[:, cols] += small
            if j == 0:
                made += biases_in[:, units:]
                sum_small[:, units:] += jnp.sum(given.astype(F32), axis=0, keepdims=True)
            else:
                made += made_sum[half, i]
                back += back_sum[half, i]
            if j < chunks - 1:
                made_sum[half, i] = made
                back_sum[half, i] = back
            else:
                rows_in[half, i] = made.astype(BF16)
                grads_in[half, i] = back.astype(BF16)
            if stride:
                at = lax.div(step_at - first, stride)
                pl.when(lax.rem(step_at - first, stride) == stride - 1)(lambda: matrix_step(base + at))
            return carry

        lax.fori_loop(first, last, block, 0)
        if stride:
            steps_done[0] += (last - first) // stride
        if half and last == many:
            d_up[:, cols] = sum_up[j % (chunks - 1)].astype(BF16)
            d_down[cols, :] = sum_down[j % (chunks - 1)].astype(BF16)

    for j in range(chunks - 1):
        ensure((j + 1) * each)
        work(0, j, 0, many, many // 2)
        if j == 0:
            go(swap_gb[few:] + swap_rb[few:])
    for c in swap_gb[:few] + swap_rb[:few]:
        c.wait()
    for j in range(chunks - 1):
        work(1, j, 0, few, few)
    for c in swap_gb[few:] + swap_rb[few:]:
        c.wait()
    for j in range(chunks - 1):
        work(1, j, few, many, few)
    while steps_done[0] + flight < parts:
        move_on(1)
    ensure(parts)
    work(0, chunks - 1)
    swap_b = place.swap(0, grads_in.at[0], back_a, sent_b, came_b)
    go(swap_b)
    work(1, chunks - 1)
    d_small[...] = jnp.zeros(d_small.shape, BF16)
    for i in range(units // width + 1):
        d_small[i : i + 1, :] = sum_small[:, i * width : (i + 1) * width].astype(BF16)

    for c in chips + over:
        c.wait_send()
    for way, more in sides:

        @pl.when(((place.row == place.root) & more) | onward(way))
        def _(way=way):
            bias_copy(landed, way).wait_send()
            for k in range(parts - flight, parts):
                for c in matrices(k, landed, way):
                    c.wait_send()

    for c in swap_b:
        c.wait()


def finish_kernel(
    images, real, parts, begin,
    back, made, back_a, up, down, small, x, cot, full, vecs, qkv, context, middle, col, both, squares,
    d_x, out, d_gates, up_out, down_out, small_out, shares_out, vec_out,
    back_b, made_a, made_b, up_l, down_l, up_r, down_r, small_rows, d_qkv, d_context, grads, vec, from_core, from_chip, cut, from_all,
    vec_group, vec_rows,
    sent_b, came_b, sent_m, came_m, sent_s, came_s, sent_c, came_l, came_r, sent_d, came_d, sent_o, came_o,
    sent_1, came_1, sent_2, came_2, sent_3, came_3, sent_4, came_4, sent_5, came_5, sent_6, came_6,
):
    place = Place()
    tokens, width = x.shape
    lines = tokens // images
    many, slots, _ = back_b.shape
    experts = 2 * many
    shards = place.shards
    chips = shards // 2
    back_in, made_in = (back_a, back_b), (made_a, made_b)
    place.greet_all()

    def go(copies):
        for c in copies:
            c.start()

    swap_b = place.swap(1, back.at[1], back_b, sent_b, came_b)
    go(swap_b)

    rightmost = shards - 1
    row, root = place.row, place.root
    mine, total = (up, down), (up_out, down_out)
    left, right = (up_l, down_l), (up_r, down_r)
    thin = up.shape[1] // parts
    hops = jnp.where(row < root, row, rightmost - row)
    far = jnp.maximum(root, rightmost - root)

    def piece(refs, i, k):
        span = pl.ds(k * thin, thin) if isinstance(k, int) else pl.ds(pl.multiple_of(k * thin, 128), thin)
        return refs[i].at[:, span] if i == 0 else refs[i].at[span, :]

    def hop(k, source, target, came, way):
        return [
            remote(piece(source, i, k), piece(target, i, k), sent_c.at[k, i], came.at[k, i], place.along(way))
            for i in range(2)
        ]

    def add(k, target, terms):
        for i in range(2):
            value = piece(terms[0], i, k)[...].astype(F32)
            for t in terms[1:]:
                value += piece(t, i, k)[...].astype(F32)
            piece(target, i, k)[...] = value.astype(BF16)

    def arrived(k, buffer, came):
        for c in hop(k, buffer, buffer, came, 1):
            c.wait_recv()

    def left_free(k):
        for c in hop(k, left, left, came_l, 1):
            c.wait_send()

    def chain(step):
        k = begin + step - 2 * hops

        @pl.when((row != root) & (k >= begin) & (k < parts))
        def _():
            @pl.when((row > 0) & (row < root))
            def _():
                arrived(k, left, came_l)
                add(k, left, [mine, left])

            @pl.when((row < rightmost) & (row > root))
            def _():
                arrived(k, right, came_r)
                add(k, right, [mine, right])

            pl.when(k >= begin + 2)(lambda: left_free(k - 2))
            pl.when((row == 0) & (row < root))(lambda: go(hop(k, mine, left, came_l, 1)))
            pl.when((row == rightmost) & (row > root))(lambda: go(hop(k, mine, right, came_r, -1)))
            pl.when((row > 0) & (row < root))(lambda: go(hop(k, left, left, came_l, 1)))
            pl.when((row < rightmost) & (row > root))(lambda: go(hop(k, right, right, came_r, -1)))

        t = begin + step - 2 * far

        @pl.when((row == root) & (t >= begin) & (t < parts))
        def _():
            @pl.when(row > 0)
            def _():
                arrived(t, left, came_l)
                add(t, total, [mine, left])

            @pl.when(row == 0)
            def _():
                arrived(t, right, came_r)
                add(t, total, [mine, right])

            @pl.when((row > 0) & (row < rightmost))
            def _():
                arrived(t, right, came_r)
                add(t, total, [total, right])

            give(t)

    def give(k):
        for step in range(1, chips):
            go(spread(k, step))
        go(cross(k))

    root_core = jnp.where(row < chips, 0, 1)
    root_chip = jnp.where(row < chips, row, rightmost - row)
    partner = (place.expert, place.shard + 1 - 2 * place.core)

    def chip_at(step):
        return lax.rem(place.chip + step, chips)

    def spread(k, step):
        there = (place.expert, chip_at(step) * 2 + place.core)
        return [
            remote(piece(total, i, k), piece(total, i, k), sent_d.at[step - 1, k, i], came_d.at[k, i], there)
            for i in range(2)
        ]

    def cross(k):
        return [
            remote(piece(total, i, k), piece(total, i, k), sent_o.at[k, i], came_o.at[k, i], partner)
            for i in range(2)
        ]

    def hand_out(k):
        @pl.when((place.core == root_core) & (place.chip != root_chip))
        def _():
            for c in spread(k, 1):
                c.wait_recv()
            go(cross(k))

        @pl.when(place.core != root_core)
        def _():
            for c in cross(k):
                c.wait_recv()

    small_sums = [
        remote(small, small_rows.at[row], sent_s.at[0], came_s.at[row], (root * place.width + lax.rem(place.expert, place.width), place.shard))
    ]
    pl.when(row != root)(lambda: go(small_sums))
    head = jnp.where(row < chips, 2 * row, 2 * (rightmost - row) + 1)

    def small_from(other):
        return remote(small, small_rows.at[other], sent_s.at[0], came_s.at[other], partner)

    def small_out_to(step):
        there = (place.expert, lax.rem(place.shard + step, shards))
        return remote(small_out, small_out, sent_s.at[step], came_s.at[shards], there)

    def small_ends():
        @pl.when(row == root)
        def _():
            small_rows[row] = small[...]
            for step in range(1, shards):
                small_from(lax.rem(row + step, shards)).wait_recv()
            value = small_rows[0].astype(F32)
            for r in range(1, shards):
                value += small_rows[r].astype(F32)
            small_out[...] = value.astype(BF16)
            go([small_out_to(step) for step in range(1, shards)])

    def small_done():
        pl.when(row != root)(lambda: small_sums[0].wait_send())
        pl.when(place.shard != head)(lambda: small_out_to(1).wait_recv())

        @pl.when(row == root)
        def _():
            for step in range(1, shards):
                small_out_to(step).wait_send()

    lag = 2 * (shards - 1) + 2 - begin
    every = max(parts - begin + 2 * (shards - 1), parts + lag)
    emitted = []

    def one_step(step):
        chain(step)
        if isinstance(step, int):
            if lag <= step < parts + lag:
                hand_out(step - lag)
        else:
            pl.when((step >= lag) & (step < parts + lag))(lambda: hand_out(step - lag))

    def advance(count):
        for _ in range(count):
            if len(emitted) < every:
                emitted.append(len(emitted))
                one_step(emitted[-1])

    @pl.when(row == root)
    def _():
        for k in range(begin):
            add(k, total, [mine])
            give(k)

    advance(4)
    for c in swap_b:
        c.wait()
    swap_m = place.swap(0, made.at[0], made_a, sent_m.at[0], came_m.at[0])
    swap_m += place.swap(1, made.at[1], made_b, sent_m.at[1], came_m.at[1])
    go(swap_m)

    gain, shift = vecs[0:2], vecs[2:4]
    w_in, w_out = full.at[:, : 3 * width], full.at[:, 3 * width :]
    back_two = jnp.zeros((tokens, width), F32)
    for j in range(experts):
        back_two += mm(taken(col, j, slots), back_in[j // many][j % many])
    unit, inverse = normalize(middle[...])
    vec[1:2, :] = jnp.sum(back_two * unit, axis=0, keepdims=True)
    vec[3:4, :] = jnp.sum(back_two, axis=0, keepdims=True)
    back_middle = cot[...].astype(F32) + normalize_back(back_two, unit, inverse, gain[1:2, :])
    d_x[...] = back_middle
    branch = back_middle.astype(BF16)
    vec[6:7, :] = jnp.sum(branch.astype(F32), axis=0, keepdims=True)
    grads[:, 3 * width :] = tm(context[...], branch).astype(BF16)
    d_context[...] = mt(branch, w_out[...]).astype(BF16)
    valid = lax.broadcasted_iota(jnp.int32, (lines, lines), 0) < real
    half = lax.broadcasted_iota(jnp.int32, (lines, SLAB), 1) < HEAD
    scale = HEAD**-0.5
    vec[4:6, :] = jnp.zeros((2, width), F32)
    advance(1)
    begun = len(emitted)

    def one_image(i, carry):
        rows = pl.ds(pl.multiple_of(i * lines, 16), lines)
        for s in range(width // SLAB):
            cols = [slice(a * width + s * SLAB, a * width + (s + 1) * SLAB) for a in range(3)]
            q, k, v = (qkv[rows, c] for c in cols)
            given = d_context[rows, cols[0]]
            heads = []
            for h in range(2):
                keep = half if h == 0 else ~half
                zero = jnp.zeros_like(k)
                scores = mt(jnp.where(keep, k, zero), q) * scale
                scores = jnp.where(valid, scores, -1e30)
                powers = jnp.exp(scores - jnp.max(scores, axis=0, keepdims=True))
                soft = powers / jnp.sum(powers, axis=0, keepdims=True)
                back_soft = mt(jnp.where(keep, v, zero), given)
                shared = jnp.sum(back_soft * soft, axis=0, keepdims=True)
                back_scores = (soft * (back_soft - shared)).astype(BF16)
                heads.append((tm(back_scores, k), mm(back_scores, q), mm(soft.astype(BF16), given)))
            both = [jnp.where(half, a, b) for a, b in zip(*heads)]
            both = [both[0] * scale, both[1] * scale, both[2]]
            vec[4:5, cols[0]] += jnp.sum(both[0], axis=0, keepdims=True)
            vec[5:6, cols[0]] += jnp.sum(both[2], axis=0, keepdims=True)
            for c, grad in zip(cols, both):
                d_qkv[rows, c] = grad.astype(BF16)

        pl.when(i < every - begun)(lambda: one_step(i + begun))
        return carry

    lax.fori_loop(0, images, one_image, 0)
    emitted.extend(range(begun, min(begun + images, every)))
    unit, inverse = normalize(x[...].astype(F32))
    normed = (unit * gain[0:1, :] + shift[0:1, :]).astype(BF16)
    grads[:, : 3 * width] = tm(normed, d_qkv[...]).astype(BF16)

    share = width // shards
    halves = [
        remote(
            grads.at[pl.ds(pl.multiple_of((2 * c + 1 - place.core) * share, 16), share)], from_core.at[c],
            sent_1.at[c], came_1.at[c], partner,
        )
        for c in range(chips)
    ]
    go(halves)
    back_one = mt(d_qkv[...], w_in[...])
    vec[0:1, :] = jnp.sum(back_one * unit, axis=0, keepdims=True)
    vec[2:3, :] = jnp.sum(back_one, axis=0, keepdims=True)
    d_x[...] += normalize_back(back_one, unit, inverse, gain[0:1, :])
    advance(1)
    for c in range(chips):
        halves[c].wait_recv()
        block = pl.ds(pl.multiple_of((2 * c + place.core) * share, 16), share)
        from_core[c] = (from_core[c].astype(F32) + grads[block, :].astype(F32)).astype(BF16)
    quarters = [
        remote(
            from_core.at[chip_at(step)], from_chip.at[place.chip], sent_2.at[step], came_2.at[step],
            (place.expert, chip_at(step) * 2 + place.core),
        )
        for step in range(1, chips)
    ]
    go(quarters)
    advance(1)

    for c in swap_m:
        c.wait()
    upstream = cot[...].astype(F32)
    stream = middle[...]

    def gathered(r):
        found = jnp.zeros((tokens, width), F32)
        for j in range(experts):
            slot = jnp.where(both[:, r : r + 1] == place.expert_at(j).astype(F32) + 1.0, col[:, j : j + 1], -1.0)
            found += mm(taken(slot, 0, slots), made_in[j // many][j % many])
        d_gates[:, r : r + 1] = jnp.sum(found * upstream, axis=1, keepdims=True)
        return found * both[:, TOP + r : TOP + r + 1]

    stream += gathered(0)
    advance(1)
    for c in quarters:
        c.wait_recv()
    whole = from_core[place.chip].astype(F32)
    for step in range(1, chips):
        whole += from_chip[chip_at(step)].astype(F32)
    whole = whole.astype(BF16)
    down_n = share // 16
    across_n = experts // down_n
    wide = cut.shape[2]
    for r in range(down_n):
        for c in range(across_n):
            cut[r * across_n + c] = whole[r * 16 : (r + 1) * 16, c * wide : (c + 1) * wide]

    def other(step):
        return lax.rem(place.expert + step, experts)

    pieces = [
        remote(
            cut.at[other(step)], from_all.at[place.expert], sent_3.at[step], came_3.at[step],
            (other(step), place.shard),
        )
        for step in range(1, experts)
    ]
    go(pieces)
    stream += gathered(1)
    advance(1)
    out[...] = stream.astype(BF16)
    index = lax.broadcasted_iota(jnp.int32, (tokens, 1), 0)
    counts = jnp.where(lax.rem(index, lines) < real, 1.0, 0.0)
    vec[7:8, :] = jnp.zeros((1, width), F32)
    vec[8:10, :] = squares[...]
    vec[10:11, :] = jnp.sum(stream * stream * counts, axis=0, keepdims=True)
    vec[11:16, :] = jnp.zeros((5, width), F32)
    vec_group[place.member] = vec[...]
    lists = [
        remote(vec, vec_group.at[place.member], sent_5.at[step], came_5.at[step], place.peer(step)[1])
        for step in range(1, experts)
    ]
    go(lists)
    for c in pieces:
        c.wait_recv()
    whole = cut[place.expert].astype(F32)
    for step in range(1, experts):
        whole += from_all[other(step)].astype(F32)
    shares_out[place.expert] = whole.astype(BF16)
    spreads = [
        remote(
            shares_out.at[place.expert], shares_out.at[place.expert], sent_4.at[step], came_4.at[step],
            (other(step), place.shard),
        )
        for step in range(1, experts)
    ]
    go(spreads)
    for c in lists:
        c.wait_recv()
    whole = vec_group[0]
    for j in range(1, experts):
        whole += vec_group[j]
    vec_rows[row] = whole
    downs = [
        remote(
            vec_rows.at[row], vec_rows.at[row], sent_6.at[step], came_6.at[step],
            (lax.rem(place.expert + step * place.width, experts), place.shard),
        )
        for step in range(1, shards)
    ]
    go(downs)
    small_ends()
    advance(every)
    small_done()
    for c in downs:
        c.wait_recv()
    whole = vec_rows[0]
    for j in range(1, shards):
        whole += vec_rows[j]
    vec_out[...] = whole
    for c in spreads:
        c.wait_recv()
    for c in halves + quarters + pieces + spreads + lists + downs:
        c.wait_send()
    for k in range(parts - 2, parts):
        pl.when(row != root)(lambda k=k: left_free(k))

    def sends(k, carry):
        @pl.when(row == root)
        def _():
            for step in range(1, chips):
                for c in spread(k, step):
                    c.wait_send()

        @pl.when(place.core == root_core)
        def _():
            for c in cross(k):
                c.wait_send()

        return carry

    lax.fori_loop(0, parts, sends, 0)


def outputs_kernel(entries, up, down, small, shares, vec, up_f, down_f, in_f, out_f, gain, shift, bias, hidden, last, sizes):
    up_f[0] = up[...].astype(F32)
    down_f[0] = down[...].astype(F32)
    width = down.shape[1]
    experts, _, wide = shares.shape
    across = 4 * width // wide
    for j in range(experts):
        rows = slice(j // across * 16, j // across * 16 + 16)
        start = j % across * wide
        block = shares[j].astype(F32)
        if start + wide <= 3 * width:
            in_f[rows, start : start + wide] = block
        elif start >= 3 * width:
            out_f[rows, start - 3 * width : start - 3 * width + wide] = block
        else:
            in_f[rows, start:] = block[:, : 3 * width - start]
            out_f[rows, :] = block[:, 3 * width - start :]
    shard, shards = lax.axis_index("shard"), lax.axis_size("shard")
    share = width // shards
    mine = jnp.zeros((8, share), F32)
    for s in range(shards):
        mine = jnp.where(shard == s, vec[0:8, s * share : (s + 1) * share], mine)
    gain[...] = mine[0:2]
    shift[...] = mine[2:4]
    bias[...] = mine[4:7]
    for i in range(hidden.shape[1] // width):
        hidden[:, i * width : (i + 1) * width] = small[i : i + 1, :].astype(F32)
    i = hidden.shape[1] // width
    last[...] = small[i : i + 1, :].astype(F32)
    sizes[...] = jnp.sqrt(jnp.sum(vec[8:16, :], axis=1, keepdims=True) / entries)


def local(
    images, attention_in, attention_out, layer_gain, layer_shift, attention_bias, expert_up, hidden_bias,
    expert_down, expert_bias, routes, gates, cotangent,
):
    count, real, width = images.shape
    lines = up_to(real, 16)
    tokens = count * lines
    experts = lax.axis_size("expert")
    shards = lax.axis_size("shard")
    slots = up_to(max(2, 4 * count * real // experts), 16)
    hidden_units = expert_up.shape[2]

    def padded(values, fill=0):
        wide = jnp.pad(values, ((0, 0), (0, lines - real), (0, 0)), constant_values=fill)
        return wide.reshape(tokens, values.shape[2])

    mats = jnp.concatenate([attention_in, attention_out], axis=1)
    vectors = jnp.concatenate([layer_gain, layer_shift, attention_bias], axis=0).astype(F32)
    vectors = lax.dynamic_update_slice(
        jnp.zeros((8, width), F32), vectors, (0, lax.axis_index("shard") * vectors.shape[1])
    )
    biases = jnp.concatenate([hidden_bias, expert_bias], axis=1).astype(F32)

    x, cot = padded(images), padded(cotangent)
    both = padded(jnp.concatenate([routes.astype(F32) + 1.0, gates], axis=2))
    parts, chunks = 16, 4
    many = experts // 2
    half_block = (many, slots, width)
    dma = pltpu.SemaphoreType.DMA
    vmem = lambda *shape: pltpu.VMEM(shape, BF16)
    wide_vmem = lambda *shape: pltpu.VMEM(shape, F32)
    back_a, back, made, d_up, d_down, d_small, middle, qkv, context, squares, full, vecs, col = call(
        functools.partial(forward_kernel, count, real, parts, chunks),
        [
            (half_block, BF16), ((2, *half_block), BF16), ((2, *half_block), BF16),
            ((width, hidden_units), BF16), ((hidden_units, width), BF16), ((16, width), BF16), ((tokens, width), F32),
            ((tokens, 3 * width), BF16), ((tokens, width), BF16), ((2, width), F32), ((width, 4 * width), BF16),
            ((8, width), F32), ((tokens, up_to(experts, 128)), F32),
        ],
        [
            x, cot, both, both.T, mats, vectors, expert_up[0], expert_down[0], biases,
        ],
        [
            vmem(2, *half_block), vmem(2, *half_block),
            vmem(width, hidden_units), vmem(hidden_units, width), wide_vmem(1, hidden_units + width),
            wide_vmem(2, *half_block), wide_vmem(2, *half_block),
            wide_vmem(chunks - 1, width, hidden_units // chunks), wide_vmem(chunks - 1, hidden_units // chunks, width), wide_vmem(1, hidden_units + width),
            wide_vmem(up_to(experts, 8), tokens), wide_vmem(shards, 8, width),
            dma((2, many)), dma((2, many)), dma((2, many)), dma((2, many)),
            dma((shards,)), dma((shards,)), dma((shards,)), dma((shards,)),
            dma((3, parts, 3)), dma((parts, 3)),
            dma((many,)), dma((many,)),
        ],
        outside=(6, 7, 8),
        collective=0,
    )

    share = width // shards
    across = experts // (share // 16)
    wide = 4 * width // across
    d_x, out, d_gates, up_total, down_total, small, owned, vector_sums = call(
        functools.partial(finish_kernel, count, real, parts, 0),
        [
            ((tokens, width), F32), ((tokens, width), BF16), ((tokens, TOP), F32), (d_up.shape, BF16),
            (d_down.shape, BF16), (d_small.shape, BF16), ((experts, 16, wide), BF16), ((16, width), F32),
        ],
        [
            back, made, back_a, d_up, d_down, d_small, x, cot, full, vecs, qkv, context, middle, col,
            both, squares,
        ],
        [
            vmem(*half_block), vmem(*half_block), vmem(*half_block), vmem(*d_up.shape), vmem(*d_down.shape),
            vmem(*d_up.shape), vmem(*d_down.shape), vmem(shards, *d_small.shape), vmem(tokens, 3 * width), vmem(tokens, width), vmem(width, 4 * width),
            pltpu.VMEM((16, width), F32), vmem(shards // 2, share, 4 * width), vmem(shards // 2, share, 4 * width),
            vmem(experts, 16, wide), vmem(experts, 16, wide), pltpu.VMEM((experts, 16, width), F32),
            pltpu.VMEM((shards, 16, width), F32),
            dma((many,)), dma((many,)), dma((2, many)), dma((2, many)),
            dma((shards,)), dma((shards + 1,)), dma((parts, 2)), dma((parts, 2)), dma((parts, 2)),
            dma((shards // 2, parts, 2)), dma((parts, 2)), dma((parts, 2)), dma((parts, 2)),
            dma((shards,)), dma((shards,)), dma((shards,)), dma((shards,)),
            dma((experts,)), dma((experts,)), dma((experts,)), dma((experts,)),
            dma((experts,)), dma((experts,)), dma((shards,)), dma((shards,)),
        ],
        outside=(0, 1),
        collective=1,
    )
    entries = float(count * real * width * experts * shards)
    up_f, down_f, in_f, out_f, d_gain, d_shift, d_bias, d_hidden, d_last, sizes = call(
        functools.partial(outputs_kernel, entries),
        [
            ((1, width, hidden_units), F32), ((1, hidden_units, width), F32), ((share, 3 * width), F32),
            ((share, width), F32), ((2, share), F32), ((2, share), F32), ((3, share), F32),
            ((1, hidden_units), F32), ((1, width), F32), ((8, 1), F32),
        ],
        [up_total, down_total, small, owned, vector_sums],
    )

    def cut(values):
        return values.reshape(count, lines, values.shape[1])[:, :real]

    return (
        cut(out),
        cut(d_x),
        in_f,
        out_f,
        d_gain,
        d_shift,
        d_bias,
        up_f,
        d_hidden,
        down_f,
        d_last,
        cut(d_gates),
        sizes[:3, 0],
    )


def solution(mesh):
    every = P(("expert", "shard"), None, None)
    return jax.shard_map(
        local,
        mesh=mesh,
        in_specs=(
            every, P("shard", None), P("shard", None), P(None, "shard"), P(None, "shard"), P(None, "shard"),
            P("expert", None, None), P("expert", None), P("expert", None, None), P("expert", None),
            every, every, every,
        ),
        out_specs=(
            every, every, P("shard", None), P("shard", None), P(None, "shard"), P(None, "shard"),
            P(None, "shard"), P("expert", None, None), P("expert", None), P("expert", None, None),
            P("expert", None), every, P(),
        ),
        check_vma=False,
    )
```

```python
import functools

import jax
import jax.numpy as jnp
from jax import lax
from jax.experimental import pallas as pl
from jax.experimental.pallas import tpu as pltpu
from jax.sharding import PartitionSpec as P

HEAD = 64
SLAB = 2 * HEAD
TOP = 2
EPSILON = 1e-06
F32, BF16 = jnp.float32, jnp.bfloat16
VMEM_LIMIT = 60 * 1024 * 1024


def dot_of(contract):
    def run(left, right):
        return lax.dot_general(
            left, right, (contract, ((), ())), preferred_element_type=F32
        )

    return run


mm = dot_of(((1,), (0,)))
mt = dot_of(((1,), (1,)))
tm = dot_of(((0,), (0,)))


def up_to(value, step):
    return -(-value // step) * step


def normalize(values):
    centre = values - jnp.mean(values, axis=-1, keepdims=True)
    inverse = lax.rsqrt(jnp.mean(centre * centre, axis=-1, keepdims=True) + EPSILON)
    return centre * inverse, inverse


def normalize_back(incoming, unit, inverse, weight):
    scaled = incoming * weight
    first_mean = jnp.mean(scaled, axis=-1, keepdims=True)
    second_mean = jnp.mean(scaled * unit, axis=-1, keepdims=True)
    return inverse * (scaled - first_mean - unit * second_mean)


def gelu_pair(value):
    size = jnp.abs(value)
    t = 1.0 / (1.0 + (0.3275911 * 0.7071067811865476) * size)
    bell = jnp.exp(-0.5 * value * value)
    poly = 0.5 * 1.061405429
    for c in (-1.453152027, 1.421413741, -0.284496736, 0.254829592):
        poly = poly * t + 0.5 * c
    tail = poly * t * bell
    normal = jnp.where(value >= 0, 1.0 - tail, tail)
    return value * normal, normal + value * (bell * 0.3989422804014327)


def call(body, outs, args, scratch=(), outside=(), collective=None):
    where = [
        pl.BlockSpec(memory_space=pl.ANY if i in outside else pltpu.VMEM) for i in range(len(args) + len(outs))
    ]
    return pl.pallas_call(
        body,
        out_shape=[jax.ShapeDtypeStruct(s, d) for s, d in outs],
        in_specs=where[: len(args)],
        out_specs=where[len(args) :],
        scratch_shapes=list(scratch),
        compiler_params=pltpu.CompilerParams(
            vmem_limit_bytes=VMEM_LIMIT, collective_id=collective, has_side_effects=collective is not None
        ),
    )(*args)


def axes():
    return (
        lax.axis_index("expert"), lax.axis_index("shard"), lax.axis_size("expert"), lax.axis_size("shard")
    )


class Place:
    def __init__(self):
        self.expert, self.shard, self.experts, self.shards = axes()
        self.width = self.experts // self.shards
        self.row = lax.div(self.expert, self.width)
        self.member = lax.rem(self.expert, self.width) * self.shards + self.shard
        self.core = lax.rem(self.shard, 2)
        self.chip = lax.div(self.shard, 2)
        self.root = self.chip * (1 - self.core) + (self.shards - 1 - self.chip) * self.core

    def peer(self, step):
        other = lax.rem(self.member + step, self.experts)
        return other, (self.row * self.width + lax.div(other, self.shards), lax.rem(other, self.shards))

    def expert_at(self, number):
        many = self.experts // 2
        chips = self.shards // 2
        half, spot = divmod(number, many)
        core = self.core * (1 - half) + (1 - self.core) * half
        chip = spot % chips
        return (chip * (1 - core) + (self.shards - 1 - chip) * core) * self.width + spot // chips

    def expert_near(self, spot):
        chips = self.shards // 2
        chip = lax.rem(spot, chips)
        row = chip * (1 - self.core) + (self.shards - 1 - chip) * self.core
        return row * self.width + lax.div(spot, chips)

    def expert_at_all(self, shape, axis):
        at = lax.broadcasted_iota(jnp.int32, shape, axis)
        experts = jnp.full(shape, -9.0, F32)
        for number in range(self.experts):
            experts = jnp.where(at == number, self.expert_at(number).astype(F32), experts)
        return experts

    def swap(self, half, send, recv, sent, came):
        many = self.experts // 2
        chips = self.shards // 2
        spot = lax.div(self.member, 2)
        core = self.core if half == 0 else 1 - self.core
        copies = []
        if half == 0:
            copies.append(pltpu.make_async_copy(send.at[spot], recv.at[spot], sent.at[0]))
        for step in range(1 - half, many):
            other = lax.rem(spot + step, many)
            device = (self.row * self.width + lax.div(other, chips), lax.rem(other, chips) * 2 + core)
            copies.append(remote(send.at[other], recv.at[spot], sent.at[step], came.at[step], device))
        return copies

    def along(self, step):
        return (self.expert + step * self.width, self.shard)

    def greet(self):
        barrier = pltpu.get_barrier_semaphore()
        for step in range(1, self.experts):
            tell(barrier, self.peer(step)[1])
        pl.when(self.row > 0)(lambda: tell(barrier, self.along(-1)))
        pl.when(self.row < self.shards - 1)(lambda: tell(barrier, self.along(1)))
        ends = jnp.where(self.row > 0, 1, 0) + jnp.where(self.row < self.shards - 1, 1, 0)
        pl.semaphore_wait(barrier, self.experts - 1 + ends)


    def greet_all(self):
        barrier = pltpu.get_barrier_semaphore()
        for step in range(1, self.experts):
            tell(barrier, self.peer(step)[1])
        for rows in range(1, self.shards):
            for at in range(self.width):
                line = lax.rem(self.row + rows, self.shards) * self.width + at
                tell(barrier, (line, self.shard))
        pl.semaphore_wait(barrier, self.experts - 1 + (self.shards - 1) * self.width)


def tell(semaphore, device):
    pl.semaphore_signal(semaphore, inc=1, device_id=device, device_id_type=pl.DeviceIdType.MESH)


def remote(src, dst, sent, came, device):
    return pltpu.make_async_remote_copy(
        src_ref=src, dst_ref=dst, send_sem=sent, recv_sem=came, device_id=device,
        device_id_type=pl.DeviceIdType.MESH,
    )


def placed(place, col_in, row_in, col_shape, row_shape):
    tokens = col_in.shape[0]
    down = lax.broadcasted_iota(jnp.int32, (tokens, tokens), 0)
    across = lax.broadcasted_iota(jnp.int32, (tokens, tokens), 1)
    lanes = place.expert_at_all(col_shape, 1)
    named = (col_in[:, 0:1] == lanes) | (col_in[:, 1:2] == lanes)
    before = (across < down).astype(F32).astype(BF16)
    ranks = mm(before, named.astype(F32).astype(BF16))
    col = jnp.where(named, ranks, -1.0)
    lines = place.expert_at_all(row_shape, 0)
    named = (row_in[0:1, :] == lines) | (row_in[1:2, :] == lines)
    before = (down < across).astype(F32).astype(BF16)
    ranks = mm(named.astype(F32).astype(BF16), before)
    return col, jnp.where(named, ranks, -1.0)


def chosen(row_ref, expert, slots):
    tokens = row_ref.shape[1]
    index = lax.broadcasted_iota(jnp.int32, (slots, tokens), 0).astype(F32)
    return jnp.where(index == row_ref[pl.ds(expert, 1), :], 1.0, 0.0).astype(BF16)


def taken(col, expert, slots):
    index = lax.broadcasted_iota(jnp.int32, (col.shape[0], slots), 1).astype(F32)
    return jnp.where(index == col[:, expert : expert + 1], 1.0, 0.0).astype(BF16)


def expert_step(x, g, up, down, bias):
    hidden = mm(x, up) + bias
    back_active = mt(g, down)
    active, slope = gelu_pair(hidden)
    active = active.astype(BF16)
    back_hidden = back_active * slope
    sums = jnp.sum(back_hidden, axis=0, keepdims=True)
    back_hidden = back_hidden.astype(BF16)
    return mm(active, down), mt(back_hidden, up), tm(x, back_hidden), tm(active, g), sums


def saving_kernel(count, late, early, options, *refs):
    operands, refs = refs[:count], refs[count:]
    outs, saved, refs = refs[:late], refs[late : late + early], refs[late + early :]
    kept, stores, refs = refs[:early], refs[early], refs[early + 1 :]
    copies = [pltpu.make_async_copy(v, h, stores.at[i]) for i, (v, h) in enumerate(zip(kept, saved))]
    forward_kernel(*options, copies, *operands, *outs, *kept, *refs)


def forward_kernel(
    images, real, parts, chunks, stores,
    x, cot, both, both_row, mats, vecs, up, down, biases,
    back_a, grads_in, rows_in, d_up, d_down, d_small, middle_out, qkv, context, squares, full, rows_of, col,
    send_g, send_r, up_in, down_in, biases_in, made_sum, back_sum, sum_up, sum_down, sum_small,
    row, vec_all,
    sent_g, came_g, sent_r, came_r, sent_p, came_p, sent_v, came_v, sent_w, came_w, sent_b, came_b,
):
    place = Place()
    tokens, width = x.shape
    routes, routes_row = both[:, 0:TOP] - 1.0, both_row[0:TOP, :] - 1.0
    gates = both[:, TOP:]
    lines = tokens // images
    _, many, slots, _ = send_r.shape
    shards = place.shards
    chips_n = shards // 2
    place.greet()

    def go(copies):
        for c in copies:
            c.start()

    share = mats.shape[0]
    mine = pl.ds(pl.multiple_of(place.shard * share, 16), share)
    partner = (place.expert, place.shard + 1 - 2 * place.core)
    own = [
        pltpu.make_async_copy(mats, full.at[mine], sent_p.at[0]),
        pltpu.make_async_copy(vecs, vec_all.at[place.shard], sent_v.at[0]),
    ]
    go(own)
    chips = []
    for step in range(1, chips_n):
        there = (place.expert, lax.rem(place.chip + step, chips_n) * 2 + place.core)
        chips.append(remote(mats, full.at[mine], sent_p.at[step], came_p.at[step], there))
        chips.append(remote(vecs, vec_all.at[place.shard], sent_v.at[step], came_v.at[step], there))
    go(chips)

    held, landed = (up, down, biases), (up_in, down_in, biases_in)
    rightmost = shards - 1
    flight = 4
    units = up.shape[1]
    thin = units // parts

    hops = jnp.abs(place.row - place.root)
    sides = ((-1, place.row > 0), (1, place.row < rightmost))

    def part_of(ref, i, k):
        span = pl.ds(k * thin, thin) if isinstance(k, int) else pl.ds(pl.multiple_of(k * thin, 128), thin)
        return ref.at[:, span] if i == 0 else ref.at[span, :]

    def matrices(k, source, way):
        return [
            remote(
                part_of(source[i], i, k), part_of(landed[i], i, k), sent_w.at[(way + 1) // 2, k, i],
                came_w.at[k, i], place.along(way),
            )
            for i in range(2)
        ]

    def bias_copy(source, way):
        return remote(source[2], landed[2], sent_w.at[(way + 1) // 2, 0, 2], came_w.at[0, 2], place.along(way))

    local = [pltpu.make_async_copy(h, t, sent_w.at[2, 0, i]) for i, (h, t) in enumerate(zip(held, landed))]

    def onward(way):
        return (place.row > 0) & (place.row < place.root) if way < 0 else (place.row < rightmost) & (place.row > place.root)

    def owner_part(k):
        for way, more in sides:

            @pl.when((place.row == place.root) & more)
            def _(way=way):
                if not isinstance(k, int) or k >= flight:
                    for c in matrices(k - flight, landed, way):
                        c.wait_send()
                go(matrices(k, held, way))

    def pass_part(k):
        for c in matrices(k, landed, 1):
            c.wait_recv()
        for way in (-1, 1):

            @pl.when(onward(way))
            def _(way=way):
                @pl.when(k >= flight)
                def _():
                    for c in matrices(k - flight, landed, way):
                        c.wait_send()

                go(matrices(k, landed, way))

    steps_done, sure = [0], [0]

    def matrix_step(p, owner=True):
        if owner:
            pl.when(p + flight < parts)(lambda: owner_part(p + flight)) if not isinstance(p, int) else (
                owner_part(p + flight) if p + flight < parts else None
            )
        k = p - 3 * (hops - 1)
        pl.when((hops > 0) & (k >= sure[0]) & (k < parts))(lambda: pass_part(k))

    def move_on(count, owner=True):
        for _ in range(count):
            matrix_step(steps_done[0], owner)
            steps_done[0] += 1

    def ensure(count):
        for k in range(sure[0], count):
            pl.when((hops > 0) & (k >= steps_done[0] - 3 * (hops - 1)))(lambda k=k: pass_part(k))
        sure[0] = max(sure[0], count)

    pl.when(place.row == place.root)(lambda: go(local))
    for way, more in sides:
        pl.when((place.row == place.root) & more)(lambda way=way: bias_copy(held, way).start())
    for k in range(flight):
        owner_part(k)

    col_all, row_all = placed(place, routes, routes_row, col.shape, row.shape)
    col[...] = col_all
    row[...] = row_all
    upstream = cot[...].astype(F32)

    spot = lax.div(place.member, 2)

    def grads_for(half, i, e):
        gate = jnp.where(routes[:, 0:1] == e, gates[:, 0:1], 0.0) + jnp.where(
            routes[:, 1:2] == e, gates[:, 1:2], 0.0
        )
        scaled = (upstream * gate).astype(BF16)
        send_g[half, i] = mm(chosen(row, half * many + i, slots), scaled).astype(BF16)

    def swap_of(half, send, recv, sent, came):
        return place.swap(half, send.at[half], recv.at[half], sent.at[half], came.at[half])

    swap_ga = swap_of(0, send_g, grads_in, sent_g, came_g)
    for step in (*range(1, many), 0):
        i = lax.rem(spot + step, many)
        grads_for(0, i, place.expert_near(i).astype(F32))
        swap_ga[step].start()
    for i in range(many):
        grads_for(1, i, place.expert_at(many + i).astype(F32))

    over = []
    for step in range(chips_n):
        source = lax.rem(place.chip + step, chips_n) * 2 + place.core
        block = pl.ds(pl.multiple_of(source * share, 16), share)
        if step:
            back = chips_n - step
            chips[2 * back - 2].wait_recv()
            chips[2 * back - 1].wait_recv()
        else:
            own[0].wait()
            own[1].wait()
        at = chips_n + step
        over.append(remote(full.at[block], full.at[block], sent_p.at[at], came_p.at[at], partner))
        over.append(remote(vec_all.at[source], vec_all.at[source], sent_v.at[at], came_v.at[at], partner))
        go(over[-2:])
    for c in over:
        c.wait_recv()
    vectors = vec_all[0]
    for s in range(1, shards):
        vectors = vectors + vec_all[s]
    rows_of[...] = vectors
    gain, shift, bias = vectors[0:2], vectors[2:4], vectors[4:7]
    w_in, w_out = full.at[:, : 3 * width], full.at[:, 3 * width :]

    stream = x[...].astype(F32)
    unit, _ = normalize(stream)
    normed = (unit * gain[0:1, :] + shift[0:1, :]).astype(BF16)
    projected = mm(normed, w_in[...])
    qkv[:, :width] = (projected[:, :width] + bias[0:1, :]).astype(BF16)
    qkv[:, width : 2 * width] = projected[:, width : 2 * width].astype(BF16)
    qkv[:, 2 * width :] = (projected[:, 2 * width :] + bias[1:2, :]).astype(BF16)
    valid = lax.broadcasted_iota(jnp.int32, (lines, lines), 0) < real
    half_lanes = lax.broadcasted_iota(jnp.int32, (lines, SLAB), 1) < HEAD

    def one_image(i, carry):
        rows = pl.ds(pl.multiple_of(i * lines, 16), lines)
        for s in range(width // SLAB):
            q = qkv[rows, s * SLAB : (s + 1) * SLAB]
            k = qkv[rows, width + s * SLAB : width + (s + 1) * SLAB]
            v = qkv[rows, 2 * width + s * SLAB : 2 * width + (s + 1) * SLAB]
            heads = []
            for h in range(2):
                keep = half_lanes if h == 0 else ~half_lanes
                scores = mt(jnp.where(keep, k, jnp.zeros_like(k)), q) * (HEAD**-0.5)
                scores = jnp.where(valid, scores, -1e30)
                powers = jnp.exp(scores - jnp.max(scores, axis=0, keepdims=True))
                soft = powers / jnp.sum(powers, axis=0, keepdims=True)
                heads.append(tm(soft.astype(BF16), v))
            context[rows, s * SLAB : (s + 1) * SLAB] = jnp.where(half_lanes, heads[0], heads[1]).astype(BF16)

        @pl.when((i > 0) & (i <= flight))
        def _():
            owner_part(i + flight - 1)

        return carry

    lax.fori_loop(0, images, one_image, 0)
    started = min(images - 1, flight)
    pl.when(place.row != place.root)(lambda: bias_copy(landed, 1).wait_recv())
    for way, more in sides:
        pl.when(onward(way))(lambda way=way: bias_copy(landed, way).start())
    move_on(started, owner=False)
    middle = stream + mm(context[...], w_out[...]) + bias[2:3, :]
    middle_out[...] = middle
    unit, _ = normalize(middle)
    normed = (unit * gain[1:2, :] + shift[1:2, :]).astype(BF16)

    def tokens_for(half, i):
        send_r[half, i] = mm(chosen(row, half * many + i, slots), normed).astype(BF16)

    swap_ra = swap_of(0, send_r, rows_in, sent_r, came_r)
    for step in (*range(1, many), 0):
        i = lax.rem(spot + step, many)
        tokens_for(0, i)
        swap_ra[step].start()
    move_on(1)
    for i in range(many):
        tokens_for(1, i)
    index = lax.broadcasted_iota(jnp.int32, (tokens, 1), 0)
    counts = jnp.where(lax.rem(index, lines) < real, 1.0, 0.0)
    squares[0:1, :] = jnp.sum(stream * stream, axis=0, keepdims=True)
    squares[1:2, :] = jnp.sum(middle * middle * counts, axis=0, keepdims=True)
    go(stores)
    move_on(3)
    for c in swap_ga + swap_ra:
        c.wait()
    swap_gb = swap_of(1, send_g, grads_in, sent_g, came_g)
    swap_rb = swap_of(1, send_r, rows_in, sent_r, came_r)
    few = many // 2
    go(swap_gb[:few] + swap_rb[:few])
    move_on(1)

    wide = units // chunks
    each = parts // chunks
    pl.when(place.row == place.root)(lambda: [c.wait() for c in local] and None)

    def work(half, j, first=0, last=many, stride=0):
        base = steps_done[0]
        cols = slice(j * wide, (j + 1) * wide)
        if half == 0:
            sum_up[j % (chunks - 1)] = jnp.zeros(sum_up.shape[1:], F32)
            sum_down[j % (chunks - 1)] = jnp.zeros(sum_down.shape[1:], F32)
            sum_small[:, cols] = jnp.zeros((1, wide), F32)
            if j == 0:
                sum_small[:, units:] = jnp.zeros((1, width), F32)

        def block(step_at, carry):
            i = lax.rem(spot + many - step_at, many)
            rows, given = rows_in[half, i], grads_in[half, i]
            made, back, part_up, part_down, small = expert_step(
                rows, given, up_in[:, cols], down_in[cols, :], biases_in[:, cols]
            )
            sum_up[j % (chunks - 1)] += part_up
            sum_down[j % (chunks - 1)] += part_down
            sum_small[:, cols] += small
            if j == 0:
                made += biases_in[:, units:]
                sum_small[:, units:] += jnp.sum(given.astype(F32), axis=0, keepdims=True)
            else:
                made += made_sum[half, i]
                back += back_sum[half, i]
            if j < chunks - 1:
                made_sum[half, i] = made
                back_sum[half, i] = back
            else:
                rows_in[half, i] = made.astype(BF16)
                grads_in[half, i] = back.astype(BF16)
            if stride:
                at = lax.div(step_at - first, stride)
                pl.when(lax.rem(step_at - first, stride) == stride - 1)(lambda: matrix_step(base + at))
            return carry

        lax.fori_loop(first, last, block, 0)
        if stride:
            steps_done[0] += (last - first) // stride
        if half and last == many:
            d_up[:, cols] = sum_up[j % (chunks - 1)].astype(BF16)
            d_down[cols, :] = sum_down[j % (chunks - 1)].astype(BF16)

    for j in range(chunks - 1):
        ensure((j + 1) * each)
        work(0, j, 0, many, many // 2)
        if j == 0:
            go(swap_gb[few:] + swap_rb[few:])
    for c in swap_gb[:few] + swap_rb[:few]:
        c.wait()
    for j in range(chunks - 1):
        work(1, j, 0, few, few)
    for c in swap_gb[few:] + swap_rb[few:]:
        c.wait()
    for j in range(chunks - 1):
        work(1, j, few, many, few)
    while steps_done[0] + flight < parts:
        move_on(1)
    ensure(parts)
    work(0, chunks - 1)
    swap_b = place.swap(0, grads_in.at[0], back_a, sent_b, came_b)
    go(swap_b)
    work(1, chunks - 1)
    d_small[...] = jnp.zeros(d_small.shape, BF16)
    for i in range(units // width + 1):
        d_small[i : i + 1, :] = sum_small[:, i * width : (i + 1) * width].astype(BF16)

    for c in chips + over:
        c.wait_send()
    for way, more in sides:

        @pl.when(((place.row == place.root) & more) | onward(way))
        def _(way=way):
            bias_copy(landed, way).wait_send()
            for k in range(parts - flight, parts):
                for c in matrices(k, landed, way):
                    c.wait_send()

    for c in swap_b + stores:
        c.wait()


def loading_kernel(count, results, options, back, made, *refs):
    held, refs = refs[:count], refs[count:]
    outs, refs = refs[:results], refs[results:]
    landed, loads, refs = refs[:count], refs[count], refs[count + 1 :]
    copies = [pltpu.make_async_copy(h, v, loads.at[i]) for i, (h, v) in enumerate(zip(held, landed))]
    for c in copies:
        c.start()
    finish_kernel(*options, copies, back, made, *landed, *outs, *refs)


def finish_kernel(
    images, real, parts, begin, loads,
    back, made, back_a, up, down, small, x, cot, full, vecs, qkv, context, middle, col, both, squares,
    d_x, out, d_gates, up_out, down_out, small_out, shares_out, vec_out, via_up, via_down,
    back_b, made_a, made_b, up_l, down_l, up_r, down_r, small_rows, d_qkv, d_context, grads, vec, from_core, from_chip, cut, from_all,
    vec_group, vec_rows,
    sent_b, came_b, sent_m, came_m, sent_s, came_s, sent_c, came_l, came_r, sent_d, came_d, sent_o, came_o,
    sent_1, came_1, sent_2, came_2, sent_3, came_3, sent_4, came_4, sent_5, came_5, sent_6, came_6,
    sent_x, came_x, sent_y, came_y,
):
    place = Place()
    tokens, width = x.shape
    lines = tokens // images
    many, slots, _ = back_b.shape
    experts = 2 * many
    shards = place.shards
    chips = shards // 2
    back_in, made_in = (back_a, back_b), (made_a, made_b)
    place.greet_all()

    def go(copies):
        for c in copies:
            c.start()

    swap_b = place.swap(1, back.at[1], back_b, sent_b, came_b)
    go(swap_b)
    for c in loads:
        c.wait()

    rightmost = shards - 1
    row, root = place.row, place.root
    mine, total = (up, down), (up_out, down_out)
    left, right = (up_l, down_l), (up_r, down_r)
    thin = up.shape[1] // parts
    hops = jnp.where(row < root, row, rightmost - row)
    far = jnp.maximum(root, rightmost - root)

    def piece(refs, i, k):
        span = pl.ds(k * thin, thin) if isinstance(k, int) else pl.ds(pl.multiple_of(k * thin, 128), thin)
        return refs[i].at[:, span] if i == 0 else refs[i].at[span, :]

    def hop(k, source, target, came, way):
        return [
            remote(piece(source, i, k), piece(target, i, k), sent_c.at[k, i], came.at[k, i], place.along(way))
            for i in range(2)
        ]

    def add(k, target, terms):
        for i in range(2):
            value = piece(terms[0], i, k)[...].astype(F32)
            for t in terms[1:]:
                value += piece(t, i, k)[...].astype(F32)
            piece(target, i, k)[...] = value.astype(BF16)

    def arrived(k, buffer, came):
        for c in hop(k, buffer, buffer, came, 1):
            c.wait_recv()

    def left_free(k):
        for c in hop(k, left, left, came_l, 1):
            c.wait_send()

    def chain(step):
        k = begin + step - 2 * hops

        @pl.when((row != root) & (k >= begin) & (k < parts))
        def _():
            @pl.when((row > 0) & (row < root))
            def _():
                arrived(k, left, came_l)
                add(k, left, [mine, left])

            @pl.when((row < rightmost) & (row > root))
            def _():
                arrived(k, right, came_r)
                add(k, right, [mine, right])

            pl.when(k >= begin + 2)(lambda: left_free(k - 2))
            pl.when((row == 0) & (row < root))(lambda: go(hop(k, mine, left, came_l, 1)))
            pl.when((row == rightmost) & (row > root))(lambda: go(hop(k, mine, right, came_r, -1)))
            pl.when((row > 0) & (row < root))(lambda: go(hop(k, left, left, came_l, 1)))
            pl.when((row < rightmost) & (row > root))(lambda: go(hop(k, right, right, came_r, -1)))

        t = begin + step - 2 * far

        @pl.when((row == root) & (t >= begin) & (t < parts))
        def _():
            @pl.when(row > 0)
            def _():
                arrived(t, left, came_l)
                add(t, total, [mine, left])

            @pl.when(row == 0)
            def _():
                arrived(t, right, came_r)
                add(t, total, [mine, right])

            @pl.when((row > 0) & (row < rightmost))
            def _():
                arrived(t, right, came_r)
                add(t, total, [total, right])

            give(t)

    detour = chips == 2
    beside = 1 - 2 * lax.rem(row, 2)
    via = (via_up, via_down)

    def odd(k):
        return (lax.rem(k, 2) == 1) & (k < parts // 2)

    def aside(k):
        return [
            remote(piece(total, i, k), piece(via, i, k), sent_d.at[0, k, i], came_x.at[k, i], place.along(beside))
            for i in range(2)
        ]

    def over(k):
        there = (place.expert, chip_at(1) * 2 + place.core)
        return [
            remote(piece(via, i, k), piece(via, i, k), sent_x.at[k, i], came_y.at[k, i], there) for i in range(2)
        ]

    def home(k):
        return [
            remote(piece(via, i, k), piece(total, i, k), sent_y.at[k, i], came_d.at[k, i], place.along(beside))
            for i in range(2)
        ]

    def relay_over(k):
        @pl.when((place.core == root_core) & (place.chip != root_chip) & odd(k))
        def _():
            for c in aside(k):
                c.wait_recv()
            go(over(k))

    def relay_home(k):
        @pl.when((row == root) & odd(k))
        def _():
            for c in over(k):
                c.wait_recv()
            go(home(k))

    def give(k):
        if detour:
            pl.when(odd(k))(lambda: go(aside(k)))
            pl.when(~odd(k))(lambda: go(spread(k, 1)))
        else:
            for step in range(1, chips):
                go(spread(k, step))
        go(cross(k))

    root_core = jnp.where(row < chips, 0, 1)
    root_chip = jnp.where(row < chips, row, rightmost - row)
    partner = (place.expert, place.shard + 1 - 2 * place.core)

    def chip_at(step):
        return lax.rem(place.chip + step, chips)

    def spread(k, step):
        there = (place.expert, chip_at(step) * 2 + place.core)
        return [
            remote(piece(total, i, k), piece(total, i, k), sent_d.at[step - 1, k, i], came_d.at[k, i], there)
            for i in range(2)
        ]

    def cross(k):
        return [
            remote(piece(total, i, k), piece(total, i, k), sent_o.at[k, i], came_o.at[k, i], partner)
            for i in range(2)
        ]

    def hand_out(k):
        @pl.when((place.core == root_core) & (place.chip != root_chip))
        def _():
            for c in spread(k, 1):
                c.wait_recv()
            go(cross(k))

        @pl.when(place.core != root_core)
        def _():
            for c in cross(k):
                c.wait_recv()

    small_sums = [
        remote(small, small_rows.at[row], sent_s.at[0], came_s.at[row], (root * place.width + lax.rem(place.expert, place.width), place.shard))
    ]
    pl.when(row != root)(lambda: go(small_sums))
    head = jnp.where(row < chips, 2 * row, 2 * (rightmost - row) + 1)

    def small_from(other):
        return remote(small, small_rows.at[other], sent_s.at[0], came_s.at[other], partner)

    def small_out_to(step):
        there = (place.expert, lax.rem(place.shard + step, shards))
        return remote(small_out, small_out, sent_s.at[step], came_s.at[shards], there)

    def small_ends():
        @pl.when(row == root)
        def _():
            small_rows[row] = small[...]
            for step in range(1, shards):
                small_from(lax.rem(row + step, shards)).wait_recv()
            value = small_rows[0].astype(F32)
            for r in range(1, shards):
                value += small_rows[r].astype(F32)
            small_out[...] = value.astype(BF16)
            go([small_out_to(step) for step in range(1, shards)])

    def small_done():
        pl.when(row != root)(lambda: small_sums[0].wait_send())
        pl.when(place.shard != head)(lambda: small_out_to(1).wait_recv())

        @pl.when(row == root)
        def _():
            for step in range(1, shards):
                small_out_to(step).wait_send()

    lag = 2 * (shards - 1) + 2
    every = parts + lag + (4 if detour else 0)
    emitted = []

    def at_lag(step, behind, act):
        if isinstance(step, int):
            if behind <= step < parts + behind:
                act(step - behind)
        else:
            pl.when((step >= behind) & (step < parts + behind))(lambda: act(step - behind))

    def one_step(step):
        chain(step)
        if detour:
            at_lag(step, lag, relay_over)
            at_lag(step, lag + 2, relay_home)
        at_lag(step, lag + (4 if detour else 0), hand_out)

    def advance(count):
        for _ in range(count):
            if len(emitted) < every:
                emitted.append(len(emitted))
                one_step(emitted[-1])

    @pl.when(row == root)
    def _():
        for k in range(begin):
            add(k, total, [mine])
            give(k)

    advance(4)
    for c in swap_b:
        c.wait()
    swap_m = place.swap(0, made.at[0], made_a, sent_m.at[0], came_m.at[0])
    swap_m += place.swap(1, made.at[1], made_b, sent_m.at[1], came_m.at[1])
    go(swap_m)

    gain, shift = vecs[0:2], vecs[2:4]
    w_in, w_out = full.at[:, : 3 * width], full.at[:, 3 * width :]
    back_two = jnp.zeros((tokens, width), F32)
    for j in range(experts):
        back_two += mm(taken(col, j, slots), back_in[j // many][j % many])
    unit, inverse = normalize(middle[...])
    vec[1:2, :] = jnp.sum(back_two * unit, axis=0, keepdims=True)
    vec[3:4, :] = jnp.sum(back_two, axis=0, keepdims=True)
    back_middle = cot[...].astype(F32) + normalize_back(back_two, unit, inverse, gain[1:2, :])
    d_x[...] = back_middle
    branch = back_middle.astype(BF16)
    vec[6:7, :] = jnp.sum(branch.astype(F32), axis=0, keepdims=True)
    grads[:, 3 * width :] = tm(context[...], branch).astype(BF16)
    d_context[...] = mt(branch, w_out[...]).astype(BF16)
    valid = lax.broadcasted_iota(jnp.int32, (lines, lines), 0) < real
    half = lax.broadcasted_iota(jnp.int32, (lines, SLAB), 1) < HEAD
    scale = HEAD**-0.5
    vec[4:6, :] = jnp.zeros((2, width), F32)
    advance(1)
    begun = len(emitted)

    def one_image(i, carry):
        rows = pl.ds(pl.multiple_of(i * lines, 16), lines)
        for s in range(width // SLAB):
            cols = [slice(a * width + s * SLAB, a * width + (s + 1) * SLAB) for a in range(3)]
            q, k, v = (qkv[rows, c] for c in cols)
            given = d_context[rows, cols[0]]
            heads = []
            for h in range(2):
                keep = half if h == 0 else ~half
                zero = jnp.zeros_like(k)
                scores = mt(jnp.where(keep, k, zero), q) * scale
                scores = jnp.where(valid, scores, -1e30)
                powers = jnp.exp(scores - jnp.max(scores, axis=0, keepdims=True))
                soft = powers / jnp.sum(powers, axis=0, keepdims=True)
                back_soft = mt(jnp.where(keep, v, zero), given)
                shared = jnp.sum(back_soft * soft, axis=0, keepdims=True)
                back_scores = (soft * (back_soft - shared)).astype(BF16)
                heads.append((tm(back_scores, k), mm(back_scores, q), mm(soft.astype(BF16), given)))
            both = [jnp.where(half, a, b) for a, b in zip(*heads)]
            both = [both[0] * scale, both[1] * scale, both[2]]
            vec[4:5, cols[0]] += jnp.sum(both[0], axis=0, keepdims=True)
            vec[5:6, cols[0]] += jnp.sum(both[2], axis=0, keepdims=True)
            for c, grad in zip(cols, both):
                d_qkv[rows, c] = grad.astype(BF16)

        pl.when(i < every - begun)(lambda: one_step(i + begun))
        return carry

    lax.fori_loop(0, images, one_image, 0)
    emitted.extend(range(begun, min(begun + images, every)))
    unit, inverse = normalize(x[...].astype(F32))
    normed = (unit * gain[0:1, :] + shift[0:1, :]).astype(BF16)
    grads[:, : 3 * width] = tm(normed, d_qkv[...]).astype(BF16)

    share = width // shards
    halves = [
        remote(
            grads.at[pl.ds(pl.multiple_of((2 * c + 1 - place.core) * share, 16), share)], from_core.at[c],
            sent_1.at[c], came_1.at[c], partner,
        )
        for c in range(chips)
    ]
    go(halves)
    back_one = mt(d_qkv[...], w_in[...])
    vec[0:1, :] = jnp.sum(back_one * unit, axis=0, keepdims=True)
    vec[2:3, :] = jnp.sum(back_one, axis=0, keepdims=True)
    d_x[...] += normalize_back(back_one, unit, inverse, gain[0:1, :])
    advance(1)
    for c in range(chips):
        halves[c].wait_recv()
        block = pl.ds(pl.multiple_of((2 * c + place.core) * share, 16), share)
        from_core[c] = (from_core[c].astype(F32) + grads[block, :].astype(F32)).astype(BF16)
    quarters = [
        remote(
            from_core.at[chip_at(step)], from_chip.at[place.chip], sent_2.at[step], came_2.at[step],
            (place.expert, chip_at(step) * 2 + place.core),
        )
        for step in range(1, chips)
    ]
    go(quarters)
    advance(1)

    for c in swap_m:
        c.wait()
    upstream = cot[...].astype(F32)
    stream = middle[...]

    def gathered(r):
        found = jnp.zeros((tokens, width), F32)
        for j in range(experts):
            slot = jnp.where(both[:, r : r + 1] == place.expert_at(j).astype(F32) + 1.0, col[:, j : j + 1], -1.0)
            found += mm(taken(slot, 0, slots), made_in[j // many][j % many])
        d_gates[:, r : r + 1] = jnp.sum(found * upstream, axis=1, keepdims=True)
        return found * both[:, TOP + r : TOP + r + 1]

    stream += gathered(0)
    advance(1)
    for c in quarters:
        c.wait_recv()
    whole = from_core[place.chip].astype(F32)
    for step in range(1, chips):
        whole += from_chip[chip_at(step)].astype(F32)
    whole = whole.astype(BF16)
    down_n = share // 16
    across_n = experts // down_n
    wide = cut.shape[2]
    for r in range(down_n):
        for c in range(across_n):
            cut[r * across_n + c] = whole[r * 16 : (r + 1) * 16, c * wide : (c + 1) * wide]

    def other(step):
        return lax.rem(place.expert + step, experts)

    pieces = [
        remote(
            cut.at[other(step)], from_all.at[place.expert], sent_3.at[step], came_3.at[step],
            (other(step), place.shard),
        )
        for step in range(1, experts)
    ]
    go(pieces)
    stream += gathered(1)
    advance(1)
    out[...] = stream.astype(BF16)
    index = lax.broadcasted_iota(jnp.int32, (tokens, 1), 0)
    counts = jnp.where(lax.rem(index, lines) < real, 1.0, 0.0)
    vec[7:8, :] = jnp.zeros((1, width), F32)
    vec[8:10, :] = squares[...]
    vec[10:11, :] = jnp.sum(stream * stream * counts, axis=0, keepdims=True)
    vec[11:16, :] = jnp.zeros((5, width), F32)
    vec_group[place.member] = vec[...]
    lists = [
        remote(vec, vec_group.at[place.member], sent_5.at[step], came_5.at[step], place.peer(step)[1])
        for step in range(1, experts)
    ]
    go(lists)
    for c in pieces:
        c.wait_recv()
    whole = cut[place.expert].astype(F32)
    for step in range(1, experts):
        whole += from_all[other(step)].astype(F32)
    shares_out[place.expert] = whole.astype(BF16)
    spreads = [
        remote(
            shares_out.at[place.expert], shares_out.at[place.expert], sent_4.at[step], came_4.at[step],
            (other(step), place.shard),
        )
        for step in range(1, experts)
    ]
    go(spreads)
    for c in lists:
        c.wait_recv()
    whole = vec_group[0]
    for j in range(1, experts):
        whole += vec_group[j]
    vec_rows[row] = whole
    downs = [
        remote(
            vec_rows.at[row], vec_rows.at[row], sent_6.at[step], came_6.at[step],
            (lax.rem(place.expert + step * place.width, experts), place.shard),
        )
        for step in range(1, shards)
    ]
    go(downs)
    small_ends()
    advance(every)
    small_done()
    for c in downs:
        c.wait_recv()
    whole = vec_rows[0]
    for j in range(1, shards):
        whole += vec_rows[j]
    vec_out[...] = whole
    for c in spreads:
        c.wait_recv()
    for c in halves + quarters + pieces + spreads + lists + downs:
        c.wait_send()
    for k in range(parts - 2, parts):
        pl.when(row != root)(lambda k=k: left_free(k))

    def sends(k, carry):
        @pl.when(row == root)
        def _():
            for step in range(1, chips):
                for c in spread(k, step):
                    c.wait_send()

        @pl.when(place.core == root_core)
        def _():
            for c in cross(k):
                c.wait_send()

        if detour:

            @pl.when((place.core == root_core) & (place.chip != root_chip) & odd(k))
            def _():
                for c in over(k):
                    c.wait_send()

            @pl.when((row == root) & odd(k))
            def _():
                for c in home(k):
                    c.wait_send()

        return carry

    lax.fori_loop(0, parts, sends, 0)


def outputs_kernel(entries, up, down, small, shares, vec, up_f, down_f, in_f, out_f, gain, shift, bias, hidden, last, sizes):
    up_f[0] = up[...].astype(F32)
    down_f[0] = down[...].astype(F32)
    width = down.shape[1]
    experts, _, wide = shares.shape
    across = 4 * width // wide
    for j in range(experts):
        rows = slice(j // across * 16, j // across * 16 + 16)
        start = j % across * wide
        block = shares[j].astype(F32)
        if start + wide <= 3 * width:
            in_f[rows, start : start + wide] = block
        elif start >= 3 * width:
            out_f[rows, start - 3 * width : start - 3 * width + wide] = block
        else:
            in_f[rows, start:] = block[:, : 3 * width - start]
            out_f[rows, :] = block[:, 3 * width - start :]
    shard, shards = lax.axis_index("shard"), lax.axis_size("shard")
    share = width // shards
    mine = jnp.zeros((8, share), F32)
    for s in range(shards):
        mine = jnp.where(shard == s, vec[0:8, s * share : (s + 1) * share], mine)
    gain[...] = mine[0:2]
    shift[...] = mine[2:4]
    bias[...] = mine[4:7]
    for i in range(hidden.shape[1] // width):
        hidden[:, i * width : (i + 1) * width] = small[i : i + 1, :].astype(F32)
    i = hidden.shape[1] // width
    last[...] = small[i : i + 1, :].astype(F32)
    sizes[...] = jnp.sqrt(jnp.sum(vec[8:16, :], axis=1, keepdims=True) / entries)


def local(
    images, attention_in, attention_out, layer_gain, layer_shift, attention_bias, expert_up, hidden_bias,
    expert_down, expert_bias, routes, gates, cotangent,
):
    count, real, width = images.shape
    lines = up_to(real, 16)
    tokens = count * lines
    experts = lax.axis_size("expert")
    shards = lax.axis_size("shard")
    slots = up_to(max(2, 4 * count * real // experts), 16)
    hidden_units = expert_up.shape[2]

    def padded(values, fill=0):
        wide = jnp.pad(values, ((0, 0), (0, lines - real), (0, 0)), constant_values=fill)
        return wide.reshape(tokens, values.shape[2])

    mats = jnp.concatenate([attention_in, attention_out], axis=1)
    vectors = jnp.concatenate([layer_gain, layer_shift, attention_bias], axis=0).astype(F32)
    vectors = lax.dynamic_update_slice(
        jnp.zeros((8, width), F32), vectors, (0, lax.axis_index("shard") * vectors.shape[1])
    )
    biases = jnp.concatenate([hidden_bias, expert_bias], axis=1).astype(F32)

    x, cot = padded(images), padded(cotangent)
    both = padded(jnp.concatenate([routes.astype(F32) + 1.0, gates], axis=2))
    parts, chunks = 16, 4
    many = experts // 2
    half_block = (many, slots, width)
    dma = pltpu.SemaphoreType.DMA
    vmem = lambda *shape: pltpu.VMEM(shape, BF16)
    wide_vmem = lambda *shape: pltpu.VMEM(shape, F32)
    early = [
        ((tokens, width), F32), ((tokens, 3 * width), BF16), ((tokens, width), BF16), ((2, width), F32),
        ((width, 4 * width), BF16), ((8, width), F32), ((tokens, up_to(experts, 128)), F32),
    ]
    back_a, back, made, d_up, d_down, d_small, middle, qkv, context, squares, full, vecs, col = call(
        functools.partial(saving_kernel, 9, 6, len(early), (count, real, parts, chunks)),
        [
            (half_block, BF16), ((2, *half_block), BF16), ((2, *half_block), BF16),
            ((width, hidden_units), BF16), ((hidden_units, width), BF16), ((16, width), BF16), *early,
        ],
        [
            x, cot, both, both.T, mats, vectors, expert_up[0], expert_down[0], biases,
        ],
        [
            *[pltpu.VMEM(s, d) for s, d in early], dma((len(early),)),
            vmem(2, *half_block), vmem(2, *half_block),
            vmem(width, hidden_units), vmem(hidden_units, width), wide_vmem(1, hidden_units + width),
            wide_vmem(2, *half_block), wide_vmem(2, *half_block),
            wide_vmem(chunks - 1, width, hidden_units // chunks), wide_vmem(chunks - 1, hidden_units // chunks, width), wide_vmem(1, hidden_units + width),
            wide_vmem(up_to(experts, 8), tokens), wide_vmem(shards, 8, width),
            dma((2, many)), dma((2, many)), dma((2, many)), dma((2, many)),
            dma((shards,)), dma((shards,)), dma((shards,)), dma((shards,)),
            dma((3, parts, 3)), dma((parts, 3)),
            dma((many,)), dma((many,)),
        ],
        outside=(6, 7, 8, *range(15, 15 + len(early))),
        collective=0,
    )

    share = width // shards
    across = experts // (share // 16)
    wide = 4 * width // across
    loaded = [
        back_a, d_up, d_down, d_small, x, cot, full, vecs, qkv, context, middle, col, both, squares,
    ]
    d_x, out, d_gates, up_total, down_total, small, owned, vector_sums, _, _ = call(
        functools.partial(loading_kernel, len(loaded), 10, (count, real, parts, 0)),
        [
            ((tokens, width), F32), ((tokens, width), BF16), ((tokens, TOP), F32), (d_up.shape, BF16),
            (d_down.shape, BF16), (d_small.shape, BF16), ((experts, 16, wide), BF16), ((16, width), F32),
            (d_up.shape, BF16), (d_down.shape, BF16),
        ],
        [back, made, *loaded],
        [
            *[pltpu.VMEM(v.shape, v.dtype) for v in loaded], dma((len(loaded),)),
            vmem(*half_block), vmem(*half_block), vmem(*half_block), vmem(*d_up.shape), vmem(*d_down.shape),
            vmem(*d_up.shape), vmem(*d_down.shape), vmem(shards, *d_small.shape), vmem(tokens, 3 * width), vmem(tokens, width), vmem(width, 4 * width),
            pltpu.VMEM((16, width), F32), vmem(shards // 2, share, 4 * width), vmem(shards // 2, share, 4 * width),
            vmem(experts, 16, wide), vmem(experts, 16, wide), pltpu.VMEM((experts, 16, width), F32),
            pltpu.VMEM((shards, 16, width), F32),
            dma((many,)), dma((many,)), dma((2, many)), dma((2, many)),
            dma((shards,)), dma((shards + 1,)), dma((parts, 2)), dma((parts, 2)), dma((parts, 2)),
            dma((shards // 2, parts, 2)), dma((parts, 2)), dma((parts, 2)), dma((parts, 2)),
            dma((shards,)), dma((shards,)), dma((shards,)), dma((shards,)),
            dma((experts,)), dma((experts,)), dma((experts,)), dma((experts,)),
            dma((experts,)), dma((experts,)), dma((shards,)), dma((shards,)),
            dma((parts, 2)), dma((parts, 2)), dma((parts, 2)), dma((parts, 2)),
        ],
        outside=(*range(2 + len(loaded)), len(loaded) + 10, len(loaded) + 11),
        collective=1,
    )
    entries = float(count * real * width * experts * shards)
    up_f, down_f, in_f, out_f, d_gain, d_shift, d_bias, d_hidden, d_last, sizes = call(
        functools.partial(outputs_kernel, entries),
        [
            ((1, width, hidden_units), F32), ((1, hidden_units, width), F32), ((share, 3 * width), F32),
            ((share, width), F32), ((2, share), F32), ((2, share), F32), ((3, share), F32),
            ((1, hidden_units), F32), ((1, width), F32), ((8, 1), F32),
        ],
        [up_total, down_total, small, owned, vector_sums],
    )

    def cut(values):
        return values.reshape(count, lines, values.shape[1])[:, :real]

    return (
        cut(out),
        cut(d_x),
        in_f,
        out_f,
        d_gain,
        d_shift,
        d_bias,
        up_f,
        d_hidden,
        down_f,
        d_last,
        cut(d_gates),
        sizes[:3, 0],
    )


def solution(mesh):
    every = P(("expert", "shard"), None, None)
    return jax.shard_map(
        local,
        mesh=mesh,
        in_specs=(
            every, P("shard", None), P("shard", None), P(None, "shard"), P(None, "shard"), P(None, "shard"),
            P("expert", None, None), P("expert", None), P("expert", None, None), P("expert", None),
            every, every, every,
        ),
        out_specs=(
            every, every, P("shard", None), P("shard", None), P(None, "shard"), P(None, "shard"),
            P(None, "shard"), P("expert", None, None), P("expert", None), P("expert", None, None),
            P("expert", None), every, P(),
        ),
        check_vma=False,
    )
```
